32 devices in a mesh: dp: 8 (over z, y), lon: 4 (over x, core).
Axes of the slice: x: 2, y: 2, z: 4, core: 2. Of those that a mesh axis runs over, the one named last changes fastest.
Arguments:
- fields: bfloat16 [8, 16, 512, 192], P('dp', None, 'lon'), may hold values from -6 to 6
- cotangent: bfloat16 [8, 16, 512, 192], P('dp', None, 'lon'), may hold values from -6 to 6
- land_sea: int32 [16, 512], P(None, 'lon'), may hold values 0 or 1
- kernel: float32 [7, 7, 192], replicated, may hold values from -0.875 to 0.875
- ln_gain: float32 [192], replicated, may hold values from 0.5 to 1.5
- weight_in: bfloat16 [192, 768], replicated, may hold values from -0.4375 to 0.4375
- bias_in: float32 [768], replicated, may hold values from -3 to 3
- weight_out: bfloat16 [768, 192], replicated, may hold values from -0.21875 to 0.21875
Outputs:
- output: bfloat16 [8, 16, 512, 192], P('dp', None, 'lon')
- grad_fields: bfloat16 [8, 16, 512, 192], P('dp', None, 'lon')
- grad_in: float32 [192, 768], P('dp')
- grad_out: float32 [768, 192], P('dp')
- grad_kernel: float32 [7, 7, 192], replicated
- grad_gain: float32 [192], replicated
- grad_bias: float32 [768], replicated
The draws below stay inside these ranges and needn't reach their ends.
All inputs are finite; a program needn't handle non-finite values. No bound on the sum of `land_sea` on one device may be relied on, other than what follows from the above.
Results may differ from the reference program's by a relative error of at most 0.025.
Values may be sent and summed in bfloat16 or wider, within the bound.
No kernel may reach another device: no remote copies, remote signals or barrier semaphores. Data moves between devices by JAX's collectives and lax.ppermute only.
A program may use at most 64 MiB of HBM per device.

```python
import math
import jax
import jax.numpy as jnp
from jax import lax

C = 192
HID = 768
KS = 7
LAT = 16
SAMPLES = 8
LON = 512


def touch_ends(values, key, least, high):
    extent = values.shape
    place = [jax.random.randint(jax.random.fold_in(key, axis), (), 0, extent[axis]) for axis in range(len(extent))]
    values = values.at[tuple(place)].set(least)
    longest = extent.index(max(extent))
    place[longest] = (place[longest] + 1) % extent[longest]
    return values.at[tuple(place)].set(high)


def block_scale(rng, dims, pieces, smallest, largest):
    factor_of, own = 1.0, jax.random.fold_in(rng, 6)
    for dim, parts in pieces:
        steps = jnp.exp(jax.random.uniform(jax.random.fold_in(own, dim), (parts,), jnp.float32, smallest / len(pieces), largest / len(pieces)))
        factor_of = factor_of * jnp.repeat(steps, dims[dim] // parts).reshape([-1 if axis == dim else 1 for axis in range(len(dims))])
    return factor_of


def gaussian(key, dims, scale, most, split=(), dtype=jnp.bfloat16):
    drawn = scale * jax.random.normal(key, dims, jnp.float32)
    if split:
        drawn = drawn * block_scale(key, dims, split, -0.22, 0.18)
    return jnp.clip(drawn, -most, most).astype(dtype)


def setup_inputs(seed: int = 0) -> dict:
    keys = jax.random.split(jax.random.key(seed), 9)
    return {
        "fields": gaussian(keys[0], (SAMPLES, LAT, LON, C), 1.0, 6.0, ((0, 8), (2, 4))),
        "cotangent": gaussian(keys[1], (SAMPLES, LAT, LON, C), 1.0, 6.0, ((0, 8), (2, 4))),
        "land_sea": touch_ends((jax.random.randint(keys[2], (LAT, LON), 0, 4) < 3).astype(jnp.int32), jax.random.fold_in(keys[2], 1), 0, 1),
        "kernel": gaussian(keys[3], (KS, KS, C), (KS * KS) ** -0.5, 0.875, (), jnp.float32),
        "ln_gain": jnp.clip(1.0 + 0.1 * jax.random.normal(keys[4], (C,), jnp.float32), 0.5, 1.5),
        "weight_in": gaussian(keys[5], (C, HID), C ** -0.5, 0.4375),
        "bias_in": gaussian(keys[6], (HID,), 0.5, 3.0, (), jnp.float32),
        "weight_out": gaussian(keys[7], (HID, C), HID ** -0.5, 0.21875),
    }


def gelu_exact(value):
    return value * (1.0 + lax.erf(value / math.sqrt(2.0))) / 2.0

def gelu_slope(value):
    return (1.0 + lax.erf(value / math.sqrt(2.0))) / 2.0 + value * jnp.exp(-value * value / 2.0) / math.sqrt(2.0 * math.pi)

def pad_band(block):
    wrapped = jnp.concatenate([block[:, :, -3:], block, block[:, :, :3]], axis=2)
    return jnp.pad(wrapped, ((0, 0), (3, 3), (0, 0), (0, 0)))

def depthwise(padded, kernel, lat_rows, lon_cols):
    total = jnp.zeros((padded.shape[0], lat_rows, lon_cols, padded.shape[3]), jnp.float32)
    for row_off in range(7):
        for col_off in range(7):
            total = total + padded[:, row_off:row_off + lat_rows, col_off:col_off + lon_cols].astype(jnp.float32) * kernel[row_off, col_off]
    return total

def transposed(padded, kernel, lat_rows, lon_cols):
    total = jnp.zeros((padded.shape[0], lat_rows, lon_cols, padded.shape[3]), jnp.float32)
    for row_off in range(7):
        for col_off in range(7):
            total = total + padded[:, 6 - row_off:6 - row_off + lat_rows, 6 - col_off:6 - col_off + lon_cols].astype(jnp.float32) * kernel[row_off, col_off]
    return total

def kernel_terms(padded, d_conv, lat_rows, lon_cols):
    d_float = d_conv.astype(jnp.float32)
    rows_out = []
    for row_off in range(7):
        cols_out = []
        for col_off in range(7):
            window = padded[:, row_off:row_off + lat_rows, col_off:col_off + lon_cols].astype(jnp.float32)
            cols_out.append(lax.optimization_barrier(jnp.sum(window * d_float, axis=(0, 1, 2))))
        rows_out.append(jnp.stack(cols_out, axis=0))
    return jnp.stack(rows_out, axis=0)

def one_pass(fields, cotangent, mask_b, kernel, ln_gain, weight_in, bias_in, weight_out, lat_rows, lon_cols):
    channels = fields.shape[3]
    masked = fields * mask_b
    padded = pad_band(masked)
    conv = depthwise(padded, kernel, lat_rows, lon_cols)
    mean_c = lax.optimization_barrier(jnp.mean(conv, axis=-1, keepdims=True))
    centered = conv - mean_c
    inv_sigma = lax.rsqrt(lax.optimization_barrier(jnp.mean(centered * centered, axis=-1, keepdims=True)) + 1e-06)
    nhat = centered * inv_sigma
    normed = (nhat * ln_gain).astype(jnp.bfloat16)
    flat = normed.reshape(-1, channels)
    pre = jnp.dot(flat, weight_in, preferred_element_type=jnp.float32) + bias_in
    act = gelu_exact(pre).astype(jnp.bfloat16)
    branch = jnp.dot(act, weight_out, preferred_element_type=jnp.float32).reshape(fields.shape)
    mask_f = mask_b.astype(jnp.float32)
    output = (mask_f * (fields.astype(jnp.float32) + branch)).astype(jnp.bfloat16)
    grad_m = cotangent * mask_b
    grad_flat = grad_m.reshape(-1, channels)
    d_act = lax.dot_general(grad_flat, weight_out, (((1,), (1,)), ((), ())), preferred_element_type=jnp.float32)
    d_pre = (d_act * gelu_slope(pre)).astype(jnp.bfloat16)
    part_out = lax.dot_general(act, grad_flat, (((0,), (0,)), ((), ())), preferred_element_type=jnp.float32)
    part_in = lax.dot_general(flat, d_pre, (((0,), (0,)), ((), ())), preferred_element_type=jnp.float32)
    part_bias = lax.optimization_barrier(jnp.sum(d_pre.astype(jnp.float32), axis=0))
    d_normed = lax.dot_general(d_pre, weight_in, (((1,), (1,)), ((), ())), preferred_element_type=jnp.float32).reshape(conv.shape)
    part_gain = lax.optimization_barrier(jnp.sum(d_normed * nhat, axis=(0, 1, 2)))
    d_hat = d_normed * ln_gain
    d_conv = (inv_sigma * (d_hat - lax.optimization_barrier(jnp.mean(d_hat, axis=-1, keepdims=True)) - nhat * lax.optimization_barrier(jnp.mean(d_hat * nhat, axis=-1, keepdims=True)))).astype(jnp.bfloat16)
    part_kernel = kernel_terms(padded, d_conv, lat_rows, lon_cols)
    spread = transposed(pad_band(d_conv), kernel, lat_rows, lon_cols)
    grad_fields = (grad_m.astype(jnp.float32) + mask_f * spread).astype(jnp.bfloat16)
    return (output, grad_fields, part_in, part_out, part_kernel, part_gain, part_bias)

def reference(fields, cotangent, land_sea, kernel, ln_gain, weight_in, bias_in, weight_out):
    samples, lat_rows, lon_cols, channels = fields.shape
    hidden = weight_in.shape[1]
    mask_b = land_sea.astype(jnp.bfloat16)[None, :, :, None]

    def step(carry, pair):
        one_field, one_cot = pair
        results = one_pass(one_field[None], one_cot[None], mask_b, kernel, ln_gain, weight_in, bias_in, weight_out, lat_rows, lon_cols)
        carry = tuple((total + part for total, part in zip(carry, results[2:])))
        return (carry, (results[0][0], results[1][0]))
    start = (jnp.zeros((channels, hidden), jnp.float32), jnp.zeros((hidden, channels), jnp.float32), jnp.zeros((7, 7, channels), jnp.float32), jnp.zeros((channels,), jnp.float32), jnp.zeros((hidden,), jnp.float32))
    sums, stacked = lax.scan(step, start, (fields, cotangent))
    scale = 1.0 / math.sqrt(samples * lat_rows * lon_cols)
    return (stacked[0], stacked[1], sums[0] * scale, sums[1] * scale, sums[2] * scale, sums[3] * scale, sums[4] * scale)
```

```python
import functools
import math

import jax
import jax.numpy as jnp
from jax import lax
from jax.experimental import pallas as pl
from jax.experimental.pallas import tpu as pltpu
from jax.sharding import PartitionSpec as P

F32 = jnp.float32
BF16 = jnp.bfloat16
LIMIT = 56 * 2**20
EDGE = 8


def dot(lhs, rhs):
    return jnp.dot(lhs, rhs, preferred_element_type=F32)


def dot_t(lhs, rhs):
    return lax.dot_general(lhs, rhs, (((1,), (1,)), ((), ())), preferred_element_type=F32)


def t_dot(lhs, rhs):
    return lax.dot_general(lhs, rhs, (((0,), (0,)), ((), ())), preferred_element_type=F32)


def build_tiles(kernel_ref, tiles_a, tiles_b, flip):
    row = lax.broadcasted_iota(jnp.int32, (128, 128), 0)
    lane = lax.broadcasted_iota(jnp.int32, (128, 128), 1)
    eye = row == lane
    eye_half = (row & 63) == (lane & 63)
    low = lane[:1] < 64
    zero_block = jnp.zeros((128, 128), BF16)
    zero_row = jnp.zeros((1, 128), F32)
    for b in range(7):
        taps = []
        for a in range(7):
            at, bt = (6 - a, 6 - b) if flip else (a, b)
            taps.append(kernel_ref[at, bt : bt + 1, :])
        blocks = [jnp.where(eye, tap[:, :128], 0.0).astype(BF16) for tap in taps]
        rests = [jnp.concatenate([tap[:, 128:]] * 2, axis=1) for tap in taps]

        def block(a):
            return blocks[a] if 0 <= a < 7 else zero_block

        def rest(a):
            return rests[a] if 0 <= a < 7 else zero_row

        for d in range(4):
            for i in range(2):
                for o in range(2):
                    tiles_a[b * 4 + d, i * 128 : (i + 1) * 128, o * 128 : (o + 1) * 128] = block(
                        2 * d + i - o
                    )
        for d in range(3):
            for i in range(2):
                for o in range(2):
                    a = 4 * d + 2 * i - 2 * o
                    top = jnp.where(low, rest(a), rest(a - 1))
                    bottom = jnp.where(low, rest(a + 1), rest(a))
                    part = jnp.where(eye_half, jnp.where(row < 64, top, bottom), 0.0)
                    tiles_b[b * 3 + d, i * 128 : (i + 1) * 128, o * 128 : (o + 1) * 128] = (
                        part.astype(BF16)
                    )


def pack_shifts(rows_a, rows_b, packed_a, packed_b, first, width):
    for b in range(7):
        at = first + b

        def pairs(q, carry):
            packed_a[b, q] = jnp.concatenate(
                [rows_a[2 * q, at : at + width], rows_a[2 * q + 1, at : at + width]], axis=1
            ).astype(BF16)
            return carry

        def quads(q, carry):
            packed_b[b, q] = jnp.concatenate(
                [rows_b[2 * q, at : at + width], rows_b[2 * q + 1, at : at + width]], axis=1
            ).astype(BF16)
            return carry

        lax.fori_loop(0, packed_a.shape[1], pairs, 0)
        lax.fori_loop(0, packed_b.shape[1], quads, 0)


def band_products(packed_a, packed_b, tiles_a, tiles_b, out_a, out_b, width):
    halves = 2
    pairs, quads = out_a.shape[0] // halves, out_b.shape[0] // halves

    def half(h, carry):
        lhs = jnp.concatenate(
            [
                packed_a[b, pl.ds(pairs * h + d, pairs)].reshape(pairs * width, 256)
                for b in range(7)
                for d in range(4)
            ],
            axis=1,
        )
        out_a[pl.ds(pairs * h, pairs)] = dot(lhs, tiles_a[...].reshape(28 * 256, 256)).reshape(
            pairs, width, 256
        )
        lhs = jnp.concatenate(
            [
                packed_b[b, pl.ds(quads * h + d, quads)].reshape(quads * width, 256)
                for b in range(7)
                for d in range(3)
            ],
            axis=1,
        )
        out_b[pl.ds(quads * h, quads)] = dot(lhs, tiles_b[...].reshape(21 * 256, 256)).reshape(
            quads, width, 256
        )
        return carry

    lax.fori_loop(0, halves, half, 0)


def gelu_parts(z):
    u = 1.0 + (0.3275911 / math.sqrt(2.0)) * jnp.abs(z)
    t = 1.0 / u
    e = jnp.exp2(z * z * (-0.5 * math.log2(math.e)))
    poly = t * (
        0.5 * 0.254829592
        + t
        * (
            0.5 * -0.284496736
            + t * (0.5 * 1.421413741 + t * (0.5 * -1.453152027 + t * (0.5 * 1.061405429)))
        )
    )
    tail = poly * e
    cumulative = jnp.where(z >= 0.0, 1.0 - tail, tail)
    return cumulative, e * (1.0 / math.sqrt(2.0 * math.pi))


def mask_columns(mask_ref, columns):
    turned = mask_ref[...].astype(F32).T
    for i in range(mask_ref.shape[0]):
        columns[i] = jnp.broadcast_to(turned[:, i : i + 1], columns.shape[1:])


def forward_kernel(
    fields,
    cotangent,
    mask,
    halo_before,
    halo_after,
    kernel,
    gain,
    w_in,
    bias,
    w_out,
    output,
    d_rows_a,
    d_rows_b,
    payload,
    gain_sum,
    bias_sum,
    columns,
    rows_a,
    rows_b,
    tiles_a,
    tiles_b,
    packed_a,
    packed_b,
    conv_a,
    conv_b,
    wide_in,
    total_in,
    total_out,
    shards,
):
    lat, lon, channels = fields.shape
    hidden = w_in.shape[1]
    width = lon + 2 * EDGE
    build_tiles(kernel, tiles_a, tiles_b, False)
    mask_columns(mask, columns)
    wide_in[0:channels] = w_in[...]
    wide_in[channels:256] = w_in[128:channels]

    rows_a[...] = jnp.zeros_like(rows_a)
    rows_b[...] = jnp.zeros_like(rows_b)
    before, after = halo_before[...].astype(F32), halo_after[...].astype(F32)
    rest = {}
    for i in range(lat):
        m = columns[i]
        x = fields[i].astype(F32)
        rows_a[i + 3, 2 * EDGE : 2 * EDGE + lon] = x[:, :128] * m
        rows_a[i + 3, EDGE : 2 * EDGE] = before[i, :EDGE, :128]
        rows_a[i + 3, 2 * EDGE + lon : 3 * EDGE + lon] = after[i, :EDGE, :128]
        rest[i] = jnp.concatenate(
            [before[i, :EDGE, 128:], x[:, 128:] * m[:, :64], after[i, :EDGE, 128:]], axis=0
        )
    blank = jnp.zeros((width, 64), F32)
    for q in range(1, 10):
        pair = [rest.get(2 * q - 3, blank), rest.get(2 * q - 2, blank)]
        rows_b[q, EDGE : EDGE + width] = jnp.concatenate(pair, axis=1)

    pack_shifts(rows_a, rows_b, packed_a, packed_b, EDGE - 3, width)
    band_products(packed_a, packed_b, tiles_a, tiles_b, conv_a, conv_b, width)

    d_rows_a[...] = jnp.zeros_like(d_rows_a)
    d_rows_b[...] = jnp.zeros_like(d_rows_b)
    total_in[...] = jnp.zeros_like(total_in)
    total_out[...] = jnp.zeros_like(total_out)
    gain_sum[...] = jnp.zeros_like(gain_sum)
    bias_sum[...] = jnp.zeros_like(bias_sum)

    sub = lax.broadcasted_iota(jnp.int32, (EDGE, 1), 0)
    near = sub < EDGE // 2
    low = lax.broadcasted_iota(jnp.int32, (1, 128), 1) < 64
    gain_row = gain[...]
    gains = jnp.concatenate([gain_row, gain_row[:, 128:]], axis=1)
    inner = 4 * lon

    def tokens(x):
        return jnp.concatenate(
            [x[EDGE : EDGE + lon], jnp.where(near, x[EDGE + lon :], x[:EDGE])], axis=0
        )

    def quad(r, carry):
        block_a = [conv_a[2 * r], conv_a[2 * r + 1]]
        block_b = conv_b[r]
        nhats, sigmas = [], []
        for i in range(4):
            here = low if i % 2 == 0 else ~low
            xa = tokens(block_a[i // 2][:, (i % 2) * 128 : (i % 2 + 1) * 128])
            xb = tokens(block_b[:, (i // 2) * 128 : (i // 2 + 1) * 128])
            xb = jnp.where(here, xb, 0.0)
            mean = jnp.sum(xa + xb, axis=1, keepdims=True) * (1.0 / channels)
            xa = xa - mean
            xb = jnp.where(here, xb - mean, 0.0)
            var = jnp.sum(xa * xa + xb * xb, axis=1, keepdims=True) * (1.0 / channels)
            sigma = lax.rsqrt(var + 1e-6)
            nhats.append(jnp.concatenate([xa * sigma, xb * sigma], axis=1))
            sigmas.append(sigma)
        normed = jnp.concatenate(
            [n[:lon] for n in nhats] + [n[lon:] for n in nhats], axis=0
        )
        normed = (normed * gains).astype(BF16)
        masked_cot = [
            cotangent[4 * r + i].astype(F32) * columns[4 * r + i][:, :1] for i in range(4)
        ]
        for i in range(4):
            masked_cot.append(
                jnp.where(
                    near,
                    halo_after[4 * r + i].astype(F32)[EDGE:],
                    halo_before[4 * r + i].astype(F32)[EDGE:],
                )
            )
        gm = jnp.concatenate(masked_cot, axis=0).astype(BF16)
        branch, d_normed = None, None
        for h in range(0, hidden, 256):
            z = dot(normed, wide_in[:, h : h + 256]) + bias[:, h : h + 256]
            cumulative, density = gelu_parts(z)
            act = (z * cumulative)[:inner].astype(BF16)
            d_act = dot_t(gm, w_out[h : h + 256, :])
            d_pre = d_act * (cumulative + z * density)
            bias_sum[:, h : h + 256] += jnp.sum(
                d_pre[:inner].reshape(inner // 8, 8, 256), axis=0
            )
            d_pre = d_pre.astype(BF16)
            part = dot(act, w_out[h : h + 256, :])
            branch = part if branch is None else branch + part
            part = dot_t(d_pre, wide_in[:, h : h + 256])
            d_normed = part if d_normed is None else d_normed + part
            total_in[:, h : h + 256] += t_dot(normed[:inner], d_pre[:inner])
            total_out[:, h : h + 256] += t_dot(gm[:inner], act)
        gained = None
        rest_d = []
        for i in range(4):
            row = 4 * r + i
            here = low if i % 2 == 0 else ~low
            x = fields[row].astype(F32) + branch[i * lon : (i + 1) * lon]
            output[row] = (x * columns[row][:, :1]).astype(BF16)
            dn = jnp.concatenate(
                [
                    d_normed[i * lon : (i + 1) * lon],
                    d_normed[inner + i * EDGE : inner + (i + 1) * EDGE],
                ],
                axis=0,
            )
            nhat = nhats[i]
            prod = dn * nhat
            part = jnp.sum(prod[:lon].reshape(lon // 8, 8, 256), axis=0)
            gained = part if gained is None else gained + part
            d_hat = dn * gains
            da, db = d_hat[:, :128], jnp.where(here, d_hat[:, 128:], 0.0)
            mean = jnp.sum(da + db, axis=1, keepdims=True) * (1.0 / channels)
            prod = prod * gains
            corr = jnp.sum(prod[:, :128] + prod[:, 128:], axis=1, keepdims=True) * (1.0 / channels)
            da = sigmas[i] * (da - mean - nhat[:, :128] * corr)
            db = sigmas[i] * (db - mean - nhat[:, 128:] * corr)
            d_rows_a[row + 3, 2 * EDGE : 2 * EDGE + lon] = da[:lon]
            d_rows_a[row + 3, EDGE : 2 * EDGE] = jnp.where(near, 0.0, da[lon:])
            d_rows_a[row + 3, 2 * EDGE + lon : 3 * EDGE + lon] = jnp.where(near, da[lon:], 0.0)
            rest_d.append(db)
        gain_sum[...] += gained

        def spread(db):
            return jnp.concatenate(
                [jnp.where(near, 0.0, db[lon:]), db[:lon], jnp.where(near, db[lon:], 0.0)], axis=0
            )

        at = slice(EDGE, EDGE + width)
        first, second, third, fourth = [
            pltpu.roll(spread(db), 64, axis=1) for db in rest_d
        ]
        d_rows_b[2 * r + 1, at] = jnp.where(low, d_rows_b[2 * r + 1, at], first)
        d_rows_b[2 * r + 2, at] = jnp.where(low, second, third)
        d_rows_b[2 * r + 3, at] = jnp.where(low, fourth, 0.0)
        return carry

    lax.fori_loop(0, lat // 4, quad, 0)

    part_in = jnp.concatenate(
        [total_in[:128], total_in[128:192] + total_in[192:256]], axis=0
    )
    rows = channels // shards
    pieces = []
    for n in range(shards):
        mine = part_in[n * rows : (n + 1) * rows]
        pieces += [mine[:, c : c + 128] for c in range(0, hidden, 128)]
    payload[0] = jnp.concatenate(pieces, axis=0).astype(BF16)
    part_out = total_out[...].T
    rows = hidden // shards
    pieces = []
    for n in range(shards):
        mine = part_out[n * rows : (n + 1) * rows]
        pieces.append(mine[:, :128])
        pieces.append(
            jnp.concatenate([mine[: rows // 2, 128:], mine[rows // 2 :, 128:]], axis=1)
        )
    payload[1] = jnp.concatenate(pieces, axis=0).astype(BF16)


def backward_kernel(
    fields,
    cotangent,
    mask,
    kernel,
    d_rows_a,
    d_rows_b,
    gain_sum,
    bias_sum,
    grad_fields,
    small,
    columns,
    tiles_a,
    tiles_b,
    packed_a,
    packed_b,
    spread_a,
    spread_b,
    turned_a,
    turned_b,
):
    lat, lon, channels = fields.shape
    build_tiles(kernel, tiles_a, tiles_b, True)
    mask_columns(mask, columns)
    pack_shifts(d_rows_a, d_rows_b, packed_a, packed_b, 2 * EDGE - 3, lon)

    for i in range(lat):
        x = fields[i].astype(F32) * columns[i][:, :1]
        x = x.T.astype(BF16)
        s = i // 2
        turned_a[(i % 2) * 128 : (i % 2 + 1) * 128, s * lon : (s + 1) * lon] = x[:128]
        s = i // 4
        turned_b[(i % 4) * 64 : (i % 4 + 1) * 64, s * lon : (s + 1) * lon] = x[128:]

    row = lax.broadcasted_iota(jnp.int32, (128, 128), 0)
    lane = lax.broadcasted_iota(jnp.int32, (128, 128), 1)
    eye = row == lane
    eye_half = (row[:64]) == (lane[:64] & 63)
    small[...] = jnp.zeros_like(small)
    for b in range(7):
        tap = 6 - b
        blocks = {}
        for d in range(4):
            rhs = packed_a[b, 3 - d : 3 - d + lat // 2].reshape(lat // 2 * lon, 256)
            g = dot(turned_a[...], rhs)
            for i in range(2):
                for o in range(2):
                    a = 2 * d + i - o
                    part = g[i * 128 : (i + 1) * 128, o * 128 : (o + 1) * 128]
                    if 0 <= a < 7:
                        blocks[a] = part if a not in blocks else blocks[a] + part
        for a in range(7):
            small[a, tap : tap + 1, :128] = jnp.sum(
                jnp.where(eye, blocks[a], 0.0), axis=0, keepdims=True
            )
        lines = []
        for d in range(3):
            rhs = packed_b[b, 2 - d : 2 - d + lat // 4].reshape(lat // 4 * lon, 256)
            g = dot(turned_b[...], rhs)
            for i in range(4):
                part = g[i * 64 : (i + 1) * 64]
                lines.append(
                    [
                        jnp.sum(
                            jnp.where(eye_half, part[:, c : c + 128], 0.0), axis=0, keepdims=True
                        )
                        for c in (0, 128)
                    ]
                )
        for a in range(7):
            total = None
            for o in range(4):
                line = lines[a + 2 + o][o // 2][:, (o % 2) * 64 : (o % 2 + 1) * 64]
                total = line if total is None else total + line
            small[a, tap : tap + 1, 128:channels] = total
    gained = jnp.sum(gain_sum[...], axis=0, keepdims=True)
    small[0, 7:8, :128] = gained[:, :128]
    small[0, 7:8, 128:channels] = gained[:, 128:192] + gained[:, 192:256]
    biased = jnp.sum(bias_sum[...], axis=0, keepdims=True)
    for k in range(biased.shape[1] // 256):
        small[1 + k, 7:8, :] = biased[:, k * 256 : (k + 1) * 256]

    band_products(packed_a, packed_b, tiles_a, tiles_b, spread_a, spread_b, lon)
    for i in range(lat):
        a = spread_a[i // 2][:, (i % 2) * 128 : (i % 2 + 1) * 128]
        b = spread_b[i // 4][:, (i % 4) * 64 : (i % 4 + 1) * 64]
        x = cotangent[i].astype(F32) + jnp.concatenate([a, b], axis=1)
        grad_fields[i] = (x * columns[i][:, :1]).astype(BF16)


def swapped(x, axis, bit):
    peers = lax.axis_size(axis)
    return lax.ppermute(x, axis, [(i, i ^ bit) for i in range(peers)])


def bits_of(count):
    return [1 << k for k in range(count.bit_length() - 1)]


def reduced(payload, small):
    shards, tiles = lax.axis_size("dp"), lax.axis_size("lon")
    me, tile = lax.axis_index("dp"), lax.axis_index("lon")
    core = tile & 1

    def both(x, y):
        return (x.astype(F32) + y.astype(F32)).astype(BF16)

    def pick(x, axis, at):
        return lax.dynamic_index_in_dim(x, at, axis, keepdims=False)

    mine = both(pick(payload, 0, core), swapped(pick(payload, 0, 1 - core), "lon", 1))
    small = small + swapped(small, "lon", 1)
    mine = mine.reshape(shards, -1, 128)
    for bit in bits_of(shards):
        have = (me // bit) & 1
        split = mine.reshape(mine.shape[0] // 2, 2, -1, 128)
        mine = both(pick(split, 1, have), swapped(pick(split, 1, 1 - have), "dp", bit))
        small = small + swapped(small, "dp", bit)
    mine = mine.reshape(-1, 128)
    for bit in bits_of(tiles)[1:]:
        mine = both(mine, swapped(mine, "lon", bit))
        small = small + swapped(small, "lon", bit)
    other = swapped(mine, "lon", 1)
    first = core == 0
    return jnp.where(first, mine, other), jnp.where(first, other, mine), small


def per_device(fields, cotangent, land_sea, kernel, ln_gain, weight_in, bias_in, weight_out):
    samples, lat, lon, channels = fields.shape
    hidden = weight_in.shape[1]
    shards, tiles = lax.axis_size("dp"), lax.axis_size("lon")
    width = lon + 2 * EDGE
    mask_b = land_sea.astype(BF16)[:, :, None]
    fields3, cot3 = fields[0], cotangent[0]

    def edge(cols):
        m = mask_b[:, cols]
        return jnp.concatenate([fields3[:, cols] * m, cot3[:, cols] * m], axis=1)

    up = [(i, (i + 1) % tiles) for i in range(tiles)]
    before = lax.ppermute(edge(slice(lon - EDGE, lon)), "lon", up)
    after = lax.ppermute(edge(slice(0, EDGE)), "lon", [(j, i) for i, j in up])

    tiles_shapes = [pltpu.VMEM((28, 256, 256), BF16), pltpu.VMEM((21, 256, 256), BF16)]
    output, d_rows_a, d_rows_b, payload, gain_sum, bias_sum = pl.pallas_call(
        functools.partial(forward_kernel, shards=shards),
        out_shape=[
            jax.ShapeDtypeStruct((lat, lon, channels), BF16),
            jax.ShapeDtypeStruct((lat + 6, width + 16, 128), F32),
            jax.ShapeDtypeStruct((lat // 2 + 4, width + 16, 128), F32),
            jax.ShapeDtypeStruct((2, channels * hidden // 128, 128), BF16),
            jax.ShapeDtypeStruct((8, 256), F32),
            jax.ShapeDtypeStruct((8, hidden), F32),
        ],
        scratch_shapes=[
            pltpu.VMEM((lat, lon, 128), F32),
            pltpu.VMEM((lat + 6, width + 16, 128), F32),
            pltpu.VMEM((lat // 2 + 4, width + 16, 128), F32),
            *tiles_shapes,
            pltpu.VMEM((7, lat // 2 + 3, width, 256), BF16),
            pltpu.VMEM((7, lat // 4 + 2, width, 256), BF16),
            pltpu.VMEM((lat // 2, width, 256), F32),
            pltpu.VMEM((lat // 4, width, 256), F32),
            pltpu.VMEM((256, hidden), BF16),
            pltpu.VMEM((256, hidden), F32),
            pltpu.VMEM((channels, hidden), F32),
        ],
        compiler_params=pltpu.CompilerParams(vmem_limit_bytes=LIMIT),
        name="forward",
    )(
        fields3,
        cot3,
        land_sea,
        before,
        after,
        kernel,
        ln_gain[None],
        weight_in,
        bias_in[None],
        weight_out,
    )
    grad_fields, small = pl.pallas_call(
        backward_kernel,
        out_shape=[
            jax.ShapeDtypeStruct((lat, lon, channels), BF16),
            jax.ShapeDtypeStruct((7, 8, 256), F32),
        ],
        scratch_shapes=[
            pltpu.VMEM((lat, lon, 128), F32),
            *tiles_shapes,
            pltpu.VMEM((7, lat // 2 + 3, lon, 256), BF16),
            pltpu.VMEM((7, lat // 4 + 2, lon, 256), BF16),
            pltpu.VMEM((lat // 2, lon, 256), F32),
            pltpu.VMEM((lat // 4, lon, 256), F32),
            pltpu.VMEM((256, lat // 2 * lon), BF16),
            pltpu.VMEM((256, lat // 4 * lon), BF16),
        ],
        compiler_params=pltpu.CompilerParams(vmem_limit_bytes=LIMIT),
        name="backward",
    )(fields3, cot3, land_sea, kernel, d_rows_a, d_rows_b, gain_sum, bias_sum)

    sum_in, sum_out, small = reduced(payload, small)
    scale = 1.0 / math.sqrt(samples * lat * lon * shards * tiles)
    rows = channels // shards
    sum_in = sum_in.reshape(hidden // 128, rows, 128).transpose(1, 0, 2).reshape(rows, hidden)
    rows = hidden // shards
    rest = sum_out[rows:]
    sum_out = jnp.concatenate(
        [sum_out[:rows], jnp.concatenate([rest[:, :64], rest[:, 64:]], axis=0)], axis=1
    )
    return (
        output[None],
        grad_fields[None],
        sum_in.astype(F32) * scale,
        sum_out.astype(F32) * scale,
        small[:, :7, :channels] * scale,
        small[0, 7, :channels] * scale,
        small[1 : 1 + hidden // 256, 7].reshape(hidden) * scale,
    )


def solution(mesh):
    placed = (
        P("dp", None, "lon", None),
        P("dp", None, "lon", None),
        P(None, "lon"),
        P(),
        P(),
        P(),
        P(),
        P(),
    )
    return jax.shard_map(
        per_device,
        mesh=mesh,
        in_specs=placed,
        out_specs=(
            P("dp", None, "lon", None),
            P("dp", None, "lon", None),
            P("dp", None),
            P("dp", None),
            P(),
            P(),
            P(),
        ),
        check_vma=False,
    )
```

```python
import functools
import math

import jax
import jax.numpy as jnp
from jax import lax
from jax.experimental import pallas as pl
from jax.experimental.pallas import tpu as pltpu
from jax.sharding import PartitionSpec as P

F32 = jnp.float32
BF16 = jnp.bfloat16
LIMIT = 56 * 2**20
EDGE = 8
GROUP = 16


def dot(lhs, rhs):
    return jnp.dot(lhs, rhs, preferred_element_type=F32)


def dot_t(lhs, rhs):
    return lax.dot_general(lhs, rhs, (((1,), (1,)), ((), ())), preferred_element_type=F32)


def iota(shape, axis):
    return lax.broadcasted_iota(jnp.int32, shape, axis)


def identity(size):
    return jnp.where(iota((size, size), 0) == iota((size, size), 1), 1.0, 0.0).astype(BF16)


def masked_row(array, mask, i):
    return (array[i].astype(F32) * mask[i : i + 1].astype(F32)).astype(BF16)


def group_of(rows, g):
    return jnp.concatenate([row[GROUP * g : GROUP * (g + 1)] for row in rows], axis=0)


def band_mask(i):
    shape = (GROUP, 256)
    lane = iota(shape, 1)
    same = (lane & (GROUP - 1)) == iota(shape, 0)
    return same & (jnp.abs((lane >> 4) - i) <= 3)


def unrolled(count, body):
    for k in range(count):
        body(k)


def build_tiles(lines, rolled, tiles):
    for i in range(16):
        rolled[i] = pltpu.roll(lines[...], ((i - 3) * GROUP) % 256, axis=1)
    masks = [band_mask(i) for i in range(16)]

    def group(g):
        for b in range(7):
            for i in range(16):
                line = rolled[i, 7 * g + b : 7 * g + b + 1, :]
                at = b * 256 + i * GROUP
                tiles[g, at : at + GROUP, :] = jnp.where(masks[i], line, 0.0).astype(BF16)

    unrolled(tiles.shape[0], group)


def pack_shifts(cells, packed, lon, edges):
    near = iota((EDGE, 1), 0) < EDGE // 2

    def group(g):
        for half in range(2):
            source = 2 * g + half
            for b in range(7):
                s = b - 3
                x = cells[source, pl.ds(2 * EDGE + s, lon), :]
                if edges:
                    left = cells[source, pl.ds(EDGE + s, EDGE), :]
                    right = cells[source, pl.ds(2 * EDGE + lon + s, EDGE), :]
                    edge = jnp.where(near, right, left)
                    x = jnp.concatenate([x, edge, edge], axis=0)
                at = b * 256 + half * 128
                packed[g, :, at : at + 128] = x.astype(BF16)

    unrolled(packed.shape[0], group)


def gelu_parts(z):
    cumulative = 0.5 + 0.5 * lax.erf(z * math.sqrt(0.5))
    density = jnp.exp2(z * z * (-0.5 * math.log2(math.e))) * (1.0 / math.sqrt(2.0 * math.pi))
    return cumulative, density


def edge_kernel(fields, cotangent, mask, first, last):
    lat, channels, lon = fields.shape
    groups = channels // GROUP
    row, lane = iota((2 * EDGE, lon), 0), iota((2 * EDGE, lon), 1)
    ends = jnp.where(lane == jnp.where(row < EDGE, row, row + lon - 2 * EDGE), 1.0, 0.0)
    ends = ends.astype(BF16)
    rows = [masked_row(fields, mask, i) for i in range(lat)]
    cells = [dot_t(ends, group_of(rows, g)) for g in range(groups)]
    column, lane = iota((lon, 256), 0), iota((lon, 256), 1)
    column = jnp.where(
        lane < 128,
        jnp.where(column < EDGE, column, -1),
        jnp.where(column >= lon - EDGE, column - (lon - EDGE), -1),
    )
    lane = lane & 127
    total = None
    for i in range(lat):
        place = (column >= 0) & (lane == column + EDGE * i)
        part = dot(masked_row(cotangent, mask, i), jnp.where(place, 1.0, 0.0).astype(BF16))
        total = part if total is None else total + part
    for k, out in enumerate((first, last)):
        for half in range(2):
            at = slice(half * 128, (half + 1) * 128)
            x = [cell[k * EDGE : (k + 1) * EDGE, at] for cell in cells]
            count = groups * EDGE
            out[half * count : (half + 1) * count] = jnp.concatenate(x, axis=0).astype(BF16)
        out[2 * groups * EDGE :] = total[:, k * 128 : (k + 1) * 128].astype(BF16)


def forward_kernel(
    core,
    fields,
    cotangent,
    mask,
    halo_before,
    halo_after,
    lines,
    gain,
    w_in,
    bias,
    w_out,
    output,
    d_conv,
    d_edge,
    keep,
    send,
    sums,
    rolled,
    tiles,
    cells,
    packed,
    conv,
    conv_edge,
    turned_in,
    turned_out,
    gain_columns,
    total_in,
    total_out,
    total_gain,
    shards,
):
    lat, channels, lon = fields.shape
    hidden = w_in.shape[1]
    groups = channels // GROUP
    build_tiles(lines, rolled, tiles)

    gain_row = gain[...].reshape(1, channels)
    gain_columns[...] = jnp.broadcast_to(gain_row, (128, channels)).T
    bias_row = bias[...].reshape(1, hidden)
    bias_columns = jnp.broadcast_to(bias_row, (64, hidden)).T
    lane = iota((hidden, 64), 1)
    high = bias_columns.astype(BF16).astype(F32)
    middle = (bias_columns - high).astype(BF16).astype(F32)
    low = bias_columns - high - middle
    bias_columns = jnp.where(
        lane == 0, high, jnp.where(lane == 1, middle, jnp.where(lane == 2, low, 0.0))
    )
    turned_in[...] = jnp.concatenate([w_in[...].astype(F32).T, bias_columns], axis=1).astype(BF16)
    turned_out[...] = w_out[...].T

    eye = identity(lon)
    before, after = halo_before[...].astype(F32), halo_after[...].astype(F32)
    blank = jnp.zeros((EDGE, 128), F32)
    rows = [masked_row(fields, mask, i) for i in range(lat)]
    for g in range(groups):
        x = dot_t(eye, group_of(rows, g))
        for half in range(2):
            at = half * groups * EDGE + g * EDGE
            cells[2 * g + half] = jnp.concatenate(
                [
                    blank,
                    before[at : at + EDGE],
                    x[:, half * 128 : (half + 1) * 128],
                    after[at : at + EDGE],
                    blank,
                ],
                axis=0,
            )
    pack_shifts(cells, packed, lon, True)

    def band(g):
        y = dot(packed[g], tiles[g])
        conv[g] = y[:lon].T
        conv_edge[g] = y[lon : lon + EDGE]

    unrolled(groups, band)

    total_in[...] = jnp.zeros_like(total_in)
    total_out[...] = jnp.zeros_like(total_out)
    total_gain[...] = jnp.zeros_like(total_gain)

    def block(y, gm, inner):
        cols = y.shape[1]
        gains = jnp.concatenate([gain_columns[...]] * (cols // 128), axis=1)
        y = y - jnp.sum(y, axis=0, keepdims=True) * (1.0 / channels)
        var = jnp.sum(y * y, axis=0, keepdims=True) * (1.0 / channels)
        sigma = lax.rsqrt(var + 1e-6)
        nhat = y * sigma
        normed = (nhat * gains).astype(BF16)
        normed = jnp.concatenate([normed, jnp.ones((64, cols), BF16)], axis=0)
        if inner:
            upright, gm_upright = normed.T, gm.T
        branch, d_normed = None, None
        for h in range(0, hidden, 256):
            at = slice(h, h + 256)
            z = dot(turned_in[at, :], normed)
            cumulative, density = gelu_parts(z)
            d_act = dot(turned_out[at, :], gm)
            d_pre = (d_act * (cumulative + z * density)).astype(BF16)
            part = dot(w_in[:, at], d_pre)
            d_normed = part if d_normed is None else d_normed + part
            if inner:
                act = (z * cumulative).astype(BF16)
                part = dot(w_out[:, at], act)
                branch = part if branch is None else branch + part
                total_in[at, :] += dot(d_pre, upright)
                total_out[at, :] += dot(act, gm_upright)
        prod = d_normed * nhat
        if inner:
            part = prod[:, :128]
            for c in range(128, cols, 128):
                part = part + prod[:, c : c + 128]
            total_gain[...] += part
        d_hat = d_normed * gains
        mean = jnp.sum(d_hat, axis=0, keepdims=True) * (1.0 / channels)
        corr = jnp.sum(prod * gains, axis=0, keepdims=True) * (1.0 / channels)
        return (sigma * (d_hat - mean - nhat * corr)).astype(BF16), branch

    count = 4

    def rows_block(r):
        y, gm, masks = [], [], []
        for k in range(count):
            i = count * r + k
            at = slice(i * GROUP, (i + 1) * GROUP)
            y.append(jnp.concatenate([conv[g, at, :] for g in range(groups)], axis=0))
            m = mask[i : i + 1].astype(F32)
            masks.append(m)
            gm.append((cotangent[i].astype(F32) * m).astype(BF16))
        d, branch = block(jnp.concatenate(y, axis=1), jnp.concatenate(gm, axis=1), True)
        for k in range(count):
            i = count * r + k
            at = slice(k * lon, (k + 1) * lon)
            output[i] = ((fields[i].astype(F32) + branch[:, at]) * masks[k]).astype(BF16)
            d_conv[i] = d[:, at]

    unrolled(lat // count, rows_block)

    lane = iota((1, 128), 1)
    y = []
    for i in range(lat):
        half, k = (i * GROUP) // 128 * 128, i % 8
        line = []
        for tile in range(0, channels, 128):
            x = jnp.zeros((EDGE, 128), F32)
            for g in range(tile // GROUP, min(tile + 128, channels) // GROUP):
                piece = pltpu.roll(conv_edge[g, :, half : half + 128], (g - k) % 8 * GROUP, axis=1)
                x = jnp.where((lane >> 4) == g % 8, piece, x)
            line.append(x)
        y.append(jnp.concatenate(line, axis=1))
    y = jnp.concatenate(y, axis=0).T[:channels]
    at = 2 * groups * EDGE
    gm = jnp.where((lane & (EDGE - 1)) < EDGE // 2, after[at:], before[at:]).astype(BF16)
    d_edge[...], _ = block(y, gm, False)

    first = core[0] == 0
    rows = channels // shards
    sum_in = total_in[...].T
    parts_in, parts_out = [], []
    for n in range(shards):
        mine = sum_in[n * rows : (n + 1) * rows]
        parts_in += [mine[:, c : c + 128] for c in range(0, hidden, 128)]
    rows = hidden // shards
    for n in range(shards):
        mine = total_out[n * rows : (n + 1) * rows]
        parts_out.append(mine[:, :128])
        parts_out.append(
            jnp.concatenate([mine[: rows // 2, 128:], mine[rows // 2 :, 128:]], axis=1)
        )
    parts_in, parts_out = jnp.concatenate(parts_in, axis=0), jnp.concatenate(parts_out, axis=0)
    keep[...] = jnp.where(first, parts_in, parts_out).astype(BF16)
    send[...] = jnp.where(first, parts_out, parts_in).astype(BF16)
    sums[:, :hidden] = sum_in[channels : channels + 8]
    sums[:, hidden:] = jnp.broadcast_to(
        jnp.sum(total_gain[...].T, axis=0, keepdims=True), (8, channels)
    )


def lay_cells(d_conv, d_edge, cells):
    lat, channels, lon = d_conv.shape
    eye = identity(lon)
    rows = [d_conv[i] for i in range(lat)]
    near = iota((EDGE, 1), 0) < EDGE // 2
    lane = iota((1, 128), 1) >> 4
    blank = jnp.zeros((EDGE, 128), F32)
    edges = d_edge[...].astype(F32).T
    for g in range(channels // GROUP):
        x = dot_t(eye, group_of(rows, g))
        tile = (g * GROUP) // 128 * 128
        for half in range(2):
            edge = blank
            for k in range(8):
                i = 8 * half + k
                piece = edges[i * EDGE : (i + 1) * EDGE, tile : min(tile + 128, channels)]
                if piece.shape[1] < 128:
                    piece = jnp.concatenate([piece, piece], axis=1)
                shift = (k * GROUP - (g * GROUP - tile)) % 128
                edge = jnp.where(lane == k, pltpu.roll(piece, shift, axis=1), edge)
            cells[2 * g + half] = jnp.concatenate(
                [
                    blank,
                    jnp.where(near, 0.0, edge),
                    x[:, half * 128 : (half + 1) * 128],
                    jnp.where(near, edge, 0.0),
                    blank,
                ],
                axis=0,
            )


def taps_kernel(core, fields, mask, d_conv, d_edge, sums, keep, send, cells, packed, masked, small):
    lat, channels, lon = fields.shape
    groups = channels // GROUP
    lay_cells(d_conv, d_edge, cells)
    pack_shifts(cells, packed, lon, False)
    rows = [masked_row(fields, mask, i) for i in range(lat)]
    for g in range(groups):
        masked[g] = group_of(rows, g)
    bands = [band_mask(i) for i in range(lat)]
    sub, lane = iota((8, 1), 0), iota((1, 128), 1) >> 4
    small[...] = jnp.zeros_like(small)

    for g in range(groups):
        g_all = dot(masked[g], packed[g])
        taps = jnp.zeros((8, 128), F32)
        for b in range(7):
            total = None
            for i in range(lat):
                part = g_all[i * GROUP : (i + 1) * GROUP, b * 256 : (b + 1) * 256]
                part = jnp.where(bands[i], part, 0.0)
                part = part[:8] + part[8:]
                part = pltpu.roll(part, ((3 - i) * GROUP) % 256, axis=1)[:, :128]
                total = part if total is None else total + part
            total = jnp.sum(total, axis=0, keepdims=True)
            taps = jnp.where(sub == 6 - b, total, taps)
        place = g * GROUP // 128
        for a in range(7):
            shift = (g * GROUP - (6 - a) * GROUP) % 128
            moved = pltpu.roll(taps, shift, axis=1)
            small[a, place] = jnp.where(lane == g % 8, moved, small[a, place])

    line = sums[0:1]
    hidden = line.shape[1] - channels
    pieces = [line[:, c : c + 128] for c in range(0, hidden, 128)]
    pieces.append(line[:, hidden : hidden + 128])
    pieces.append(
        jnp.concatenate([line[:, hidden + 128 :], jnp.zeros((1, 256 - channels), F32)], axis=1)
    )
    for k, piece in enumerate(pieces):
        small[k // 2, k % 2, 7:8] = piece
    flat = small[...].reshape(112, 128)
    first = core[0] == 0
    keep[...] = jnp.where(first, flat[:56], flat[56:])
    send[...] = jnp.where(first, flat[56:], flat[:56])


def spread_kernel(cotangent, mask, lines, d_conv, d_edge, grad_fields, rolled, tiles, cells, packed, spread):
    lat, channels, lon = cotangent.shape
    groups = channels // GROUP
    build_tiles(lines, rolled, tiles)
    lay_cells(d_conv, d_edge, cells)
    pack_shifts(cells, packed, lon, False)

    def band(g):
        spread[g] = dot(packed[g], tiles[g]).T

    unrolled(groups, band)
    for i in range(lat):
        x = jnp.concatenate(
            [spread[g, i * GROUP : (i + 1) * GROUP, :] for g in range(groups)], axis=0
        )
        x = cotangent[i].astype(F32) + x
        grad_fields[i] = (x * mask[i : i + 1].astype(F32)).astype(BF16)


def final_kernel(core, mine, other, small_mine, small_other, grad_in, grad_out, grad_kernel, grad_gain, grad_bias, scale):
    first = core[0] == 0
    mine, other = mine[...].astype(F32) * scale, other[...].astype(F32) * scale
    sum_in, sum_out = jnp.where(first, mine, other), jnp.where(first, other, mine)
    mine, other = small_mine[...] * scale, small_other[...] * scale
    small = jnp.concatenate(
        [jnp.where(first, mine, other), jnp.where(first, other, mine)], axis=0
    )
    rows, hidden = grad_in.shape
    for k in range(hidden // 128):
        grad_in[:, k * 128 : (k + 1) * 128] = sum_in[k * rows : (k + 1) * rows]
    rows, channels = grad_out.shape
    grad_out[:, :128] = sum_out[:rows]
    rest = sum_out[rows:]
    grad_out[:, 128:] = jnp.concatenate([rest[:, :64], rest[:, 64:]], axis=0)
    for a in range(7):
        grad_kernel[a, :, :128] = small[16 * a : 16 * a + 7]
        grad_kernel[a, :, 128:] = small[16 * a + 8 : 16 * a + 15, : channels - 128]
    lines = [small[8 * k + 7 : 8 * k + 8] for k in range(hidden // 128 + 2)]
    grad_bias[...] = jnp.concatenate(lines[:-2], axis=1).reshape(hidden)
    grad_gain[...] = jnp.concatenate([lines[-2], lines[-1][:, : channels - 128]], axis=1).reshape(
        channels
    )


def swapped(x, axis, bit):
    peers = lax.axis_size(axis)
    return lax.ppermute(x, axis, [(i, i ^ bit) for i in range(peers)])


def bits_of(count):
    return [1 << k for k in range(count.bit_length() - 1)]


def pick(x, axis, at):
    return lax.dynamic_index_in_dim(x, at, axis, keepdims=False)


def both(x, y):
    return (x.astype(F32) + y.astype(F32)).astype(BF16)


def halved(mine, bit):
    have = (lax.axis_index("dp") // bit) & 1
    split = mine.reshape(mine.shape[0] // 2, 2, -1, 128)
    kept, sent = pick(split, 1, have), pick(split, 1, 1 - have)
    return kept, sent.reshape(-1, 128)


def two_parts(x):
    high = lax.reduce_precision(x, exponent_bits=8, mantissa_bits=7)
    return jnp.concatenate([high, x - high], axis=0).astype(BF16)


def one_part(x):
    rows = x.shape[0] // 2
    return x[:rows].astype(F32) + x[rows:].astype(F32)


def call(body, name, outs, scratch=(), specs=None):
    extra = {} if specs is None else {"in_specs": specs}
    return pl.pallas_call(
        body,
        out_shape=[jax.ShapeDtypeStruct(shape, dtype) for shape, dtype in outs],
        scratch_shapes=[pltpu.VMEM(shape, dtype) for shape, dtype in scratch],
        compiler_params=pltpu.CompilerParams(vmem_limit_bytes=LIMIT),
        name=name,
        **extra,
    )


def with_core(count):
    vmem = pl.BlockSpec(memory_space=pltpu.VMEM)
    return [pl.BlockSpec(memory_space=pltpu.SMEM)] + [vmem] * count


def lines_of(kernel):
    taps, cols, channels = kernel.shape
    lines = kernel.reshape(taps, cols, channels // GROUP, GROUP).transpose(2, 1, 0, 3)
    lines = lines.reshape(-1, taps * GROUP)
    return jnp.pad(lines, ((0, (-lines.shape[0]) % 8), (0, 256 - lines.shape[1])))


def shapes(lat, channels, lon, hidden, shards):
    groups = channels // GROUP
    rows = channels * hidden // 128
    tiles = [((16, 88, 256), F32), ((groups, 7 * 256, 256), BF16)]
    cells = ((2 * groups, lon + 4 * EDGE, 128), F32)
    wide = ((groups, lon + 2 * EDGE, 7 * 256), BF16)
    packed = ((groups, lon, 7 * 256), BF16)
    field = ((lat, channels, lon), BF16)
    edge = ((channels, 128), BF16)
    return {
        "edges": ([((2 * channels, 128), BF16)] * 2, []),
        "forward": (
            [
                field,
                field,
                edge,
                ((rows, 128), BF16),
                ((rows, 128), BF16),
                ((8, hidden + channels), F32),
            ],
            [
                *tiles,
                cells,
                wide,
                ((groups, 256, lon), F32),
                ((groups, EDGE, 256), F32),
                ((hidden, 256), BF16),
                ((hidden, channels), BF16),
                ((channels, 128), F32),
                ((hidden, 256), F32),
                ((hidden, channels), F32),
                ((channels, 128), F32),
            ],
        ),
        "taps": (
            [((56, 128), F32)] * 2,
            [cells, packed, ((groups, 256, lon), BF16), ((7, 2, 8, 128), F32)],
        ),
        "spread": ([field], [*tiles, cells, packed, ((groups, 256, lon), F32)]),
        "final": (
            [
                ((channels // shards, hidden), F32),
                ((hidden // shards, channels), F32),
                ((7, 7, channels), F32),
                ((channels,), F32),
                ((hidden,), F32),
            ],
            [],
        ),
    }


def per_device(fields, cotangent, land_sea, kernel, ln_gain, weight_in, bias_in, weight_out):
    samples, lat, lon, channels = fields.shape
    hidden = weight_in.shape[1]
    shards, tiles = lax.axis_size("dp"), lax.axis_size("lon")
    core = (lax.axis_index("lon") & 1).reshape(1)
    fields = fields[0].transpose(0, 2, 1)
    cotangent = cotangent[0].transpose(0, 2, 1)
    w_out = weight_out.T
    of = shapes(lat, channels, lon, hidden, shards)

    first, last = call(edge_kernel, "edges", *of["edges"])(fields, cotangent, land_sea)
    up = [(i, (i + 1) % tiles) for i in range(tiles)]
    before = lax.ppermute(last, "lon", up)
    after = lax.ppermute(first, "lon", [(j, i) for i, j in up])
    lines, flipped = lines_of(kernel[::-1]), lines_of(kernel[:, ::-1])

    output, d_conv, d_edge, keep, send, sums = call(
        functools.partial(forward_kernel, shards=shards),
        "forward",
        *of["forward"],
        specs=with_core(10),
    )(core, fields, cotangent, land_sea, before, after, lines, ln_gain, weight_in, bias_in, w_out)

    dp_bits, lon_bits = bits_of(shards), bits_of(tiles)
    mine = both(keep, swapped(send, "lon", 1)).reshape(shards, -1, 128)
    kept, sent = halved(mine, dp_bits[0])
    arrived = swapped(sent, "dp", dp_bits[0])

    small, send = call(taps_kernel, "taps", *of["taps"], specs=with_core(5))(
        core, fields, land_sea, d_conv, d_edge, sums
    )
    small = small + swapped(send, "lon", 1)

    (grad_fields,) = call(spread_kernel, "spread", *of["spread"])(
        cotangent, land_sea, flipped, d_conv, d_edge
    )

    mine = both(kept, arrived.reshape(kept.shape))
    for bit in dp_bits[1:]:
        kept, sent = halved(mine, bit)
        arrived = swapped(jnp.concatenate([sent, two_parts(small)], axis=0), "dp", bit)
        mine = both(kept, arrived[: sent.shape[0]].reshape(kept.shape))
        small = small + one_part(arrived[sent.shape[0] :])
    mine = mine.reshape(-1, 128)
    for bit in lon_bits[1:]:
        arrived = swapped(jnp.concatenate([mine, two_parts(small)], axis=0), "lon", bit)
        small = small + one_part(arrived[mine.shape[0] :])
        mine = both(mine, arrived[: mine.shape[0]])
    small = small + one_part(swapped(two_parts(small), "dp", dp_bits[0]))
    other = swapped(mine, "lon", 1)
    small_other = swapped(small, "lon", 1)

    scale = 1.0 / math.sqrt(samples * lat * lon * shards * tiles)
    grads = call(
        functools.partial(final_kernel, scale=scale), "final", *of["final"], specs=with_core(4)
    )(core, mine, other, small, small_other)
    return (output.transpose(0, 2, 1)[None], grad_fields.transpose(0, 2, 1)[None], *grads)


def solution(mesh):
    placed = (
        P("dp", None, "lon", None),
        P("dp", None, "lon", None),
        P(None, "lon"),
        P(),
        P(),
        P(),
        P(),
        P(),
    )
    return jax.shard_map(
        per_device,
        mesh=mesh,
        in_specs=placed,
        out_specs=(
            P("dp", None, "lon", None),
            P("dp", None, "lon", None),
            P("dp", None),
            P("dp", None),
            P(),
            P(),
            P(),
        ),
        check_vma=False,
    )
```

```python
import functools
import math

import jax
import jax.numpy as jnp
from jax import lax
from jax.experimental import pallas as pl
from jax.experimental.pallas import tpu as pltpu
from jax.sharding import PartitionSpec as P

F32 = jnp.float32
BF16 = jnp.bfloat16
EDGE = 8
GROUP = 16


def dot(lhs, rhs):
    return jnp.dot(lhs, rhs, preferred_element_type=F32)


def dot_t(lhs, rhs):
    return lax.dot_general(lhs, rhs, (((1,), (1,)), ((), ())), preferred_element_type=F32)


def iota(shape, axis):
    return lax.broadcasted_iota(jnp.int32, shape, axis)


def identity(size):
    return jnp.where(iota((size, size), 0) == iota((size, size), 1), 1.0, 0.0).astype(BF16)


def masked_row(array, mask, i):
    return (array[i].astype(F32) * mask[i : i + 1].astype(F32)).astype(BF16)


def group_of(rows, g):
    return jnp.concatenate([row[GROUP * g : GROUP * (g + 1)] for row in rows], axis=0)


def band_mask(i):
    shape = (GROUP, 256)
    lane = iota(shape, 1)
    same = (lane & (GROUP - 1)) == iota(shape, 0)
    return same & (jnp.abs((lane >> 4) - i) <= 3)


def unrolled(count, body):
    for k in range(count):
        body(k)


def lay_lines(kernel, lines):
    taps, cols, channels = kernel.shape
    lane = iota((1, 128), 1) >> 4
    zero = jnp.zeros((1, channels), F32)
    rows = [jnp.concatenate([kernel[a], zero], axis=0) for a in range(taps)]
    for g in range(channels // GROUP):
        tile = g * GROUP // 128 * 128
        halves = [jnp.zeros((8, 128), F32)] * 2
        for a in range(taps):
            piece = rows[a][:, tile : min(tile + 128, channels)]
            if piece.shape[1] < 128:
                piece = jnp.concatenate([piece, piece], axis=1)
            for half, slot in ((0, taps - 1 - a), (1, a)):
                moved = pltpu.roll(piece, (slot - g) % 8 * GROUP, axis=1)
                halves[half] = jnp.where(lane == slot, moved, halves[half])
        lines[8 * g : 8 * g + 8] = jnp.concatenate(halves, axis=1)


def build_tiles(lines, rolled, tiles, flip):
    here = iota((1, 256), 1) < 128
    own = jnp.where(here, pltpu.roll(lines[...], 128, axis=1) if flip else lines[...], 0.0)
    for i in range(16):
        rolled[i] = pltpu.roll(own, ((i - 3) * GROUP) % 256, axis=1)
    masks = [band_mask(i) for i in range(16)]

    def group(g):
        for b in range(7):
            for i in range(16):
                k = 8 * g + (6 - b if flip else b)
                line = rolled[i, k : k + 1, :]
                at = b * 256 + i * GROUP
                tiles[g, at : at + GROUP, :] = jnp.where(masks[i], line, 0.0).astype(BF16)

    unrolled(tiles.shape[0], group)


def pack_shifts(cells, packed, lon):
    def group(g):
        for half in range(2):
            for b in range(7):
                x = cells[2 * g + half, 2 * EDGE + b - 3 : 2 * EDGE + b - 3 + lon, :]
                at = b * 256 + half * 128
                packed[g, :, at : at + 128] = x.astype(BF16)

    unrolled(packed.shape[0], group)


BORDER = 24


def pack_borders(before, after, borders, left, right, packed):
    groups = packed.shape[0]
    near = iota((EDGE, 1), 0) < EDGE // 2
    blank = jnp.zeros((EDGE, 128), F32)

    def group(g):
        for half in range(2):
            k = 2 * g + half
            at = half * groups * EDGE + g * EDGE
            halo = slice(at, at + EDGE)
            left[k] = jnp.concatenate([blank, before[halo], borders[k, :BORDER]], axis=0)
            right[k] = jnp.concatenate([borders[k, BORDER:], after[halo], blank], axis=0)
            for b in range(7):
                s = b - 3
                inner = left[k, 2 * EDGE + s : 2 * EDGE + s + 16, :]
                outer = right[k, BORDER - 16 + s : BORDER + s, :]
                beyond = jnp.where(
                    near,
                    right[k, BORDER + s : BORDER + s + EDGE, :],
                    left[k, EDGE + s : 2 * EDGE + s, :],
                )
                x = jnp.concatenate([inner, outer, beyond, beyond], axis=0)
                at = b * 256 + half * 128
                packed[g, :, at : at + 128] = x.astype(BF16)

    unrolled(groups, group)


def gelu_parts(z):
    cumulative = 0.5 + 0.5 * lax.erf(z * math.sqrt(0.5))
    density = jnp.exp2(z * z * (-0.5 * math.log2(math.e))) * (1.0 / math.sqrt(2.0 * math.pi))
    return cumulative, density


def edge_kernel(fields, cotangent, mask, first, last, masked, gm):
    lat, channels, lon = fields.shape
    groups = channels // GROUP
    row, lane = iota((2 * EDGE, lon), 0), iota((2 * EDGE, lon), 1)
    ends = jnp.where(lane == jnp.where(row < EDGE, row, row + lon - 2 * EDGE), 1.0, 0.0)
    ends = ends.astype(BF16)
    rows = [masked_row(fields, mask, i) for i in range(lat)]
    cells = [dot_t(ends, group_of(rows, g)) for g in range(groups)]
    turned = [masked_row(cotangent, mask, i) for i in range(lat)]
    outer = [dot_t(ends, g) for g in turned]
    for i in range(lat):
        masked[i] = rows[i]
        gm[i] = turned[i]
    for k, out in enumerate((first, last)):
        for half in range(2):
            at = slice(half * 128, (half + 1) * 128)
            x = [cell[k * EDGE : (k + 1) * EDGE, at] for cell in cells]
            count = groups * EDGE
            out[half * count : (half + 1) * count] = jnp.concatenate(x, axis=0).astype(BF16)
        g = jnp.concatenate([x[k * EDGE : (k + 1) * EDGE] for x in outer], axis=0)
        out[2 * groups * EDGE :] = g.T.astype(BF16)


def prepare_kernel(
    masked,
    kernel,
    gain,
    w_in,
    bias,
    w_out,
    tiles,
    packed,
    borders,
    turned_in,
    turned_out,
    near_in,
    near_out,
    gain_columns,
    lines,
    rolled,
    cells,
):
    lat, channels, lon = masked.shape
    hidden = w_in.shape[1]
    groups = channels // GROUP
    lay_lines(kernel, lines)
    build_tiles(lines, rolled, tiles, False)
    gain_row = gain[...].reshape(1, channels)
    gain_columns[...] = jnp.broadcast_to(gain_row, (128, channels)).T
    bias_row = bias[...].reshape(1, hidden)
    bias_columns = jnp.broadcast_to(bias_row, (64, hidden)).T
    lane = iota((hidden, 64), 1)
    high = bias_columns.astype(BF16).astype(F32)
    middle = (bias_columns - high).astype(BF16).astype(F32)
    low = bias_columns - high - middle
    bias_columns = jnp.where(
        lane == 0, high, jnp.where(lane == 1, middle, jnp.where(lane == 2, low, 0.0))
    )
    turned_in[...] = jnp.concatenate([w_in[...].astype(F32).T, bias_columns], axis=1).astype(BF16)
    turned_out[...] = w_out[...].T
    near_in[...] = w_in[...]
    near_out[...] = w_out[...]

    rows = [masked[i] for i in range(lat)]
    blank = jnp.zeros((2 * EDGE, 128), F32)
    for g in range(groups):
        x = group_of(rows, g).astype(F32).T
        for half in range(2):
            k = 2 * g + half
            part = x[:, half * 128 : (half + 1) * 128]
            cells[k] = jnp.concatenate([blank, part, blank], axis=0)
            borders[k] = jnp.concatenate([part[:BORDER], part[lon - BORDER :]], axis=0)
    pack_shifts(cells, packed, lon)


def forward_kernel(
    core,
    halo_before,
    halo_after,
    masked,
    gm,
    mask,
    tiles,
    packed,
    borders,
    turned_in,
    turned_out,
    w_in,
    w_out,
    gain_columns,
    output,
    d_conv,
    d_edge,
    keep,
    send,
    sums,
    left,
    right,
    packed_border,
    conv,
    conv_edge,
    total_in,
    total_out,
    total_gain,
    rows_out,
    sent,
    shards,
):
    lat, channels, lon = masked.shape
    hidden = w_in.shape[1]
    groups = channels // GROUP
    before, after = halo_before[...].astype(F32), halo_after[...].astype(F32)
    pack_borders(before, after, borders, left, right, packed_border)

    def band(g):
        border = packed_border[g]
        x = jnp.concatenate([border[:16], packed[g, 16 : lon - 16], border[16:]], axis=0)
        y = dot(x, tiles[g])
        conv[g] = y[:lon].T
        conv_edge[g] = y[lon : lon + EDGE]

    unrolled(groups, band)

    total_in[...] = jnp.zeros_like(total_in)
    total_out[...] = jnp.zeros_like(total_out)
    total_gain[...] = jnp.zeros_like(total_gain)

    def block(y, g, inner):
        cols = y.shape[1]
        gains = jnp.concatenate([gain_columns[...]] * (cols // 128), axis=1)
        y = y - jnp.sum(y, axis=0, keepdims=True) * (1.0 / channels)
        var = jnp.sum(y * y, axis=0, keepdims=True) * (1.0 / channels)
        sigma = lax.rsqrt(var + 1e-6)
        nhat = y * sigma
        normed = (nhat * gains).astype(BF16)
        normed = jnp.concatenate([normed, jnp.ones((64, cols), BF16)], axis=0)
        if inner:
            upright, g_upright = normed.T, g.T
        branch, d_normed = None, None
        for h in range(0, hidden, 256):
            at = slice(h, h + 256)
            z = dot(turned_in[at, :], normed)
            cumulative, density = gelu_parts(z)
            d_act = dot(turned_out[at, :], g)
            d_pre = (d_act * (cumulative + z * density)).astype(BF16)
            part = dot(w_in[:, at], d_pre)
            d_normed = part if d_normed is None else d_normed + part
            if inner:
                act = (z * cumulative).astype(BF16)
                part = dot(w_out[:, at], act)
                branch = part if branch is None else branch + part
                total_in[at, :] += dot(d_pre, upright)
                total_out[at, :] += dot(act, g_upright)
        prod = d_normed * nhat
        if inner:
            part = prod[:, :128]
            for c in range(128, cols, 128):
                part = part + prod[:, c : c + 128]
            total_gain[...] += part
        d_hat = d_normed * gains
        mean = jnp.sum(d_hat, axis=0, keepdims=True) * (1.0 / channels)
        corr = jnp.sum(prod * gains, axis=0, keepdims=True) * (1.0 / channels)
        return (sigma * (d_hat - mean - nhat * corr)).astype(BF16), branch

    count = 4
    copies = []

    def rows_block(r):
        rows = range(count * r, count * (r + 1))
        y = []
        for i in rows:
            at = slice(i * GROUP, (i + 1) * GROUP)
            y.append(jnp.concatenate([conv[g, at, :] for g in range(groups)], axis=0))
        d, branch = block(
            jnp.concatenate(y, axis=1), jnp.concatenate([gm[i] for i in rows], axis=1), True
        )
        for k, i in enumerate(rows):
            at = slice(k * lon, (k + 1) * lon)
            m = mask[i : i + 1].astype(F32)
            rows_out[i] = ((masked[i].astype(F32) + branch[:, at]) * m).astype(BF16)
            d_conv[i] = d[:, at]
        copies.append(
            pltpu.make_async_copy(
                rows_out.at[count * r : count * (r + 1)],
                output.at[count * r : count * (r + 1)],
                sent.at[r],
            )
        )
        copies[-1].start()

    unrolled(lat // count, rows_block)

    lane = iota((1, 128), 1)
    y = []
    for i in range(lat):
        half, k = (i * GROUP) // 128 * 128, i % 8
        line = []
        for tile in range(0, channels, 128):
            x = jnp.zeros((EDGE, 128), F32)
            for g in range(tile // GROUP, min(tile + 128, channels) // GROUP):
                piece = pltpu.roll(conv_edge[g, :, half : half + 128], (g - k) % 8 * GROUP, axis=1)
                x = jnp.where((lane >> 4) == g % 8, piece, x)
            line.append(x)
        y.append(jnp.concatenate(line, axis=1))
    y = jnp.concatenate(y, axis=0).T[:channels]
    at = 2 * groups * EDGE
    g = jnp.where((lane & (EDGE - 1)) < EDGE // 2, after[at:], before[at:]).astype(BF16)
    d_edge[...], _ = block(y, g, False)

    first = core[0] == 0
    rows = channels // shards
    sum_in = total_in[...].T
    parts_in, parts_out = [], []
    for n in range(shards):
        mine = sum_in[n * rows : (n + 1) * rows]
        parts_in += [mine[:, c : c + 128] for c in range(0, hidden, 128)]
    rows = hidden // shards
    for n in range(shards):
        mine = total_out[n * rows : (n + 1) * rows]
        parts_out.append(mine[:, :128])
        parts_out.append(
            jnp.concatenate([mine[: rows // 2, 128:], mine[rows // 2 :, 128:]], axis=1)
        )
    parts_in, parts_out = jnp.concatenate(parts_in, axis=0), jnp.concatenate(parts_out, axis=0)
    keep[...] = jnp.where(first, parts_in, parts_out).astype(BF16)
    send[...] = jnp.where(first, parts_out, parts_in).astype(BF16)
    sums[:, :hidden] = sum_in[channels : channels + 8]
    sums[:, hidden:] = jnp.broadcast_to(
        jnp.sum(total_gain[...].T, axis=0, keepdims=True), (8, channels)
    )
    for copy in copies:
        copy.wait()


def lay_cells(d_conv, d_edge, cells):
    lat, channels, lon = d_conv.shape
    rows = [d_conv[i] for i in range(lat)]
    near = iota((EDGE, 1), 0) < EDGE // 2
    lane = iota((1, 128), 1) >> 4
    blank = jnp.zeros((EDGE, 128), F32)
    edges = d_edge[...].astype(F32).T
    for g in range(channels // GROUP):
        x = group_of(rows, g).astype(F32).T
        tile = (g * GROUP) // 128 * 128
        for half in range(2):
            edge = blank
            for k in range(8):
                i = 8 * half + k
                piece = edges[i * EDGE : (i + 1) * EDGE, tile : min(tile + 128, channels)]
                if piece.shape[1] < 128:
                    piece = jnp.concatenate([piece, piece], axis=1)
                shift = (k * GROUP - (g * GROUP - tile)) % 128
                edge = jnp.where(lane == k, pltpu.roll(piece, shift, axis=1), edge)
            cells[2 * g + half] = jnp.concatenate(
                [
                    blank,
                    jnp.where(near, 0.0, edge),
                    x[:, half * 128 : (half + 1) * 128],
                    jnp.where(near, edge, 0.0),
                    blank,
                ],
                axis=0,
            )


def taps_kernel(core, masked, d_conv, d_edge, sums, keep, send, cells, packed, small):
    lat, channels, lon = masked.shape
    groups = channels // GROUP
    lay_cells(d_conv, d_edge, cells)
    pack_shifts(cells, packed, lon)
    rows = [masked[i] for i in range(lat)]
    bands = [band_mask(i) for i in range(lat)]
    sub, lane = iota((8, 1), 0), iota((1, 128), 1) >> 4
    small[...] = jnp.zeros_like(small)

    for g in range(groups):
        g_all = dot(group_of(rows, g), packed[g])
        taps = jnp.zeros((8, 128), F32)
        for b in range(7):
            total = None
            for i in range(lat):
                part = g_all[i * GROUP : (i + 1) * GROUP, b * 256 : (b + 1) * 256]
                part = jnp.where(bands[i], part, 0.0)
                part = part[:8] + part[8:]
                part = pltpu.roll(part, ((3 - i) * GROUP) % 256, axis=1)[:, :128]
                total = part if total is None else total + part
            total = jnp.sum(total, axis=0, keepdims=True)
            taps = jnp.where(sub == 6 - b, total, taps)
        place = g * GROUP // 128
        for a in range(7):
            shift = (g * GROUP - (6 - a) * GROUP) % 128
            moved = pltpu.roll(taps, shift, axis=1)
            small[a, place] = jnp.where(lane == g % 8, moved, small[a, place])

    line = sums[0:1]
    hidden = line.shape[1] - channels
    pieces = [line[:, c : c + 128] for c in range(0, hidden, 128)]
    pieces.append(line[:, hidden : hidden + 128])
    pieces.append(
        jnp.concatenate([line[:, hidden + 128 :], jnp.zeros((1, 256 - channels), F32)], axis=1)
    )
    for k, piece in enumerate(pieces):
        small[k // 2, k % 2, 7:8] = piece
    flat = small[...].reshape(112, 128)
    first = core[0] == 0
    keep[...] = jnp.where(first, flat[:56], flat[56:])
    send[...] = jnp.where(first, flat[56:], flat[:56])


def spread_kernel(gm, mask, lines, d_conv, d_edge, grad_fields, rolled, tiles, cells, packed, spread):
    lat, channels, lon = gm.shape
    groups = channels // GROUP
    build_tiles(lines, rolled, tiles, True)
    lay_cells(d_conv, d_edge, cells)
    pack_shifts(cells, packed, lon)

    def band(g):
        spread[g] = dot(packed[g], tiles[g]).T

    unrolled(groups, band)
    for i in range(lat):
        x = jnp.concatenate(
            [spread[g, i * GROUP : (i + 1) * GROUP, :] for g in range(groups)], axis=0
        )
        x = gm[i].astype(F32) + x * mask[i : i + 1].astype(F32)
        grad_fields[i] = x.astype(BF16)


def final_kernel(core, mine, other, small_mine, small_other, grad_in, grad_out, grad_kernel, grad_gain, grad_bias, scale):
    first = core[0] == 0
    mine, other = mine[...].astype(F32) * scale, other[...].astype(F32) * scale
    sum_in, sum_out = jnp.where(first, mine, other), jnp.where(first, other, mine)
    mine, other = small_mine[...] * scale, small_other[...] * scale
    small = jnp.concatenate(
        [jnp.where(first, mine, other), jnp.where(first, other, mine)], axis=0
    )
    rows, hidden = grad_in.shape
    for k in range(hidden // 128):
        grad_in[:, k * 128 : (k + 1) * 128] = sum_in[k * rows : (k + 1) * rows]
    rows, channels = grad_out.shape
    grad_out[:, :128] = sum_out[:rows]
    rest = sum_out[rows:]
    grad_out[:, 128:] = jnp.concatenate([rest[:, :64], rest[:, 64:]], axis=0)
    for a in range(7):
        grad_kernel[a, :, :128] = small[16 * a : 16 * a + 7]
        grad_kernel[a, :, 128:] = small[16 * a + 8 : 16 * a + 15, : channels - 128]
    lines = [small[8 * k + 7 : 8 * k + 8] for k in range(hidden // 128 + 2)]
    grad_bias[...] = jnp.concatenate(lines[:-2], axis=1).reshape(hidden)
    grad_gain[...] = jnp.concatenate([lines[-2], lines[-1][:, : channels - 128]], axis=1).reshape(
        channels
    )


def swapped(x, axis, bit):
    peers = lax.axis_size(axis)
    return lax.ppermute(x, axis, [(i, i ^ bit) for i in range(peers)])


def bits_of(count):
    return [1 << k for k in range(count.bit_length() - 1)]


def pick(x, axis, at):
    return lax.dynamic_index_in_dim(x, at, axis, keepdims=False)


def both(x, y):
    return (x.astype(F32) + y.astype(F32)).astype(BF16)


def halved(mine, bit):
    have = (lax.axis_index("dp") // bit) & 1
    split = mine.reshape(mine.shape[0] // 2, 2, -1, 128)
    kept, sent = pick(split, 1, have), pick(split, 1, 1 - have)
    return kept, sent.reshape(-1, 128)


def two_parts(x):
    high = lax.reduce_precision(x, exponent_bits=8, mantissa_bits=7)
    return jnp.concatenate([high, x - high], axis=0).astype(BF16)


def one_part(x):
    rows = x.shape[0] // 2
    return x[:rows].astype(F32) + x[rows:].astype(F32)


HBM, VMEM, SMEM = pltpu.HBM, pltpu.VMEM, pltpu.SMEM


def call(body, name, outs, scratch, megabytes, spaces, out_spaces):
    def held(space, shape, dtype):
        return VMEM(shape, dtype) if space is VMEM else jax.ShapeDtypeStruct(shape, dtype)

    def spec(space):
        return pl.BlockSpec(memory_space={SMEM: SMEM, pl.ANY: pl.ANY}.get(space, VMEM))

    kernel = pl.pallas_call(
        body,
        out_shape=[held(space, *out) for space, out in zip(out_spaces, outs, strict=True)],
        in_specs=[spec(space) for space in spaces],
        out_specs=[spec(space) for space in out_spaces],
        scratch_shapes=[x if not isinstance(x, tuple) else VMEM(*x) for x in scratch],
        compiler_params=pltpu.CompilerParams(vmem_limit_bytes=megabytes * 2**20),
        name=name,
    )

    def run(*args):
        return kernel(
            *[
                pltpu.with_memory_space_constraint(x, space) if space in (HBM, VMEM) else x
                for x, space in zip(args, spaces, strict=True)
            ]
        )

    return run


def per_device(fields, cotangent, land_sea, kernel, ln_gain, weight_in, bias_in, weight_out):
    samples, lat, lon, channels = fields.shape
    hidden = weight_in.shape[1]
    shards, tiles = lax.axis_size("dp"), lax.axis_size("lon")
    groups = channels // GROUP
    rows = channels * hidden // 128
    core = (lax.axis_index("lon") & 1).reshape(1)
    fields = fields[0].transpose(0, 2, 1)
    cotangent = cotangent[0].transpose(0, 2, 1)
    w_out = weight_out.T

    field = ((lat, channels, lon), BF16)
    halo = ((2 * channels, 128), BF16)
    edge = ((channels, 128), BF16)
    rolled = ((16, 8 * groups, 256), F32)
    tile = ((groups, 7 * 256, 256), BF16)
    cells = ((2 * groups, lon + 4 * EDGE, 128), F32)
    packed = ((groups, lon, 7 * 256), BF16)
    border = ((2 * groups, 2 * EDGE + BORDER, 128), F32)
    held = ((groups, 256, lon), F32)

    first, last, masked, gm = call(
        edge_kernel, "edges", [halo, halo, field, field], [], 8, [HBM] * 3, [None, None, VMEM, VMEM]
    )(fields, cotangent, land_sea)
    up = [(i, (i + 1) % tiles) for i in range(tiles)]
    before = lax.ppermute(last, "lon", up)
    after = lax.ppermute(first, "lon", [(j, i) for i, j in up])

    ready = call(
        prepare_kernel,
        "prepare",
        [
            tile,
            packed,
            ((2 * groups, 2 * BORDER, 128), F32),
            ((hidden, 256), BF16),
            ((hidden, channels), BF16),
            ((channels, hidden), BF16),
            ((channels, hidden), BF16),
            ((channels, 128), F32),
            ((8 * groups, 256), F32),
        ],
        [rolled, cells],
        16,
        [VMEM] + [HBM] * 5,
        [VMEM] * 9,
    )(masked, kernel, ln_gain, weight_in, bias_in, w_out)
    lines = ready[-1]

    output, d_conv, d_edge, keep, send, sums = call(
        functools.partial(forward_kernel, shards=shards),
        "forward",
        [
            field,
            field,
            edge,
            ((rows, 128), BF16),
            ((rows, 128), BF16),
            ((8, hidden + channels), F32),
        ],
        [
            border,
            border,
            ((groups, 48, 7 * 256), BF16),
            held,
            ((groups, EDGE, 256), F32),
            ((hidden, 256), F32),
            ((hidden, channels), F32),
            ((channels, 128), F32),
            field,
            pltpu.SemaphoreType.DMA((lat // 4,)),
        ],
        20,
        [SMEM, HBM, HBM, VMEM, VMEM, HBM] + [VMEM] * 8,
        [pl.ANY] + [VMEM] * 2 + [None] * 2 + [VMEM],
    )(core, before, after, masked, gm, land_sea, *ready[:-1])

    dp_bits, lon_bits = bits_of(shards), bits_of(tiles)
    arrived = swapped(send, "lon", 1)
    small, send = call(
        taps_kernel,
        "taps",
        [((56, 128), F32)] * 2,
        [cells, packed, ((7, 2, 8, 128), F32)],
        20,
        [SMEM] + [VMEM] * 4,
        [None] * 2,
    )(core, masked, d_conv, d_edge, sums)
    small = small + swapped(send, "lon", 1)
    mine = both(keep, arrived).reshape(shards, -1, 128)
    for bit in dp_bits:
        kept, sent = halved(mine, bit)
        sent = jnp.concatenate([sent, two_parts(small)], axis=0)
        if bit == 1:
            sent, d_conv = lax.optimization_barrier((sent, d_conv))
        arrived = swapped(sent, "dp", bit)
        if bit == 1:
            (grad_fields,) = call(
                spread_kernel,
                "spread",
                [field],
                [rolled, tile, cells, packed, held],
                32,
                [VMEM, HBM] + [VMEM] * 3,
                [None],
            )(gm, land_sea, lines, d_conv, d_edge)
            arrived, grad_fields = lax.optimization_barrier((arrived, grad_fields))
        count = kept.size // 128
        mine = both(kept, arrived[:count].reshape(kept.shape))
        small = small + one_part(arrived[count:])
    mine = mine.reshape(-1, 128)
    for bit in lon_bits[1:]:
        arrived = swapped(jnp.concatenate([mine, two_parts(small)], axis=0), "lon", bit)
        small = small + one_part(arrived[mine.shape[0] :])
        mine = both(mine, arrived[: mine.shape[0]])
    other = swapped(mine, "lon", 1)
    small_other = swapped(small, "lon", 1)

    scale = 1.0 / math.sqrt(samples * lat * lon * shards * tiles)
    grads = call(
        functools.partial(final_kernel, scale=scale),
        "final",
        [
            ((channels // shards, hidden), F32),
            ((hidden // shards, channels), F32),
            ((7, 7, channels), F32),
            ((channels,), F32),
            ((hidden,), F32),
        ],
        [],
        8,
        [SMEM] + [None] * 4,
        [None] * 5,
    )(core, mine, other, small, small_other)
    return (output.transpose(0, 2, 1)[None], grad_fields.transpose(0, 2, 1)[None], *grads)


def solution(mesh):
    placed = (
        P("dp", None, "lon", None),
        P("dp", None, "lon", None),
        P(None, "lon"),
        P(),
        P(),
        P(),
        P(),
        P(),
    )
    return jax.shard_map(
        per_device,
        mesh=mesh,
        in_specs=placed,
        out_specs=(
            P("dp", None, "lon", None),
            P("dp", None, "lon", None),
            P("dp", None),
            P("dp", None),
            P(),
            P(),
            P(),
        ),
        check_vma=False,
    )
```

```python
import functools
import math

import jax
import jax.numpy as jnp
from jax import lax
from jax.experimental import pallas as pl
from jax.experimental.pallas import tpu as pltpu
from jax.sharding import PartitionSpec as P

F32 = jnp.float32
BF16 = jnp.bfloat16
EDGE = 8
GROUP = 16


def dot(lhs, rhs):
    return jnp.dot(lhs, rhs, preferred_element_type=F32)


def dot_t(lhs, rhs):
    return lax.dot_general(lhs, rhs, (((1,), (1,)), ((), ())), preferred_element_type=F32)


def iota(shape, axis):
    return lax.broadcasted_iota(jnp.int32, shape, axis)


def identity(size):
    return jnp.where(iota((size, size), 0) == iota((size, size), 1), 1.0, 0.0).astype(BF16)


def masked_row(array, mask, i):
    return (array[i].astype(F32) * mask[i : i + 1]).astype(BF16)


def group_of(rows, g):
    return jnp.concatenate([row[GROUP * g : GROUP * (g + 1)] for row in rows], axis=0)


def band_mask(i):
    shape = (GROUP, 256)
    lane = iota(shape, 1)
    same = (lane & (GROUP - 1)) == iota(shape, 0)
    return same & (jnp.abs((lane >> 4) - i) <= 3)


def unrolled(count, body):
    for k in range(count):
        body(k)


def lay_lines(kernel, lines):
    taps, cols, channels = kernel.shape
    lane = iota((1, 128), 1) >> 4
    zero = jnp.zeros((1, channels), F32)
    rows = [jnp.concatenate([kernel[a], zero], axis=0) for a in range(taps)]
    for g in range(channels // GROUP):
        tile = g * GROUP // 128 * 128
        halves = [jnp.zeros((8, 128), F32)] * 2
        for a in range(taps):
            piece = rows[a][:, tile : min(tile + 128, channels)]
            if piece.shape[1] < 128:
                piece = jnp.concatenate([piece, piece], axis=1)
            for half, slot in ((0, taps - 1 - a), (1, a)):
                moved = pltpu.roll(piece, (slot - g) % 8 * GROUP, axis=1)
                halves[half] = jnp.where(lane == slot, moved, halves[half])
        lines[8 * g : 8 * g + 8] = jnp.concatenate(halves, axis=1)


def build_tiles(lines, rolled, tiles, flip):
    here = iota((1, 256), 1) < 128
    own = jnp.where(here, pltpu.roll(lines[...], 128, axis=1) if flip else lines[...], 0.0)
    for i in range(16):
        rolled[i] = pltpu.roll(own, ((i - 3) * GROUP) % 256, axis=1)
    masks = [band_mask(i) for i in range(16)]

    def group(g):
        for b in range(7):
            for i in range(16):
                k = 8 * g + (6 - b if flip else b)
                line = rolled[i, k : k + 1, :]
                at = b * 256 + i * GROUP
                tiles[g, at : at + GROUP, :] = jnp.where(masks[i], line, 0.0).astype(BF16)

    unrolled(tiles.shape[0], group)


def pack_group(cells, packed, lon, g):
    for half in range(2):
        for b in range(7):
            x = cells[2 * g + half, 2 * EDGE + b - 3 : 2 * EDGE + b - 3 + lon, :]
            at = b * 256 + half * 128
            packed[g, :, at : at + 128] = x.astype(BF16)


BORDER = 24
SMALL = 64


def pack_borders(before, after, borders, left, right, packed):
    groups = packed.shape[0]
    near = iota((EDGE, 1), 0) < EDGE // 2
    blank = jnp.zeros((EDGE, 128), F32)

    def place(g):
        for half in range(2):
            k = 2 * g + half
            at = half * groups * EDGE + g * EDGE
            halo = slice(at, at + EDGE)
            left[k] = jnp.concatenate([blank, before[halo], borders[k, :BORDER]], axis=0)
            right[k] = jnp.concatenate([borders[k, BORDER:], after[halo], blank], axis=0)
            for b in range(7):
                s = b - 3
                inner = left[k, 2 * EDGE + s : 2 * EDGE + s + 16, :]
                outer = right[k, BORDER - 16 + s : BORDER + s, :]
                beyond = jnp.where(
                    near,
                    right[k, BORDER + s : BORDER + s + EDGE, :],
                    left[k, EDGE + s : 2 * EDGE + s, :],
                )
                x = jnp.concatenate([inner, outer, beyond, beyond], axis=0)
                at = b * 256 + half * 128
                packed[g, :, at : at + 128] = x.astype(BF16)

    return place


def gelu_parts(z):
    cumulative = 0.5 + 0.5 * lax.erf(z * math.sqrt(0.5))
    density = jnp.exp2(z * z * (-0.5 * math.log2(math.e))) * (1.0 / math.sqrt(2.0 * math.pi))
    return cumulative, density


def edge_kernel(
    fields, cotangent, mask, first, last, masked, gm, near_mask, held_x, held_g, held_mask, arrived
):
    lat, channels, lon = fields.shape
    groups = channels // GROUP
    count = lat // 4
    copies = [pltpu.make_async_copy(mask, held_mask, arrived.at[0])]
    for r in range(4):
        at = slice(count * r, count * (r + 1))
        for k, (far, held) in enumerate(((fields, held_x), (cotangent, held_g))):
            copies.append(
                pltpu.make_async_copy(far.at[at], held.at[at], arrived.at[1 + 2 * r + k])
            )
    for copy in copies:
        copy.start()
    row, lane = iota((2 * EDGE, lon), 0), iota((2 * EDGE, lon), 1)
    ends = jnp.where(lane == jnp.where(row < EDGE, row, row + lon - 2 * EDGE), 1.0, 0.0)
    ends = ends.astype(BF16)
    copies[0].wait()
    near_mask[...] = held_mask[...].astype(F32)
    rows, outer = [], []
    for r in range(4):
        copies[1 + 2 * r].wait()
        copies[2 + 2 * r].wait()
        for i in range(count * r, count * (r + 1)):
            rows.append(masked_row(held_x, near_mask, i))
            turned = masked_row(held_g, near_mask, i)
            outer.append(dot_t(ends, turned))
            masked[i] = rows[i]
            gm[i] = turned
    cells = [dot_t(ends, group_of(rows, g)) for g in range(groups)]
    for k, out in enumerate((first, last)):
        for half in range(2):
            at = slice(half * 128, (half + 1) * 128)
            x = [cell[k * EDGE : (k + 1) * EDGE, at] for cell in cells]
            count = groups * EDGE
            out[half * count : (half + 1) * count] = jnp.concatenate(x, axis=0).astype(BF16)
        g = jnp.concatenate([x[k * EDGE : (k + 1) * EDGE] for x in outer], axis=0)
        out[2 * groups * EDGE :] = g.T.astype(BF16)


def prepare_kernel(
    masked,
    kernel,
    gain,
    w_in,
    bias,
    w_out,
    tiles,
    packed,
    borders,
    turned_in,
    turned_out,
    near_in,
    near_out,
    gain_columns,
    lines,
    rolled,
    cells,
    near_kernel,
    near_gain,
    near_bias,
    arrived,
):
    lat, channels, lon = masked.shape
    hidden = w_in.shape[1]
    groups = channels // GROUP
    far = (kernel, gain, w_in, bias, w_out)
    near = (near_kernel, near_gain, near_in, near_bias, near_out)
    copies = [
        pltpu.make_async_copy(x, y, arrived.at[k])
        for k, (x, y) in enumerate(zip(far, near, strict=True))
    ]
    for copy in copies:
        copy.start()

    rows = [masked[i] for i in range(lat)]
    blank = jnp.zeros((2 * EDGE, 128), F32)
    for g in range(groups):
        x = group_of(rows, g).astype(F32).T
        for half in range(2):
            k = 2 * g + half
            part = x[:, half * 128 : (half + 1) * 128]
            cells[k] = jnp.concatenate([blank, part, blank], axis=0)
            borders[k] = jnp.concatenate([part[:BORDER], part[lon - BORDER :]], axis=0)
        pack_group(cells, packed, lon, g)

    for copy in copies:
        copy.wait()
    lay_lines(near_kernel, lines)
    build_tiles(lines, rolled, tiles, False)
    gain_row = near_gain[...].reshape(1, channels)
    gain_columns[...] = jnp.broadcast_to(gain_row, (128, channels)).T
    bias_row = near_bias[...].reshape(1, hidden)
    bias_columns = jnp.broadcast_to(bias_row, (64, hidden)).T
    lane = iota((hidden, 64), 1)
    high = bias_columns.astype(BF16).astype(F32)
    middle = (bias_columns - high).astype(BF16).astype(F32)
    low = bias_columns - high - middle
    bias_columns = jnp.where(
        lane == 0, high, jnp.where(lane == 1, middle, jnp.where(lane == 2, low, 0.0))
    )
    turned_in[...] = jnp.concatenate(
        [near_in[...].astype(F32).T, bias_columns], axis=1
    ).astype(BF16)
    turned_out[...] = near_out[...].T


def forward_kernel(
    core,
    halo_before,
    halo_after,
    masked,
    gm,
    mask,
    tiles,
    packed,
    borders,
    turned_in,
    turned_out,
    w_in,
    w_out,
    gain_columns,
    output,
    d_conv,
    d_edge,
    keep,
    send,
    sums,
    left,
    right,
    packed_border,
    conv,
    conv_edge,
    total_in,
    total_out,
    total_gain,
    rows_out,
    sent,
    shards,
):
    lat, channels, lon = gm.shape
    hidden = w_in.shape[1]
    groups = channels // GROUP
    before, after = halo_before[...].astype(F32), halo_after[...].astype(F32)
    place_borders = pack_borders(before, after, borders, left, right, packed_border)

    def band(g):
        place_borders(g)
        border = packed_border[g]
        x = jnp.concatenate([border[:16], packed[g, 16 : lon - 16], border[16:]], axis=0)
        y = dot(x, tiles[g])
        conv[g] = y[:lon].T
        conv_edge[g] = y[lon : lon + EDGE]

    unrolled(groups, band)

    total_in[...] = jnp.zeros_like(total_in)
    total_out[...] = jnp.zeros_like(total_out)
    total_gain[...] = jnp.zeros_like(total_gain)

    gain_tile = gain_columns[...]

    def normalise(y, g, inner):
        cols = y.shape[1]
        gains = jnp.concatenate([gain_tile] * (cols // 128), axis=1)
        y = y - jnp.sum(y, axis=0, keepdims=True) * (1.0 / channels)
        var = jnp.sum(y * y, axis=0, keepdims=True) * (1.0 / channels)
        sigma = lax.rsqrt(var + 1e-6)
        nhat = y * sigma
        normed = (nhat * gains).astype(BF16)
        normed = jnp.concatenate([normed, jnp.ones((64, cols), BF16)], axis=0)
        state = dict(inner=inner, gains=gains, sigma=sigma, nhat=nhat, normed=normed, g=g)
        if inner:
            state.update(upright=normed.T, g_upright=g.T)
        return state

    def head(state, h):
        at = slice(h, h + 256)
        return dot(turned_in[at, :], state["normed"]), dot(turned_out[at, :], state["g"])

    def tail(state, h, z, d_act):
        at = slice(h, h + 256)
        cumulative, density = gelu_parts(z)
        d_pre = (d_act * (cumulative + z * density)).astype(BF16)
        part = dot(w_in[:, at], d_pre)
        state["d_normed"] = part if h == 0 else state["d_normed"] + part
        if state["inner"]:
            act = (z * cumulative).astype(BF16)
            part = dot(w_out[:, at], act)
            state["branch"] = part if h == 0 else state["branch"] + part
            total_in[at, :] += dot(d_pre, state["upright"])
            total_out[at, :] += dot(act, state["g_upright"])

    def finish(state):
        nhat, gains = state["nhat"], state["gains"]
        prod = state["d_normed"] * nhat
        if state["inner"]:
            part = prod[:, :128]
            for c in range(128, prod.shape[1], 128):
                part = part + prod[:, c : c + 128]
            total_gain[...] += part
        d_hat = state["d_normed"] * gains
        mean = jnp.sum(d_hat, axis=0, keepdims=True) * (1.0 / channels)
        corr = jnp.sum(prod * gains, axis=0, keepdims=True) * (1.0 / channels)
        return (state["sigma"] * (d_hat - mean - nhat * corr)).astype(BF16)

    count = 4
    blocks = lat // count
    copies = []

    def start(r):
        rows = range(count * r, count * (r + 1))
        y = []
        for i in rows:
            at = slice(i * GROUP, (i + 1) * GROUP)
            y.append(jnp.concatenate([conv[g, at, :] for g in range(groups)], axis=0))
        return normalise(
            jnp.concatenate(y, axis=1), jnp.concatenate([gm[i] for i in rows], axis=1), True
        )

    def start_edges():
        lane = iota((1, 128), 1)
        y = []
        for i in range(lat):
            half, k = (i * GROUP) // 128 * 128, i % 8
            line = []
            for tile in range(0, channels, 128):
                x = jnp.zeros((EDGE, 128), F32)
                for g in range(tile // GROUP, min(tile + 128, channels) // GROUP):
                    piece = conv_edge[g, :, half : half + 128]
                    piece = pltpu.roll(piece, (g - k) % 8 * GROUP, axis=1)
                    x = jnp.where((lane >> 4) == g % 8, piece, x)
                line.append(x)
            y.append(jnp.concatenate(line, axis=1))
        y = jnp.concatenate(y, axis=0).T[:channels]
        at = 2 * groups * EDGE
        g = jnp.where((lane & (EDGE - 1)) < EDGE // 2, after[at:], before[at:]).astype(BF16)
        return normalise(y, g, False)

    def end(r, state):
        d = finish(state)
        if r == blocks:
            d_edge[...] = d
            return
        for k in range(count):
            i = count * r + k
            at = slice(k * lon, (k + 1) * lon)
            x = masked[i].astype(F32) + state["branch"][:, at]
            rows_out[i] = (x * mask[i : i + 1]).astype(BF16)
            d_conv[i] = d[:, at]
        at = slice(count * r, count * (r + 1))
        copies.append(pltpu.make_async_copy(rows_out.at[at], output.at[at], sent.at[r]))
        copies[-1].start()

    steps = [(r, h) for r in range(blocks + 1) for h in range(0, hidden, 256)]
    states = {0: start(0)}
    coming = head(states[0], 0)
    for n, (r, h) in enumerate(steps):
        here = coming
        if h == 0 and r < blocks:
            states[r + 1] = start(r + 1) if r + 1 < blocks else start_edges()
        if n + 1 < len(steps):
            coming = head(states[steps[n + 1][0]], steps[n + 1][1])
        tail(states[r], h, *here)
        if h + 256 == hidden:
            end(r, states.pop(r))

    first = core[0] == 0
    rows = channels // shards
    sum_in = total_in[...].T
    parts_in, parts_out = [], []
    for n in range(shards):
        mine = sum_in[n * rows : (n + 1) * rows]
        parts_in += [mine[:, c : c + 128] for c in range(0, hidden, 128)]
    rows = hidden // shards
    for n in range(shards):
        mine = total_out[n * rows : (n + 1) * rows]
        parts_out.append(mine[:, :128])
        parts_out.append(
            jnp.concatenate([mine[: rows // 2, 128:], mine[rows // 2 :, 128:]], axis=1)
        )
    parts_in, parts_out = jnp.concatenate(parts_in, axis=0), jnp.concatenate(parts_out, axis=0)
    keep[...] = jnp.where(first, parts_in, parts_out).astype(BF16)
    send[...] = jnp.where(first, parts_out, parts_in).astype(BF16)
    sums[:, :hidden] = sum_in[channels : channels + 8]
    sums[:, hidden:] = jnp.broadcast_to(
        jnp.sum(total_gain[...].T, axis=0, keepdims=True), (8, channels)
    )
    for copy in copies:
        copy.wait()


def laid_cells(d_conv, d_edge, cells):
    lat, channels, lon = d_conv.shape
    rows = [d_conv[i] for i in range(lat)]
    near = iota((EDGE, 1), 0) < EDGE // 2
    lane = iota((1, 128), 1) >> 4
    blank = jnp.zeros((EDGE, 128), F32)
    edges = d_edge[...].astype(F32).T

    def place(g):
        x = group_of(rows, g).astype(F32).T
        tile = (g * GROUP) // 128 * 128
        for half in range(2):
            edge = blank
            for k in range(8):
                i = 8 * half + k
                piece = edges[i * EDGE : (i + 1) * EDGE, tile : min(tile + 128, channels)]
                if piece.shape[1] < 128:
                    piece = jnp.concatenate([piece, piece], axis=1)
                shift = (k * GROUP - (g * GROUP - tile)) % 128
                edge = jnp.where(lane == k, pltpu.roll(piece, shift, axis=1), edge)
            cells[2 * g + half] = jnp.concatenate(
                [
                    blank,
                    jnp.where(near, 0.0, edge),
                    x[:, half * 128 : (half + 1) * 128],
                    jnp.where(near, edge, 0.0),
                    blank,
                ],
                axis=0,
            )

    return place


def taps_kernel(core, masked, d_conv, d_edge, sums, own, others, keep, send, cells, packed, small):
    lat, channels, lon = masked.shape
    groups = channels // GROUP
    place_cells = laid_cells(d_conv, d_edge, cells)
    rows = [masked[i] for i in range(lat)]
    bands = [band_mask(i) for i in range(lat)]
    sub, lane = iota((8, 1), 0), iota((1, 128), 1) >> 4
    small[...] = jnp.zeros_like(small)

    for g in range(groups):
        place_cells(g)
        pack_group(cells, packed, lon, g)
        products = dot(group_of(rows, g), packed[g])
        taps = jnp.zeros((8, 128), F32)
        for b in range(7):
            parts = [None] * 8
            for i in range(lat):
                at = slice(i * GROUP, (i + 1) * GROUP)
                part = jnp.zeros((GROUP, 128), F32)
                if i < 11:
                    part = jnp.where(bands[i][:, :128], products[at, b * 256 : b * 256 + 128], part)
                if i > 4:
                    part = jnp.where(bands[i][:, 128:], products[at, b * 256 + 128 : b * 256 + 256], part)
                part = part[:8] + part[8:]
                parts[i % 8] = part if parts[i % 8] is None else parts[i % 8] + part
            total = None
            for i in range(8):
                part = pltpu.roll(parts[i], (3 - i) % 8 * GROUP, axis=1)
                total = part if total is None else total + part
            total = jnp.sum(total, axis=0, keepdims=True)
            taps = jnp.where(sub == 6 - b, total, taps)
        place = g * GROUP // 128
        for a in range(7):
            moved = pltpu.roll(taps, (g + a - 6) % 8 * GROUP, axis=1)
            small[a, place] = jnp.where(lane == g % 8, moved, small[a, place])

    line = sums[0:1]
    hidden = line.shape[1] - channels
    pieces = [line[:, c : c + 128] for c in range(0, hidden, 128)]
    pieces.append(line[:, hidden : hidden + 128])
    pieces.append(
        jnp.concatenate([line[:, hidden + 128 :], jnp.zeros((1, 256 - channels), F32)], axis=1)
    )
    for k, piece in enumerate(pieces):
        small[k // 2, k % 2, 7:8] = piece
    flat = small[...].reshape(2 * SMALL, 128)
    first = core[0] == 0
    rows = own.shape[0]
    keep[:rows] = own[...]
    keep[rows:] = jnp.where(first, flat[:SMALL], flat[SMALL:]).astype(BF16)
    send[:rows] = others[...]
    send[rows:] = jnp.where(first, flat[SMALL:], flat[:SMALL]).astype(BF16)


def spread_kernel(gm, mask, lines, d_conv, d_edge, grad_fields, rolled, tiles, cells, packed, spread):
    lat, channels, lon = gm.shape
    groups = channels // GROUP
    build_tiles(lines, rolled, tiles, True)
    place_cells = laid_cells(d_conv, d_edge, cells)

    def band(g):
        place_cells(g)
        pack_group(cells, packed, lon, g)
        spread[g] = dot(packed[g], tiles[g]).T

    unrolled(groups, band)
    for i in range(lat):
        x = jnp.concatenate(
            [spread[g, i * GROUP : (i + 1) * GROUP, :] for g in range(groups)], axis=0
        )
        x = gm[i].astype(F32) + x * mask[i : i + 1]
        grad_fields[i] = x.astype(BF16)


def final_kernel(core, mine, other, grad_in, grad_out, grad_kernel, grad_gain, grad_bias, scale):
    first = core[0] == 0
    mine, other = mine[...].astype(F32) * scale, other[...].astype(F32) * scale
    sum_in, sum_out = jnp.where(first, mine, other), jnp.where(first, other, mine)
    at = mine.shape[0] - SMALL
    small = jnp.concatenate([sum_in[at:], sum_out[at:]], axis=0)
    sum_in, sum_out = sum_in[:at], sum_out[:at]
    rows, hidden = grad_in.shape
    for k in range(hidden // 128):
        grad_in[:, k * 128 : (k + 1) * 128] = sum_in[k * rows : (k + 1) * rows]
    rows, channels = grad_out.shape
    grad_out[:, :128] = sum_out[:rows]
    rest = sum_out[rows:]
    grad_out[:, 128:] = jnp.concatenate([rest[:, :64], rest[:, 64:]], axis=0)
    for a in range(7):
        grad_kernel[a, :, :128] = small[16 * a : 16 * a + 7]
        grad_kernel[a, :, 128:] = small[16 * a + 8 : 16 * a + 15, : channels - 128]
    lines = [small[8 * k + 7 : 8 * k + 8] for k in range(hidden // 128 + 2)]
    grad_bias[...] = jnp.concatenate(lines[:-2], axis=1).reshape(hidden)
    grad_gain[...] = jnp.concatenate([lines[-2], lines[-1][:, : channels - 128]], axis=1).reshape(
        channels
    )


def swapped(x, axis, bit):
    peers = lax.axis_size(axis)
    return lax.ppermute(x, axis, [(i, i ^ bit) for i in range(peers)])


def bits_of(count):
    return [1 << k for k in range(count.bit_length() - 1)]


def pick(x, axis, at):
    return lax.dynamic_index_in_dim(x, at, axis, keepdims=False)


def both(x, y):
    return (x.astype(F32) + y.astype(F32)).astype(BF16)


def halved(mine, bit):
    have = (lax.axis_index("dp") // bit) & 1
    split = mine.reshape(mine.shape[0] // 2, 2, -1, 128)
    kept, sent = pick(split, 1, have), pick(split, 1, 1 - have)
    return kept, sent.reshape(-1, 128)


VMEM, SMEM, FAR = pltpu.VMEM, pltpu.SMEM, pltpu.HBM


def call(body, name, outs, scratch, megabytes, spaces, out_spaces):
    def held(space, shape, dtype):
        return VMEM(shape, dtype) if space is VMEM else jax.ShapeDtypeStruct(shape, dtype)

    def spec(space):
        return pl.BlockSpec(memory_space={SMEM: SMEM, FAR: pl.ANY}.get(space, VMEM))

    kernel = pl.pallas_call(
        body,
        out_shape=[held(space, *out) for space, out in zip(out_spaces, outs, strict=True)],
        in_specs=[spec(space) for space in spaces],
        out_specs=[spec(space) for space in out_spaces],
        scratch_shapes=[x if not isinstance(x, tuple) else VMEM(*x) for x in scratch],
        compiler_params=pltpu.CompilerParams(vmem_limit_bytes=megabytes * 2**20),
        name=name,
    )

    def run(*args):
        return kernel(
            *[
                pltpu.with_memory_space_constraint(x, space) if space in (FAR, VMEM) else x
                for x, space in zip(args, spaces, strict=True)
            ]
        )

    return run


def per_device(fields, cotangent, land_sea, kernel, ln_gain, weight_in, bias_in, weight_out):
    samples, lat, lon, channels = fields.shape
    hidden = weight_in.shape[1]
    shards, tiles = lax.axis_size("dp"), lax.axis_size("lon")
    groups = channels // GROUP
    rows = channels * hidden // 128
    core = (lax.axis_index("lon") & 1).reshape(1)
    fields = fields[0].transpose(0, 2, 1)
    cotangent = cotangent[0].transpose(0, 2, 1)
    w_out = weight_out.T

    field = ((lat, channels, lon), BF16)
    halo = ((2 * channels, 128), BF16)
    edge = ((channels, 128), BF16)
    rolled = ((16, 8 * groups, 256), F32)
    tile = ((groups, 7 * 256, 256), BF16)
    cells = ((2 * groups, lon + 4 * EDGE, 128), F32)
    packed = ((groups, lon, 7 * 256), BF16)
    border = ((2 * groups, 2 * EDGE + BORDER, 128), F32)
    held = ((groups, 256, lon), F32)

    first, last, masked, gm, mask = call(
        edge_kernel,
        "edges",
        [halo, halo, field, field, ((lat, lon), F32)],
        [field, field, ((lat, lon), jnp.int32), pltpu.SemaphoreType.DMA((9,))],
        8,
        [FAR] * 3,
        [VMEM] * 5,
    )(fields, cotangent, land_sea)
    up = [(i, (i + 1) % tiles) for i in range(tiles)]
    before = lax.ppermute(last, "lon", up)
    after = lax.ppermute(first, "lon", [(j, i) for i, j in up])

    ready = call(
        prepare_kernel,
        "prepare",
        [
            tile,
            packed,
            ((2 * groups, 2 * BORDER, 128), F32),
            ((hidden, 256), BF16),
            ((hidden, channels), BF16),
            ((channels, hidden), BF16),
            ((channels, hidden), BF16),
            ((channels, 128), F32),
            ((8 * groups, 256), F32),
        ],
        [
            rolled,
            cells,
            ((7, 7, channels), F32),
            ((channels,), F32),
            ((hidden,), F32),
            pltpu.SemaphoreType.DMA((5,)),
        ],
        8,
        [VMEM] + [FAR] * 5,
        [VMEM] * 9,
    )(masked, kernel, ln_gain, weight_in, bias_in, w_out)
    lines = ready[-1]

    lines = ready[-1]
    output, d_conv, d_edge, keep, send, sums = call(
        functools.partial(forward_kernel, shards=shards),
        "forward",
        [
            field,
            field,
            edge,
            ((rows, 128), BF16),
            ((rows, 128), BF16),
            ((8, hidden + channels), F32),
        ],
        [
            border,
            border,
            ((groups, 48, 7 * 256), BF16),
            held,
            ((groups, EDGE, 256), F32),
            ((hidden, 256), F32),
            ((hidden, channels), F32),
            ((channels, 128), F32),
            field,
            pltpu.SemaphoreType.DMA((lat // 4,)),
        ],
        14,
        [SMEM] + [VMEM] * 13,
        [FAR] + [VMEM] * 5,
    )(core, before, after, masked, gm, mask, *ready[:-1])

    keep, send = call(
        taps_kernel,
        "taps",
        [((rows + SMALL, 128), BF16)] * 2,
        [cells, packed, ((8, 2, 8, 128), F32)],
        10,
        [SMEM] + [VMEM] * 6,
        [VMEM] * 2,
    )(core, masked, d_conv, d_edge, sums, keep, send)
    mine = both(keep, swapped(send, "lon", 1))
    mine, small = mine[:rows].reshape(shards, -1, 128), mine[rows:]

    def spread(d_conv):
        return call(
            spread_kernel,
            "spread",
            [field],
            [rolled, tile, cells, packed, held],
            24,
            [VMEM] * 5,
            [None],
        )(gm, mask, lines, d_conv, d_edge)

    beside = [(spread, d_conv)]
    made = []
    for bit in bits_of(shards):
        kept, sent = halved(mine, bit)
        count = sent.shape[0]
        sent = jnp.concatenate([sent, small], axis=0)
        if beside:
            work, needs = beside.pop(0)
            sent, needs = lax.optimization_barrier((sent, needs))
            arrived = swapped(sent, "dp", bit)
            (result,) = work(needs)
            arrived, result = lax.optimization_barrier((arrived, result))
            made.append(result)
        else:
            arrived = swapped(sent, "dp", bit)
        mine, small = both(kept, arrived[:count].reshape(kept.shape)), both(small, arrived[count:])
    (grad_fields,) = made
    mine = jnp.concatenate([mine.reshape(-1, 128), small], axis=0)
    for bit in bits_of(tiles)[1:]:
        mine = both(mine, swapped(mine, "lon", bit))
    other = swapped(mine, "lon", 1)

    scale = 1.0 / math.sqrt(samples * lat * lon * shards * tiles)
    grads = call(
        functools.partial(final_kernel, scale=scale),
        "final",
        [
            ((channels // shards, hidden), F32),
            ((hidden // shards, channels), F32),
            ((7, 7, channels), F32),
            ((channels,), F32),
            ((hidden,), F32),
        ],
        [],
        8,
        [SMEM] + [VMEM] * 2,
        [None] * 5,
    )(core, mine, other)
    return (output.transpose(0, 2, 1)[None], grad_fields.transpose(0, 2, 1)[None], *grads)


def solution(mesh):
    placed = (
        P("dp", None, "lon", None),
        P("dp", None, "lon", None),
        P(None, "lon"),
        P(),
        P(),
        P(),
        P(),
        P(),
    )
    return jax.shard_map(
        per_device,
        mesh=mesh,
        in_specs=placed,
        out_specs=(
            P("dp", None, "lon", None),
            P("dp", None, "lon", None),
            P("dp", None),
            P("dp", None),
            P(),
            P(),
            P(),
        ),
        check_vma=False,
    )
```

```python
import functools
import math

import jax
import jax.numpy as jnp
from jax import lax
from jax.experimental import pallas as pl
from jax.experimental.pallas import tpu as pltpu
from jax.sharding import PartitionSpec as P

F32 = jnp.float32
BF16 = jnp.bfloat16
EDGE = 8
GROUP = 16


def dot(lhs, rhs):
    return jnp.dot(lhs, rhs, preferred_element_type=F32)


def dot_t(lhs, rhs):
    return lax.dot_general(lhs, rhs, (((1,), (1,)), ((), ())), preferred_element_type=F32)


def iota(shape, axis):
    return lax.broadcasted_iota(jnp.int32, shape, axis)


def identity(size):
    return jnp.where(iota((size, size), 0) == iota((size, size), 1), 1.0, 0.0).astype(BF16)


def masked_row(array, mask, i):
    return (array[i].astype(F32) * mask[i : i + 1]).astype(BF16)


def group_of(rows, g):
    return jnp.concatenate([row[GROUP * g : GROUP * (g + 1)] for row in rows], axis=0)


def band_mask(i):
    shape = (GROUP, 256)
    lane = iota(shape, 1)
    same = (lane & (GROUP - 1)) == iota(shape, 0)
    return same & (jnp.abs((lane >> 4) - i) <= 3)


def unrolled(count, body):
    for k in range(count):
        body(k)


def lay_lines(kernel, lines):
    taps, cols, channels = kernel.shape
    lane = iota((1, 128), 1) >> 4
    zero = jnp.zeros((1, channels), F32)
    rows = [jnp.concatenate([kernel[a], zero], axis=0) for a in range(taps)]
    for g in range(channels // GROUP):
        tile = g * GROUP // 128 * 128
        halves = [jnp.zeros((8, 128), F32)] * 2
        for a in range(taps):
            piece = rows[a][:, tile : min(tile + 128, channels)]
            if piece.shape[1] < 128:
                piece = jnp.concatenate([piece, piece], axis=1)
            for half, slot in ((0, taps - 1 - a), (1, a)):
                moved = pltpu.roll(piece, (slot - g) % 8 * GROUP, axis=1)
                halves[half] = jnp.where(lane == slot, moved, halves[half])
        lines[8 * g : 8 * g + 8] = jnp.concatenate(halves, axis=1)


def build_tiles(lines, rolled, tiles, flip):
    here = iota((1, 256), 1) < 128
    own = jnp.where(here, pltpu.roll(lines[...], 128, axis=1) if flip else lines[...], 0.0)
    for i in range(16):
        rolled[i] = pltpu.roll(own, ((i - 3) * GROUP) % 256, axis=1)
    masks = [band_mask(i) for i in range(16)]

    def group(g):
        for b in range(7):
            for i in range(16):
                k = 8 * g + (6 - b if flip else b)
                line = rolled[i, k : k + 1, :]
                at = b * 256 + i * GROUP
                tiles[g, at : at + GROUP, :] = jnp.where(masks[i], line, 0.0).astype(BF16)

    unrolled(tiles.shape[0], group)


def pack_group(cells, packed, lon, g):
    for half in range(2):
        for b in range(7):
            x = cells[2 * g + half, 2 * EDGE + b - 3 : 2 * EDGE + b - 3 + lon, :]
            at = b * 256 + half * 128
            packed[g, :, at : at + 128] = x.astype(BF16)


BORDER = 24
SMALL = 96


def pack_borders(before, after, borders, left, right, packed):
    groups = packed.shape[0]
    near = iota((EDGE, 1), 0) < EDGE // 2
    blank = jnp.zeros((EDGE, 128), F32)

    def place(g):
        for half in range(2):
            k = 2 * g + half
            at = half * groups * EDGE + g * EDGE
            halo = slice(at, at + EDGE)
            left[k] = jnp.concatenate([blank, before[halo], borders[k, :BORDER]], axis=0)
            right[k] = jnp.concatenate([borders[k, BORDER:], after[halo], blank], axis=0)
            for b in range(7):
                s = b - 3
                inner = left[k, 2 * EDGE + s : 2 * EDGE + s + 16, :]
                outer = right[k, BORDER - 16 + s : BORDER + s, :]
                beyond = jnp.where(
                    near,
                    right[k, BORDER + s : BORDER + s + EDGE, :],
                    left[k, EDGE + s : 2 * EDGE + s, :],
                )
                x = jnp.concatenate([inner, outer, beyond, beyond], axis=0)
                at = b * 256 + half * 128
                packed[g, :, at : at + 128] = x.astype(BF16)

    return place


def gelu_parts(z):
    cumulative = 0.5 + 0.5 * lax.erf(z * math.sqrt(0.5))
    density = jnp.exp2(z * z * (-0.5 * math.log2(math.e))) * (1.0 / math.sqrt(2.0 * math.pi))
    return cumulative, density


def edge_kernel(
    fields, cotangent, mask, first, last, masked, gm, near_mask, held_x, held_g, held_mask, arrived
):
    lat, channels, lon = fields.shape
    groups = channels // GROUP
    count = lat // 4
    copies = [pltpu.make_async_copy(mask, held_mask, arrived.at[0])]
    for r in range(4):
        at = slice(count * r, count * (r + 1))
        for k, (far, held) in enumerate(((fields, held_x), (cotangent, held_g))):
            copies.append(
                pltpu.make_async_copy(far.at[at], held.at[at], arrived.at[1 + 2 * r + k])
            )
    for copy in copies:
        copy.start()
    row, lane = iota((2 * EDGE, lon), 0), iota((2 * EDGE, lon), 1)
    ends = jnp.where(lane == jnp.where(row < EDGE, row, row + lon - 2 * EDGE), 1.0, 0.0)
    ends = ends.astype(BF16)
    copies[0].wait()
    near_mask[...] = held_mask[...].astype(F32)
    rows, outer = [], []
    for r in range(4):
        copies[1 + 2 * r].wait()
        copies[2 + 2 * r].wait()
        for i in range(count * r, count * (r + 1)):
            rows.append(masked_row(held_x, near_mask, i))
            turned = masked_row(held_g, near_mask, i)
            outer.append(dot_t(ends, turned))
            masked[i] = rows[i]
            gm[i] = turned
    cells = [dot_t(ends, group_of(rows, g)) for g in range(groups)]
    for k, out in enumerate((first, last)):
        for half in range(2):
            at = slice(half * 128, (half + 1) * 128)
            x = [cell[k * EDGE : (k + 1) * EDGE, at] for cell in cells]
            count = groups * EDGE
            out[half * count : (half + 1) * count] = jnp.concatenate(x, axis=0).astype(BF16)
        g = jnp.concatenate([x[k * EDGE : (k + 1) * EDGE] for x in outer], axis=0)
        out[2 * groups * EDGE :] = g.T.astype(BF16)


def prepare_kernel(
    masked,
    kernel,
    gain,
    w_in,
    bias,
    w_out,
    tiles,
    packed,
    borders,
    turned_in,
    turned_out,
    near_in,
    near_out,
    gain_columns,
    lines,
    rolled,
    cells,
    near_kernel,
    near_gain,
    near_bias,
    arrived,
):
    lat, channels, lon = masked.shape
    hidden = w_in.shape[1]
    groups = channels // GROUP
    far = (kernel, gain, w_in, bias, w_out)
    near = (near_kernel, near_gain, near_in, near_bias, near_out)
    copies = [
        pltpu.make_async_copy(x, y, arrived.at[k])
        for k, (x, y) in enumerate(zip(far, near, strict=True))
    ]
    for copy in copies:
        copy.start()

    rows = [masked[i] for i in range(lat)]
    blank = jnp.zeros((2 * EDGE, 128), F32)
    for g in range(groups):
        x = group_of(rows, g).astype(F32).T
        for half in range(2):
            k = 2 * g + half
            part = x[:, half * 128 : (half + 1) * 128]
            cells[k] = jnp.concatenate([blank, part, blank], axis=0)
            borders[k] = jnp.concatenate([part[:BORDER], part[lon - BORDER :]], axis=0)
        pack_group(cells, packed, lon, g)

    for copy in copies:
        copy.wait()
    lay_lines(near_kernel, lines)
    build_tiles(lines, rolled, tiles, False)
    gain_row = near_gain[...].reshape(1, channels)
    gain_columns[...] = jnp.broadcast_to(gain_row, (128, channels)).T
    bias_row = near_bias[...].reshape(1, hidden)
    bias_columns = jnp.broadcast_to(bias_row, (64, hidden)).T
    lane = iota((hidden, 64), 1)
    high = bias_columns.astype(BF16).astype(F32)
    middle = (bias_columns - high).astype(BF16).astype(F32)
    low = bias_columns - high - middle
    bias_columns = jnp.where(
        lane == 0, high, jnp.where(lane == 1, middle, jnp.where(lane == 2, low, 0.0))
    )
    turned_in[...] = jnp.concatenate(
        [near_in[...].astype(F32).T, bias_columns], axis=1
    ).astype(BF16)
    turned_out[...] = near_out[...].T


def forward_kernel(
    core,
    halo_before,
    halo_after,
    masked,
    gm,
    mask,
    tiles,
    packed,
    borders,
    turned_in,
    turned_out,
    w_in,
    w_out,
    gain_columns,
    output,
    d_conv,
    d_edge,
    keep,
    send,
    sums,
    left,
    right,
    packed_border,
    conv,
    conv_edge,
    total_in,
    total_out,
    total_gain,
    rows_out,
    sent,
    shards,
):
    lat, channels, lon = gm.shape
    hidden = w_in.shape[1]
    groups = channels // GROUP
    before, after = halo_before[...].astype(F32), halo_after[...].astype(F32)
    place_borders = pack_borders(before, after, borders, left, right, packed_border)

    def band(g):
        place_borders(g)
        border = packed_border[g]
        x = jnp.concatenate([border[:16], packed[g, 16 : lon - 16], border[16:]], axis=0)
        y = dot(x, tiles[g])
        conv[g] = y[:lon].T
        conv_edge[g] = y[lon : lon + EDGE]

    unrolled(groups, band)

    total_in[...] = jnp.zeros_like(total_in)
    total_out[...] = jnp.zeros_like(total_out)
    total_gain[...] = jnp.zeros_like(total_gain)

    gain_tile = gain_columns[...]

    def normalise(y, g, inner):
        cols = y.shape[1]
        gains = jnp.concatenate([gain_tile] * (cols // 128), axis=1)
        y = y - jnp.sum(y, axis=0, keepdims=True) * (1.0 / channels)
        var = jnp.sum(y * y, axis=0, keepdims=True) * (1.0 / channels)
        sigma = lax.rsqrt(var + 1e-6)
        nhat = y * sigma
        normed = (nhat * gains).astype(BF16)
        normed = jnp.concatenate([normed, jnp.ones((64, cols), BF16)], axis=0)
        state = dict(inner=inner, gains=gains, sigma=sigma, nhat=nhat, normed=normed, g=g)
        if inner:
            state.update(upright=normed.T, g_upright=g.T)
        return state

    def head(state, h):
        at = slice(h, h + 256)
        return dot(turned_in[at, :], state["normed"]), dot(turned_out[at, :], state["g"])

    def tail(state, h, z, d_act):
        at = slice(h, h + 256)
        cumulative, density = gelu_parts(z)
        d_pre = (d_act * (cumulative + z * density)).astype(BF16)
        state.setdefault("d_pre", []).append(d_pre)
        if h + 256 == hidden:
            state["d_normed"] = dot(w_in[...], jnp.concatenate(state["d_pre"], axis=0))
        if state["inner"]:
            act = (z * cumulative).astype(BF16)
            state.setdefault("act", []).append(act)
            if h + 256 == hidden:
                state["branch"] = dot(w_out[...], jnp.concatenate(state["act"], axis=0))
            total_in[at, :] += dot(d_pre, state["upright"])
            total_out[at, :] += dot(act, state["g_upright"])

    def finish(state):
        nhat, gains = state["nhat"], state["gains"]
        prod = state["d_normed"] * nhat
        if state["inner"]:
            part = prod[:, :128]
            for c in range(128, prod.shape[1], 128):
                part = part + prod[:, c : c + 128]
            total_gain[...] += part
        d_hat = state["d_normed"] * gains
        mean = jnp.sum(d_hat, axis=0, keepdims=True) * (1.0 / channels)
        corr = jnp.sum(prod * gains, axis=0, keepdims=True) * (1.0 / channels)
        return (state["sigma"] * (d_hat - mean - nhat * corr)).astype(BF16)

    count = 4
    blocks = lat // count
    copies = []

    def start(r):
        rows = range(count * r, count * (r + 1))
        y = []
        for i in rows:
            at = slice(i * GROUP, (i + 1) * GROUP)
            y.append(jnp.concatenate([conv[g, at, :] for g in range(groups)], axis=0))
        return normalise(
            jnp.concatenate(y, axis=1), jnp.concatenate([gm[i] for i in rows], axis=1), True
        )

    def start_edges():
        lane = iota((1, 128), 1)
        y = []
        for i in range(lat):
            half, k = (i * GROUP) // 128 * 128, i % 8
            line = []
            for tile in range(0, channels, 128):
                x = jnp.zeros((EDGE, 128), F32)
                for g in range(tile // GROUP, min(tile + 128, channels) // GROUP):
                    piece = conv_edge[g, :, half : half + 128]
                    piece = pltpu.roll(piece, (g - k) % 8 * GROUP, axis=1)
                    x = jnp.where((lane >> 4) == g % 8, piece, x)
                line.append(x)
            y.append(jnp.concatenate(line, axis=1))
        y = jnp.concatenate(y, axis=0).T[:channels]
        at = 2 * groups * EDGE
        g = jnp.where((lane & (EDGE - 1)) < EDGE // 2, after[at:], before[at:]).astype(BF16)
        return normalise(y, g, False)

    def end(r, state):
        d = finish(state)
        if r == blocks:
            d_edge[...] = d
            return
        for k in range(count):
            i = count * r + k
            at = slice(k * lon, (k + 1) * lon)
            x = masked[i].astype(F32) + state["branch"][:, at]
            rows_out[i] = (x * mask[i : i + 1]).astype(BF16)
            d_conv[i] = d[:, at]
        at = slice(count * r, count * (r + 1))
        copies.append(pltpu.make_async_copy(rows_out.at[at], output.at[at], sent.at[r]))
        copies[-1].start()

    steps = [(r, h) for r in range(blocks + 1) for h in range(0, hidden, 256)]
    states = {0: start(0)}
    coming = head(states[0], 0)
    for n, (r, h) in enumerate(steps):
        here = coming
        if h == 0 and r < blocks:
            states[r + 1] = start(r + 1) if r + 1 < blocks else start_edges()
        if n + 1 < len(steps):
            coming = head(states[steps[n + 1][0]], steps[n + 1][1])
        tail(states[r], h, *here)
        if h + 256 == hidden:
            end(r, states.pop(r))

    first = core[0] == 0
    rows = channels // shards
    sum_in = total_in[...].T
    parts_in, parts_out = [], []
    for n in range(shards):
        mine = sum_in[n * rows : (n + 1) * rows]
        parts_in += [mine[:, c : c + 128] for c in range(0, hidden, 128)]
    rows = hidden // shards
    for n in range(shards):
        mine = total_out[n * rows : (n + 1) * rows]
        parts_out.append(mine[:, :128])
        parts_out.append(
            jnp.concatenate([mine[: rows // 2, 128:], mine[rows // 2 :, 128:]], axis=1)
        )
    parts_in, parts_out = jnp.concatenate(parts_in, axis=0), jnp.concatenate(parts_out, axis=0)
    keep[...] = jnp.where(first, parts_in, parts_out).astype(BF16)
    send[...] = jnp.where(first, parts_out, parts_in).astype(BF16)
    sums[:, :hidden] = sum_in[channels : channels + 8]
    sums[:, hidden:] = jnp.broadcast_to(
        jnp.sum(total_gain[...].T, axis=0, keepdims=True), (8, channels)
    )
    for copy in copies:
        copy.wait()


def laid_cells(d_conv, d_edge, cells):
    lat, channels, lon = d_conv.shape
    rows = [d_conv[i] for i in range(lat)]
    near = iota((EDGE, 1), 0) < EDGE // 2
    lane = iota((1, 128), 1) >> 4
    blank = jnp.zeros((EDGE, 128), F32)
    edges = d_edge[...].astype(F32).T

    def place(g):
        x = group_of(rows, g).astype(F32).T
        tile = (g * GROUP) // 128 * 128
        for half in range(2):
            edge = blank
            for k in range(8):
                i = 8 * half + k
                piece = edges[i * EDGE : (i + 1) * EDGE, tile : min(tile + 128, channels)]
                if piece.shape[1] < 128:
                    piece = jnp.concatenate([piece, piece], axis=1)
                shift = (k * GROUP - (g * GROUP - tile)) % 128
                edge = jnp.where(lane == k, pltpu.roll(piece, shift, axis=1), edge)
            cells[2 * g + half] = jnp.concatenate(
                [
                    blank,
                    jnp.where(near, 0.0, edge),
                    x[:, half * 128 : (half + 1) * 128],
                    jnp.where(near, edge, 0.0),
                    blank,
                ],
                axis=0,
            )

    return place


def taps_kernel(masked, d_conv, d_edge, sums, out, cells, packed, small):
    lat, channels, lon = masked.shape
    groups = channels // GROUP
    place_cells = laid_cells(d_conv, d_edge, cells)
    rows = [masked[i] for i in range(lat)]
    bands = [band_mask(i) for i in range(lat)]
    sub, lane = iota((8, 1), 0), iota((1, 128), 1) >> 4
    small[...] = jnp.zeros_like(small)

    for g in range(groups):
        place_cells(g)
        pack_group(cells, packed, lon, g)
        products = dot(group_of(rows, g), packed[g])
        taps = jnp.zeros((8, 128), F32)
        for b in range(7):
            parts = [None] * 8
            for i in range(lat):
                at = slice(i * GROUP, (i + 1) * GROUP)
                part = jnp.zeros((GROUP, 128), F32)
                if i < 11:
                    part = jnp.where(bands[i][:, :128], products[at, b * 256 : b * 256 + 128], part)
                if i > 4:
                    part = jnp.where(bands[i][:, 128:], products[at, b * 256 + 128 : b * 256 + 256], part)
                part = part[:8] + part[8:]
                parts[i % 8] = part if parts[i % 8] is None else parts[i % 8] + part
            total = None
            for i in range(8):
                part = pltpu.roll(parts[i], (3 - i) % 8 * GROUP, axis=1)
                total = part if total is None else total + part
            total = jnp.sum(total, axis=0, keepdims=True)
            taps = jnp.where(sub == 6 - b, total, taps)
        for a in range(7):
            place, slot = (a, g) if g < 8 else (7 + a // 2, g % 4 + 4 * (a % 2))
            moved = pltpu.roll(taps, (slot + a - 6) % 8 * GROUP, axis=1)
            small[place] = jnp.where(lane == slot, moved, small[place])

    line = sums[0:1]
    hidden = line.shape[1] - channels
    pieces = [line[:, c : c + 128] for c in range(0, hidden, 128)]
    pieces.append(line[:, hidden : hidden + 128])
    pieces.append(
        jnp.concatenate([line[:, hidden + 128 :], jnp.zeros((1, 256 - channels), F32)], axis=1)
    )
    for k, piece in enumerate(pieces):
        small[k, 7:8] = piece
    out[...] = small[...].reshape(SMALL, 128).astype(BF16)


def fold_kernel(have, keep, arrived, small, kept, sent, shards):
    rows = kept.shape[0]
    total = keep[...].astype(F32) + arrived[...].astype(F32)
    total = total.reshape(-1, 2, total.shape[0] // shards, 128)
    even, odd = total[:, 0].reshape(rows, 128), total[:, 1].reshape(rows, 128)
    first = have[0] == 0
    kept[...] = jnp.where(first, even, odd).astype(BF16)
    sent[:rows] = jnp.where(first, odd, even).astype(BF16)
    sent[rows:] = small[...]


def spread_kernel(gm, mask, lines, d_conv, d_edge, grad_fields, rolled, tiles, cells, packed, spread):
    lat, channels, lon = gm.shape
    groups = channels // GROUP
    build_tiles(lines, rolled, tiles, True)
    place_cells = laid_cells(d_conv, d_edge, cells)

    def band(g):
        place_cells(g)
        pack_group(cells, packed, lon, g)
        spread[g] = dot(packed[g], tiles[g]).T

    unrolled(groups, band)
    for i in range(lat):
        x = jnp.concatenate(
            [spread[g, i * GROUP : (i + 1) * GROUP, :] for g in range(groups)], axis=0
        )
        x = gm[i].astype(F32) + x * mask[i : i + 1]
        grad_fields[i] = x.astype(BF16)


def final_kernel(core, mine, other, grad_in, grad_out, grad_kernel, grad_gain, grad_bias, scale):
    first = core[0] == 0
    mine, other = mine[...].astype(F32) * scale, other[...].astype(F32) * scale
    sum_in, sum_out = jnp.where(first, mine, other), jnp.where(first, other, mine)
    at = mine.shape[0] - SMALL
    small = mine[at:] + other[at:]
    sum_in, sum_out = sum_in[:at], sum_out[:at]
    rows, hidden = grad_in.shape
    for k in range(hidden // 128):
        grad_in[:, k * 128 : (k + 1) * 128] = sum_in[k * rows : (k + 1) * rows]
    rows, channels = grad_out.shape
    grad_out[:, :128] = sum_out[:rows]
    rest = sum_out[rows:]
    grad_out[:, 128:] = jnp.concatenate([rest[:, :64], rest[:, 64:]], axis=0)
    for a in range(7):
        at = 8 * (7 + a // 2)
        half = slice(64 * (a % 2), 64 * (a % 2) + 64)
        grad_kernel[a, :, :128] = small[8 * a : 8 * a + 7]
        grad_kernel[a, :, 128:] = small[at : at + 7, half]
    lines = [small[8 * k + 7 : 8 * k + 8] for k in range(hidden // 128 + 2)]
    grad_bias[...] = jnp.concatenate(lines[:-2], axis=1).reshape(hidden)
    grad_gain[...] = jnp.concatenate([lines[-2], lines[-1][:, : channels - 128]], axis=1).reshape(
        channels
    )


def swapped(x, axis, bit):
    peers = lax.axis_size(axis)
    return lax.ppermute(x, axis, [(i, i ^ bit) for i in range(peers)])


def bits_of(count):
    return [1 << k for k in range(count.bit_length() - 1)]


def pick(x, axis, at):
    return lax.dynamic_index_in_dim(x, at, axis, keepdims=False)


def both(x, y):
    return (x.astype(F32) + y.astype(F32)).astype(BF16)


def halved(mine, bit):
    have = (lax.axis_index("dp") // bit) & 1
    split = mine.reshape(mine.shape[0] // 2, 2, -1, 128)
    kept, sent = pick(split, 1, have), pick(split, 1, 1 - have)
    return kept, sent.reshape(-1, 128)


VMEM, SMEM, FAR = pltpu.VMEM, pltpu.SMEM, pltpu.HBM


def call(body, name, outs, scratch, megabytes, spaces, out_spaces):
    def held(space, shape, dtype):
        return VMEM(shape, dtype) if space is VMEM else jax.ShapeDtypeStruct(shape, dtype)

    def spec(space):
        return pl.BlockSpec(memory_space={SMEM: SMEM, FAR: pl.ANY}.get(space, VMEM))

    kernel = pl.pallas_call(
        body,
        out_shape=[held(space, *out) for space, out in zip(out_spaces, outs, strict=True)],
        in_specs=[spec(space) for space in spaces],
        out_specs=[spec(space) for space in out_spaces],
        scratch_shapes=[x if not isinstance(x, tuple) else VMEM(*x) for x in scratch],
        compiler_params=pltpu.CompilerParams(vmem_limit_bytes=megabytes * 2**20),
        name=name,
    )

    def run(*args):
        return kernel(
            *[
                pltpu.with_memory_space_constraint(x, space) if space in (FAR, VMEM) else x
                for x, space in zip(args, spaces, strict=True)
            ]
        )

    return run


def per_device(fields, cotangent, land_sea, kernel, ln_gain, weight_in, bias_in, weight_out):
    samples, lat, lon, channels = fields.shape
    hidden = weight_in.shape[1]
    shards, tiles = lax.axis_size("dp"), lax.axis_size("lon")
    groups = channels // GROUP
    rows = channels * hidden // 128
    core = (lax.axis_index("lon") & 1).reshape(1)
    fields = fields[0].transpose(0, 2, 1)
    cotangent = cotangent[0].transpose(0, 2, 1)
    w_out = weight_out.T

    field = ((lat, channels, lon), BF16)
    halo = ((2 * channels, 128), BF16)
    edge = ((channels, 128), BF16)
    rolled = ((16, 8 * groups, 256), F32)
    tile = ((groups, 7 * 256, 256), BF16)
    cells = ((2 * groups, lon + 4 * EDGE, 128), F32)
    packed = ((groups, lon, 7 * 256), BF16)
    border = ((2 * groups, 2 * EDGE + BORDER, 128), F32)
    held = ((groups, 256, lon), F32)

    first, last, masked, gm, mask = call(
        edge_kernel,
        "edges",
        [halo, halo, field, field, ((lat, lon), F32)],
        [field, field, ((lat, lon), jnp.int32), pltpu.SemaphoreType.DMA((9,))],
        8,
        [FAR] * 3,
        [VMEM] * 5,
    )(fields, cotangent, land_sea)
    up = [(i, (i + 1) % tiles) for i in range(tiles)]
    before = lax.ppermute(last, "lon", up)
    after = lax.ppermute(first, "lon", [(j, i) for i, j in up])

    ready = call(
        prepare_kernel,
        "prepare",
        [
            tile,
            packed,
            ((2 * groups, 2 * BORDER, 128), F32),
            ((hidden, 256), BF16),
            ((hidden, channels), BF16),
            ((channels, hidden), BF16),
            ((channels, hidden), BF16),
            ((channels, 128), F32),
            ((8 * groups, 256), F32),
        ],
        [
            rolled,
            cells,
            ((7, 7, channels), F32),
            ((channels,), F32),
            ((hidden,), F32),
            pltpu.SemaphoreType.DMA((5,)),
        ],
        8,
        [VMEM] + [FAR] * 5,
        [VMEM] * 9,
    )(masked, kernel, ln_gain, weight_in, bias_in, w_out)
    lines = ready[-1]

    lines = ready[-1]
    output, d_conv, d_edge, keep, send, sums = call(
        functools.partial(forward_kernel, shards=shards),
        "forward",
        [
            field,
            field,
            edge,
            ((rows, 128), BF16),
            ((rows, 128), BF16),
            ((8, hidden + channels), F32),
        ],
        [
            border,
            border,
            ((groups, 48, 7 * 256), BF16),
            held,
            ((groups, EDGE, 256), F32),
            ((hidden, 256), F32),
            ((hidden, channels), F32),
            ((channels, 128), F32),
            field,
            pltpu.SemaphoreType.DMA((lat // 4,)),
        ],
        14,
        [SMEM] + [VMEM] * 13,
        [FAR] + [VMEM] * 5,
    )(core, before, after, masked, gm, mask, *ready[:-1])

    arrived = swapped(send, "lon", 1)
    (small,) = call(
        taps_kernel,
        "taps",
        [((SMALL, 128), BF16)],
        [cells, packed, ((12, 8, 128), F32)],
        10,
        [VMEM] * 4,
        [VMEM],
    )(masked, d_conv, d_edge, sums)
    have = (lax.axis_index("dp") & 1).reshape(1)
    kept, sent = call(
        functools.partial(fold_kernel, shards=shards),
        "fold",
        [((rows // 2, 128), BF16), ((rows // 2 + SMALL, 128), BF16)],
        [],
        6,
        [SMEM] + [VMEM] * 3,
        [VMEM] * 2,
    )(have, keep, arrived, small)

    sent, d_conv = lax.optimization_barrier((sent, d_conv))
    arrived = swapped(sent, "dp", 1)
    (grad_fields,) = call(
        spread_kernel,
        "spread",
        [field],
        [rolled, tile, cells, packed, held],
        24,
        [VMEM] * 5,
        [None],
    )(gm, mask, lines, d_conv, d_edge)
    arrived, grad_fields = lax.optimization_barrier((arrived, grad_fields))
    mine = both(kept, arrived[: rows // 2]).reshape(shards // 2, -1, 128)
    small = both(small, arrived[rows // 2 :])
    for bit in bits_of(shards)[1:]:
        kept, sent = halved(mine, bit)
        count = sent.shape[0]
        arrived = swapped(jnp.concatenate([sent, small], axis=0), "dp", bit)
        mine = both(kept, arrived[:count].reshape(kept.shape))
        small = both(small, arrived[count:])
    mine = jnp.concatenate([mine.reshape(-1, 128), small], axis=0)
    for bit in bits_of(tiles)[1:]:
        mine = both(mine, swapped(mine, "lon", bit))
    other = swapped(mine, "lon", 1)

    scale = 1.0 / math.sqrt(samples * lat * lon * shards * tiles)
    grads = call(
        functools.partial(final_kernel, scale=scale),
        "final",
        [
            ((channels // shards, hidden), F32),
            ((hidden // shards, channels), F32),
            ((7, 7, channels), F32),
            ((channels,), F32),
            ((hidden,), F32),
        ],
        [],
        8,
        [SMEM] + [VMEM] * 2,
        [None] * 5,
    )(core, mine, other)
    return (output.transpose(0, 2, 1)[None], grad_fields.transpose(0, 2, 1)[None], *grads)


def solution(mesh):
    placed = (
        P("dp", None, "lon", None),
        P("dp", None, "lon", None),
        P(None, "lon"),
        P(),
        P(),
        P(),
        P(),
        P(),
    )
    return jax.shard_map(
        per_device,
        mesh=mesh,
        in_specs=placed,
        out_specs=(
            P("dp", None, "lon", None),
            P("dp", None, "lon", None),
            P("dp", None),
            P("dp", None),
            P(),
            P(),
            P(),
        ),
        check_vma=False,
    )
```

```python
import functools
import math

import jax
import jax.numpy as jnp
from jax import lax
from jax.experimental import pallas as pl
from jax.experimental.pallas import tpu as pltpu
from jax.sharding import PartitionSpec as P

F32 = jnp.float32
BF16 = jnp.bfloat16
EDGE = 8
GROUP = 16


def dot(lhs, rhs):
    return jnp.dot(lhs, rhs, preferred_element_type=F32)


def dot_t(lhs, rhs):
    return lax.dot_general(lhs, rhs, (((1,), (1,)), ((), ())), preferred_element_type=F32)


def iota(shape, axis):
    return lax.broadcasted_iota(jnp.int32, shape, axis)


def identity(size):
    return jnp.where(iota((size, size), 0) == iota((size, size), 1), 1.0, 0.0).astype(BF16)


def masked_row(array, mask, i):
    return (array[i].astype(F32) * mask[i : i + 1]).astype(BF16)


def group_of(rows, g):
    return jnp.concatenate([row[GROUP * g : GROUP * (g + 1)] for row in rows], axis=0)


def band_mask(i):
    shape = (GROUP, 256)
    lane = iota(shape, 1)
    same = (lane & (GROUP - 1)) == iota(shape, 0)
    return same & (jnp.abs((lane >> 4) - i) <= 3)


def unrolled(count, body):
    for k in range(count):
        body(k)


def lay_lines(kernel, lines):
    taps, cols, channels = kernel.shape
    lane = iota((1, 128), 1) >> 4
    zero = jnp.zeros((1, channels), F32)
    rows = [jnp.concatenate([kernel[a], zero], axis=0) for a in range(taps)]
    for g in range(channels // GROUP):
        tile = g * GROUP // 128 * 128
        halves = [jnp.zeros((8, 128), F32)] * 2
        for a in range(taps):
            piece = rows[a][:, tile : min(tile + 128, channels)]
            if piece.shape[1] < 128:
                piece = jnp.concatenate([piece, piece], axis=1)
            for half, slot in ((0, taps - 1 - a), (1, a)):
                moved = pltpu.roll(piece, (slot - g) % 8 * GROUP, axis=1)
                halves[half] = jnp.where(lane == slot, moved, halves[half])
        lines[8 * g : 8 * g + 8] = jnp.concatenate(halves, axis=1)


def build_tiles(lines, rolled, tiles, flip):
    here = iota((1, 256), 1) < 128
    own = jnp.where(here, pltpu.roll(lines[...], 128, axis=1) if flip else lines[...], 0.0)
    for i in range(16):
        rolled[i] = pltpu.roll(own, ((i - 3) * GROUP) % 256, axis=1)
    masks = [band_mask(i) for i in range(16)]

    def group(g):
        for b in range(7):
            for i in range(16):
                k = 8 * g + (6 - b if flip else b)
                line = rolled[i, k : k + 1, :]
                at = b * 256 + i * GROUP
                tiles[g, at : at + GROUP, :] = jnp.where(masks[i], line, 0.0).astype(BF16)

    unrolled(tiles.shape[0], group)


def pack_group(cells, packed, lon, g):
    for half in range(2):
        for b in range(7):
            x = cells[2 * g + half, 2 * EDGE + b - 3 : 2 * EDGE + b - 3 + lon, :]
            at = b * 256 + half * 128
            packed[g, :, at : at + 128] = x.astype(BF16)


BORDER = 24
SMALL = 96


def pack_borders(before, after, borders, left, right, packed):
    groups = packed.shape[0]
    near = iota((EDGE, 1), 0) < EDGE // 2
    blank = jnp.zeros((EDGE, 128), F32)

    def place(g):
        for half in range(2):
            k = 2 * g + half
            at = half * groups * EDGE + g * EDGE
            halo = slice(at, at + EDGE)
            left[k] = jnp.concatenate([blank, before[halo], borders[k, :BORDER]], axis=0)
            right[k] = jnp.concatenate([borders[k, BORDER:], after[halo], blank], axis=0)
            for b in range(7):
                s = b - 3
                inner = left[k, 2 * EDGE + s : 2 * EDGE + s + 16, :]
                outer = right[k, BORDER - 16 + s : BORDER + s, :]
                beyond = jnp.where(
                    near,
                    right[k, BORDER + s : BORDER + s + EDGE, :],
                    left[k, EDGE + s : 2 * EDGE + s, :],
                )
                x = jnp.concatenate([inner, outer, beyond, beyond], axis=0)
                at = b * 256 + half * 128
                packed[g, :, at : at + 128] = x.astype(BF16)

    return place


def gelu_parts(z):
    cumulative = 0.5 + 0.5 * lax.erf(z * math.sqrt(0.5))
    density = jnp.exp2(z * z * (-0.5 * math.log2(math.e))) * (1.0 / math.sqrt(2.0 * math.pi))
    return cumulative, density


def edge_kernel(
    fields, cotangent, mask, first, last, masked, gm, near_mask, held_x, held_g, held_mask, arrived
):
    lat, channels, lon = fields.shape
    groups = channels // GROUP
    count = lat // 4
    copies = [pltpu.make_async_copy(mask, held_mask, arrived.at[0])]
    for r in range(4):
        at = slice(count * r, count * (r + 1))
        for k, (far, held) in enumerate(((fields, held_x), (cotangent, held_g))):
            copies.append(
                pltpu.make_async_copy(far.at[at], held.at[at], arrived.at[1 + 2 * r + k])
            )
    for copy in copies:
        copy.start()
    row, lane = iota((2 * EDGE, lon), 0), iota((2 * EDGE, lon), 1)
    ends = jnp.where(lane == jnp.where(row < EDGE, row, row + lon - 2 * EDGE), 1.0, 0.0)
    ends = ends.astype(BF16)
    copies[0].wait()
    near_mask[...] = held_mask[...].astype(F32)
    rows, outer = [], []
    for r in range(4):
        copies[1 + 2 * r].wait()
        copies[2 + 2 * r].wait()
        for i in range(count * r, count * (r + 1)):
            rows.append(masked_row(held_x, near_mask, i))
            turned = masked_row(held_g, near_mask, i)
            outer.append(dot_t(ends, turned))
            masked[i] = rows[i]
            gm[i] = turned
    cells = [dot_t(ends, group_of(rows, g)) for g in range(groups)]
    for k, out in enumerate((first, last)):
        for half in range(2):
            at = slice(half * 128, (half + 1) * 128)
            x = [cell[k * EDGE : (k + 1) * EDGE, at] for cell in cells]
            count = groups * EDGE
            out[half * count : (half + 1) * count] = jnp.concatenate(x, axis=0).astype(BF16)
        g = jnp.concatenate([x[k * EDGE : (k + 1) * EDGE] for x in outer], axis=0).T
        top, bottom = g[: channels // 2], g[channels // 2 :]
        near = (iota((1, 128), 1) & (EDGE - 1)) < EDGE // 2
        if k == 0:
            g = jnp.where(near, top, pltpu.roll(bottom, EDGE // 2, axis=1))
        else:
            g = jnp.where(near, pltpu.roll(bottom, 128 - EDGE // 2, axis=1), top)
        out[2 * groups * EDGE :] = g.astype(BF16)


def prepare_kernel(
    masked,
    kernel,
    gain,
    w_in,
    bias,
    w_out,
    tiles,
    packed,
    borders,
    turned_in,
    turned_out,
    near_in,
    near_out,
    gain_columns,
    lines,
    rolled,
    cells,
    near_kernel,
    near_gain,
    near_bias,
    arrived,
):
    lat, channels, lon = masked.shape
    hidden = w_in.shape[1]
    groups = channels // GROUP
    far = (kernel, gain, w_in, bias, w_out)
    near = (near_kernel, near_gain, near_in, near_bias, near_out)
    copies = [
        pltpu.make_async_copy(x, y, arrived.at[k])
        for k, (x, y) in enumerate(zip(far, near, strict=True))
    ]
    for copy in copies:
        copy.start()

    rows = [masked[i] for i in range(lat)]
    blank = jnp.zeros((2 * EDGE, 128), F32)
    for g in range(groups):
        x = group_of(rows, g).astype(F32).T
        for half in range(2):
            k = 2 * g + half
            part = x[:, half * 128 : (half + 1) * 128]
            cells[k] = jnp.concatenate([blank, part, blank], axis=0)
            borders[k] = jnp.concatenate([part[:BORDER], part[lon - BORDER :]], axis=0)
        pack_group(cells, packed, lon, g)

    for copy in copies:
        copy.wait()
    lay_lines(near_kernel, lines)
    build_tiles(lines, rolled, tiles, False)
    gain_row = near_gain[...].reshape(1, channels)
    gain_columns[...] = jnp.broadcast_to(gain_row, (128, channels)).T
    bias_row = near_bias[...].reshape(1, hidden)
    bias_columns = jnp.broadcast_to(bias_row, (64, hidden)).T
    lane = iota((hidden, 64), 1)
    high = bias_columns.astype(BF16).astype(F32)
    middle = (bias_columns - high).astype(BF16).astype(F32)
    low = bias_columns - high - middle
    bias_columns = jnp.where(
        lane == 0, high, jnp.where(lane == 1, middle, jnp.where(lane == 2, low, 0.0))
    )
    turned_in[...] = jnp.concatenate([near_in[...].T, bias_columns.astype(BF16)], axis=1)
    turned_out[...] = near_out[...].T


def forward_kernel(
    core,
    halo_before,
    halo_after,
    masked,
    gm,
    mask,
    tiles,
    packed,
    borders,
    turned_in,
    turned_out,
    w_in,
    w_out,
    gain_columns,
    output,
    d_conv,
    d_edge,
    keep,
    send,
    sums,
    left,
    right,
    packed_border,
    conv,
    conv_edge,
    total_in,
    total_out,
    total_gain,
    rows_out,
    sent,
    shards,
):
    lat, channels, lon = gm.shape
    hidden = w_in.shape[1]
    groups = channels // GROUP
    before, after = halo_before[...].astype(F32), halo_after[...].astype(F32)
    place_borders = pack_borders(before, after, borders, left, right, packed_border)

    def band(g):
        place_borders(g)
        border = packed_border[g]
        x = jnp.concatenate([border[:16], packed[g, 16 : lon - 16], border[16:]], axis=0)
        y = dot(x, tiles[g])
        conv[g] = y[:lon].T
        conv_edge[g] = y[lon : lon + EDGE]

    unrolled(groups, band)

    total_in[...] = jnp.zeros_like(total_in)
    total_out[...] = jnp.zeros_like(total_out)
    total_gain[...] = jnp.zeros_like(total_gain)

    gain_tile = gain_columns[...]

    def normalise(y, g, inner):
        cols = y.shape[1]
        gains = jnp.concatenate([gain_tile] * (cols // 128), axis=1)
        y = y - jnp.sum(y, axis=0, keepdims=True) * (1.0 / channels)
        var = jnp.sum(y * y, axis=0, keepdims=True) * (1.0 / channels)
        sigma = lax.rsqrt(var + 1e-6)
        nhat = y * sigma
        normed = (nhat * gains).astype(BF16)
        normed = jnp.concatenate([normed, jnp.ones((64, cols), BF16)], axis=0)
        state = dict(inner=inner, gains=gains, sigma=sigma, nhat=nhat, normed=normed, g=g)
        if inner:
            state.update(upright=normed.T, g_upright=g.T)
        return state

    def head(state, h):
        at = slice(h, h + 256)
        return dot(turned_in[at, :], state["normed"]), dot(turned_out[at, :], state["g"])

    def tail(state, h, z, d_act):
        at = slice(h, h + 256)
        cumulative, density = gelu_parts(z)
        d_pre = (d_act * (cumulative + z * density)).astype(BF16)
        state.setdefault("d_pre", []).append(d_pre)
        if h + 256 == hidden:
            state["d_normed"] = dot(w_in[...], jnp.concatenate(state["d_pre"], axis=0))
        if state["inner"]:
            act = (z * cumulative).astype(BF16)
            state.setdefault("act", []).append(act)
            if h + 256 == hidden:
                state["branch"] = dot(w_out[...], jnp.concatenate(state["act"], axis=0))
            total_in[at, :] += dot(d_pre, state["upright"])
            total_out[at, :] += dot(act, state["g_upright"])

    def finish(state):
        nhat, gains = state["nhat"], state["gains"]
        prod = state["d_normed"] * nhat
        if state["inner"]:
            part = prod[:, :128]
            for c in range(128, prod.shape[1], 128):
                part = part + prod[:, c : c + 128]
            total_gain[...] += part
        d_hat = state["d_normed"] * gains
        mean = jnp.sum(d_hat, axis=0, keepdims=True) * (1.0 / channels)
        corr = jnp.sum(prod * gains, axis=0, keepdims=True) * (1.0 / channels)
        return (state["sigma"] * (d_hat - mean - nhat * corr)).astype(BF16)

    count = 4
    blocks = lat // count
    copies = []

    def start(r):
        rows = range(count * r, count * (r + 1))
        y = []
        for i in rows:
            at = slice(i * GROUP, (i + 1) * GROUP)
            y.append(jnp.concatenate([conv[g, at, :] for g in range(groups)], axis=0))
        return normalise(
            jnp.concatenate(y, axis=1), jnp.concatenate([gm[i] for i in rows], axis=1), True
        )

    def start_edges():
        lane = iota((1, 128), 1)
        y = []
        for i in range(lat):
            half, k = (i * GROUP) // 128 * 128, i % 8
            line = []
            for tile in range(0, channels, 128):
                x = jnp.zeros((EDGE, 128), F32)
                for g in range(tile // GROUP, min(tile + 128, channels) // GROUP):
                    piece = conv_edge[g, :, half : half + 128]
                    piece = pltpu.roll(piece, (g - k) % 8 * GROUP, axis=1)
                    x = jnp.where((lane >> 4) == g % 8, piece, x)
                line.append(x)
            y.append(jnp.concatenate(line, axis=1))
        y = jnp.concatenate(y, axis=0).T[:channels]
        at = 2 * groups * EDGE
        near = (lane & (EDGE - 1)) < EDGE // 2
        top = jnp.where(near, after[at:], before[at:])
        bottom = jnp.where(
            near,
            pltpu.roll(after[at:], 128 - EDGE // 2, axis=1),
            pltpu.roll(before[at:], EDGE // 2, axis=1),
        )
        g = jnp.concatenate([top, bottom], axis=0).astype(BF16)
        return normalise(y, g, False)

    def end(r, state):
        d = finish(state)
        if r == blocks:
            d_edge[...] = d
            return
        for k in range(count):
            i = count * r + k
            at = slice(k * lon, (k + 1) * lon)
            x = masked[i].astype(F32) + state["branch"][:, at]
            rows_out[i] = (x * mask[i : i + 1]).astype(BF16)
            d_conv[i] = d[:, at]
        at = slice(count * r, count * (r + 1))
        copies.append(pltpu.make_async_copy(rows_out.at[at], output.at[at], sent.at[r]))
        copies[-1].start()

    steps = [(r, h) for r in range(blocks + 1) for h in range(0, hidden, 256)]
    states = {0: start(0)}
    coming = head(states[0], 0)
    for n, (r, h) in enumerate(steps):
        here = coming
        if h == 256 and r < blocks:
            states[r + 1] = start(r + 1) if r + 1 < blocks else start_edges()
        if n + 1 < len(steps):
            coming = head(states[steps[n + 1][0]], steps[n + 1][1])
        tail(states[r], h, *here)
        if h + 256 == hidden:
            end(r, states.pop(r))

    first = core[0] == 0
    rows = channels // shards
    sum_in = total_in[...].T
    parts_in, parts_out = [], []
    for n in range(shards):
        mine = sum_in[n * rows : (n + 1) * rows]
        parts_in += [mine[:, c : c + 128] for c in range(0, hidden, 128)]
    rows = hidden // shards
    for n in range(shards):
        mine = total_out[n * rows : (n + 1) * rows]
        parts_out.append(mine[:, :128])
        parts_out.append(
            jnp.concatenate([mine[: rows // 2, 128:], mine[rows // 2 :, 128:]], axis=1)
        )
    parts_in, parts_out = jnp.concatenate(parts_in, axis=0), jnp.concatenate(parts_out, axis=0)
    keep[...] = jnp.where(first, parts_in, parts_out).astype(BF16)
    send[...] = jnp.where(first, parts_out, parts_in).astype(BF16)
    sums[:, :hidden] = sum_in[channels : channels + 8]
    sums[:, hidden:] = jnp.broadcast_to(
        jnp.sum(total_gain[...].T, axis=0, keepdims=True), (8, channels)
    )
    for copy in copies:
        copy.wait()


def laid_cells(d_conv, d_edge, cells):
    lat, channels, lon = d_conv.shape
    rows = [d_conv[i] for i in range(lat)]
    near = iota((EDGE, 1), 0) < EDGE // 2
    lane = iota((1, 128), 1) >> 4
    blank = jnp.zeros((EDGE, 128), F32)
    edges = d_edge[...].astype(F32).T

    def place(g):
        x = group_of(rows, g).astype(F32).T
        tile = (g * GROUP) // 128 * 128
        for half in range(2):
            edge = blank
            for k in range(8):
                i = 8 * half + k
                piece = edges[i * EDGE : (i + 1) * EDGE, tile : min(tile + 128, channels)]
                if piece.shape[1] < 128:
                    piece = jnp.concatenate([piece, piece], axis=1)
                shift = (k * GROUP - (g * GROUP - tile)) % 128
                edge = jnp.where(lane == k, pltpu.roll(piece, shift, axis=1), edge)
            cells[2 * g + half] = jnp.concatenate(
                [
                    blank,
                    jnp.where(near, 0.0, edge),
                    x[:, half * 128 : (half + 1) * 128],
                    jnp.where(near, edge, 0.0),
                    blank,
                ],
                axis=0,
            )

    return place


def taps_kernel(masked, d_conv, d_edge, sums, out, cells, packed, small):
    lat, channels, lon = masked.shape
    groups = channels // GROUP
    place_cells = laid_cells(d_conv, d_edge, cells)
    rows = [masked[i] for i in range(lat)]
    bands = [band_mask(i) for i in range(lat)]
    sub, lane = iota((8, 1), 0), iota((1, 128), 1) >> 4
    small[...] = jnp.zeros_like(small)

    for g in range(groups):
        place_cells(g)
        pack_group(cells, packed, lon, g)
        products = dot(group_of(rows, g), packed[g])
        taps = jnp.zeros((8, 128), F32)
        for b in range(7):
            parts = [None] * 8
            for i in range(lat):
                at = slice(i * GROUP, (i + 1) * GROUP)
                part = jnp.zeros((GROUP, 128), F32)
                if i < 11:
                    part = jnp.where(bands[i][:, :128], products[at, b * 256 : b * 256 + 128], part)
                if i > 4:
                    part = jnp.where(bands[i][:, 128:], products[at, b * 256 + 128 : b * 256 + 256], part)
                part = part[:8] + part[8:]
                parts[i % 8] = part if parts[i % 8] is None else parts[i % 8] + part
            total = None
            for i in range(8):
                part = pltpu.roll(parts[i], (3 - i) % 8 * GROUP, axis=1)
                total = part if total is None else total + part
            total = jnp.sum(total, axis=0, keepdims=True)
            taps = jnp.where(sub == 6 - b, total, taps)
        for a in range(7):
            place, slot = (a, g) if g < 8 else (7 + a // 2, g % 4 + 4 * (a % 2))
            moved = pltpu.roll(taps, (slot + a - 6) % 8 * GROUP, axis=1)
            small[place] = jnp.where(lane == slot, moved, small[place])

    line = sums[0:1]
    hidden = line.shape[1] - channels
    pieces = [line[:, c : c + 128] for c in range(0, hidden, 128)]
    pieces.append(line[:, hidden : hidden + 128])
    pieces.append(
        jnp.concatenate([line[:, hidden + 128 :], jnp.zeros((1, 256 - channels), F32)], axis=1)
    )
    for k, piece in enumerate(pieces):
        small[k, 7:8] = piece
    out[...] = small[...].reshape(SMALL, 128).astype(BF16)


def fold_kernel(have, keep, arrived, small, kept, sent, shards):
    rows = kept.shape[0]
    total = keep[...].astype(F32) + arrived[...].astype(F32)
    total = total.reshape(-1, 2, total.shape[0] // shards, 128)
    even, odd = total[:, 0].reshape(rows, 128), total[:, 1].reshape(rows, 128)
    first = have[0] == 0
    kept[...] = jnp.where(first, even, odd).astype(BF16)
    sent[:rows] = jnp.where(first, odd, even).astype(BF16)
    sent[rows:] = small[...]


def spread_kernel(gm, mask, lines, d_conv, d_edge, grad_fields, rolled, tiles, cells, packed, spread):
    lat, channels, lon = gm.shape
    groups = channels // GROUP
    build_tiles(lines, rolled, tiles, True)
    place_cells = laid_cells(d_conv, d_edge, cells)

    def band(g):
        place_cells(g)
        pack_group(cells, packed, lon, g)
        spread[g] = dot(packed[g], tiles[g]).T

    unrolled(groups, band)
    for i in range(lat):
        x = jnp.concatenate(
            [spread[g, i * GROUP : (i + 1) * GROUP, :] for g in range(groups)], axis=0
        )
        x = gm[i].astype(F32) + x * mask[i : i + 1]
        grad_fields[i] = x.astype(BF16)


def final_kernel(core, mine, other, grad_in, grad_out, grad_kernel, grad_gain, grad_bias, scale):
    first = core[0] == 0
    mine, other = mine[...].astype(F32) * scale, other[...].astype(F32) * scale
    sum_in, sum_out = jnp.where(first, mine, other), jnp.where(first, other, mine)
    at = mine.shape[0] - SMALL
    small = mine[at:] + other[at:]
    sum_in, sum_out = sum_in[:at], sum_out[:at]
    rows, hidden = grad_in.shape
    for k in range(hidden // 128):
        grad_in[:, k * 128 : (k + 1) * 128] = sum_in[k * rows : (k + 1) * rows]
    rows, channels = grad_out.shape
    grad_out[:, :128] = sum_out[:rows]
    rest = sum_out[rows:]
    grad_out[:, 128:] = jnp.concatenate([rest[:, :64], rest[:, 64:]], axis=0)
    for a in range(7):
        at = 8 * (7 + a // 2)
        half = slice(64 * (a % 2), 64 * (a % 2) + 64)
        grad_kernel[a, :, :128] = small[8 * a : 8 * a + 7]
        grad_kernel[a, :, 128:] = small[at : at + 7, half]
    lines = [small[8 * k + 7 : 8 * k + 8] for k in range(hidden // 128 + 2)]
    grad_bias[...] = jnp.concatenate(lines[:-2], axis=1).reshape(hidden)
    grad_gain[...] = jnp.concatenate([lines[-2], lines[-1][:, : channels - 128]], axis=1).reshape(
        channels
    )


def swapped(x, axis, bit):
    peers = lax.axis_size(axis)
    return lax.ppermute(x, axis, [(i, i ^ bit) for i in range(peers)])


def bits_of(count):
    return [1 << k for k in range(count.bit_length() - 1)]


def pick(x, axis, at):
    return lax.dynamic_index_in_dim(x, at, axis, keepdims=False)


def both(x, y):
    return (x.astype(F32) + y.astype(F32)).astype(BF16)


def halved(mine, bit):
    have = (lax.axis_index("dp") // bit) & 1
    split = mine.reshape(mine.shape[0] // 2, 2, -1, 128)
    kept, sent = pick(split, 1, have), pick(split, 1, 1 - have)
    return kept, sent.reshape(-1, 128)


VMEM, SMEM, FAR = pltpu.VMEM, pltpu.SMEM, pltpu.HBM


def call(body, name, outs, scratch, megabytes, spaces, out_spaces):
    def held(space, shape, dtype):
        return VMEM(shape, dtype) if space is VMEM else jax.ShapeDtypeStruct(shape, dtype)

    def spec(space):
        return pl.BlockSpec(memory_space={SMEM: SMEM, FAR: pl.ANY}.get(space, VMEM))

    kernel = pl.pallas_call(
        body,
        out_shape=[held(space, *out) for space, out in zip(out_spaces, outs, strict=True)],
        in_specs=[spec(space) for space in spaces],
        out_specs=[spec(space) for space in out_spaces],
        scratch_shapes=[x if not isinstance(x, tuple) else VMEM(*x) for x in scratch],
        compiler_params=pltpu.CompilerParams(vmem_limit_bytes=megabytes * 2**20),
        name=name,
    )

    def run(*args):
        return kernel(
            *[
                pltpu.with_memory_space_constraint(x, space) if space in (FAR, VMEM) else x
                for x, space in zip(args, spaces, strict=True)
            ]
        )

    return run


def per_device(fields, cotangent, land_sea, kernel, ln_gain, weight_in, bias_in, weight_out):
    samples, lat, lon, channels = fields.shape
    hidden = weight_in.shape[1]
    shards, tiles = lax.axis_size("dp"), lax.axis_size("lon")
    groups = channels // GROUP
    rows = channels * hidden // 128
    core = (lax.axis_index("lon") & 1).reshape(1)
    fields = fields[0].transpose(0, 2, 1)
    cotangent = cotangent[0].transpose(0, 2, 1)
    w_out = weight_out.T

    field = ((lat, channels, lon), BF16)
    halo = ((channels + channels // 2, 128), BF16)
    edge = ((channels, 128), BF16)
    rolled = ((16, 8 * groups, 256), F32)
    tile = ((groups, 7 * 256, 256), BF16)
    cells = ((2 * groups, lon + 4 * EDGE, 128), F32)
    packed = ((groups, lon, 7 * 256), BF16)
    border = ((2 * groups, 2 * EDGE + BORDER, 128), F32)
    held = ((groups, 256, lon), F32)

    first, last, masked, gm, mask = call(
        edge_kernel,
        "edges",
        [halo, halo, field, field, ((lat, lon), F32)],
        [field, field, ((lat, lon), jnp.int32), pltpu.SemaphoreType.DMA((9,))],
        8,
        [FAR] * 3,
        [VMEM] * 5,
    )(fields, cotangent, land_sea)
    up = [(i, (i + 1) % tiles) for i in range(tiles)]
    before = lax.ppermute(last, "lon", up)
    after = lax.ppermute(first, "lon", [(j, i) for i, j in up])

    ready = call(
        prepare_kernel,
        "prepare",
        [
            tile,
            packed,
            ((2 * groups, 2 * BORDER, 128), F32),
            ((hidden, 256), BF16),
            ((hidden, channels), BF16),
            ((channels, hidden), BF16),
            ((channels, hidden), BF16),
            ((channels, 128), F32),
            ((8 * groups, 256), F32),
        ],
        [
            rolled,
            cells,
            ((7, 7, channels), F32),
            ((channels,), F32),
            ((hidden,), F32),
            pltpu.SemaphoreType.DMA((5,)),
        ],
        8,
        [VMEM] + [FAR] * 5,
        [VMEM] * 9,
    )(masked, kernel, ln_gain, weight_in, bias_in, w_out)
    lines = ready[-1]

    lines = ready[-1]
    output, d_conv, d_edge, keep, send, sums = call(
        functools.partial(forward_kernel, shards=shards),
        "forward",
        [
            field,
            field,
            edge,
            ((rows, 128), BF16),
            ((rows, 128), BF16),
            ((8, hidden + channels), F32),
        ],
        [
            border,
            border,
            ((groups, 48, 7 * 256), BF16),
            held,
            ((groups, EDGE, 256), F32),
            ((hidden, 256), F32),
            ((hidden, channels), F32),
            ((channels, 128), F32),
            field,
            pltpu.SemaphoreType.DMA((lat // 4,)),
        ],
        14,
        [SMEM] + [VMEM] * 13,
        [FAR] + [VMEM] * 5,
    )(core, before, after, masked, gm, mask, *ready[:-1])

    arrived = swapped(send, "lon", 1)
    (small,) = call(
        taps_kernel,
        "taps",
        [((SMALL, 128), BF16)],
        [cells, packed, ((12, 8, 128), F32)],
        10,
        [VMEM] * 4,
        [VMEM],
    )(masked, d_conv, d_edge, sums)
    have = (lax.axis_index("dp") & 1).reshape(1)
    kept, sent = call(
        functools.partial(fold_kernel, shards=shards),
        "fold",
        [((rows // 2, 128), BF16), ((rows // 2 + SMALL, 128), BF16)],
        [],
        6,
        [SMEM] + [VMEM] * 3,
        [VMEM] * 2,
    )(have, keep, arrived, small)

    sent, d_conv = lax.optimization_barrier((sent, d_conv))
    arrived = swapped(sent, "dp", 1)
    (grad_fields,) = call(
        spread_kernel,
        "spread",
        [field],
        [rolled, tile, cells, packed, held],
        24,
        [VMEM] * 5,
        [None],
    )(gm, mask, lines, d_conv, d_edge)
    arrived, grad_fields = lax.optimization_barrier((arrived, grad_fields))
    mine = both(kept, arrived[: rows // 2]).reshape(shards // 2, -1, 128)
    small = both(small, arrived[rows // 2 :])
    for bit in bits_of(shards)[1:]:
        kept, sent = halved(mine, bit)
        count = sent.shape[0]
        arrived = swapped(jnp.concatenate([sent, small], axis=0), "dp", bit)
        mine = both(kept, arrived[:count].reshape(kept.shape))
        small = both(small, arrived[count:])
    mine = jnp.concatenate([mine.reshape(-1, 128), small], axis=0)
    for bit in bits_of(tiles)[1:]:
        mine = both(mine, swapped(mine, "lon", bit))
    other = swapped(mine, "lon", 1)

    scale = 1.0 / math.sqrt(samples * lat * lon * shards * tiles)
    grads = call(
        functools.partial(final_kernel, scale=scale),
        "final",
        [
            ((channels // shards, hidden), F32),
            ((hidden // shards, channels), F32),
            ((7, 7, channels), F32),
            ((channels,), F32),
            ((hidden,), F32),
        ],
        [],
        8,
        [SMEM] + [VMEM] * 2,
        [None] * 5,
    )(core, mine, other)
    return (output.transpose(0, 2, 1)[None], grad_fields.transpose(0, 2, 1)[None], *grads)


def solution(mesh):
    placed = (
        P("dp", None, "lon", None),
        P("dp", None, "lon", None),
        P(None, "lon"),
        P(),
        P(),
        P(),
        P(),
        P(),
    )
    return jax.shard_map(
        per_device,
        mesh=mesh,
        in_specs=placed,
        out_specs=(
            P("dp", None, "lon", None),
            P("dp", None, "lon", None),
            P("dp", None),
            P("dp", None),
            P(),
            P(),
            P(),
        ),
        check_vma=False,
    )
```

```python
import functools
import math

import jax
import jax.numpy as jnp
from jax import lax
from jax.experimental import pallas as pl
from jax.experimental.pallas import tpu as pltpu
from jax.sharding import PartitionSpec as P

F32 = jnp.float32
BF16 = jnp.bfloat16
EDGE = 8
GROUP = 16


def dot(lhs, rhs):
    return jnp.dot(lhs, rhs, preferred_element_type=F32)


def dot_t(lhs, rhs):
    return lax.dot_general(lhs, rhs, (((1,), (1,)), ((), ())), preferred_element_type=F32)


def iota(shape, axis):
    return lax.broadcasted_iota(jnp.int32, shape, axis)


def identity(size):
    return jnp.where(iota((size, size), 0) == iota((size, size), 1), 1.0, 0.0).astype(BF16)


def masked_row(array, mask, i):
    return (array[i].astype(F32) * mask[i : i + 1]).astype(BF16)


def group_of(rows, g):
    return jnp.concatenate([row[GROUP * g : GROUP * (g + 1)] for row in rows], axis=0)


def band_mask(i):
    shape = (GROUP, 256)
    lane = iota(shape, 1)
    same = (lane & (GROUP - 1)) == iota(shape, 0)
    return same & (jnp.abs((lane >> 4) - i) <= 3)


def unrolled(count, body):
    for k in range(count):
        body(k)


def lay_lines(kernel, lines):
    taps, cols, channels = kernel.shape
    lane = iota((1, 128), 1) >> 4
    zero = jnp.zeros((1, channels), F32)
    rows = [jnp.concatenate([kernel[a], zero], axis=0) for a in range(taps)]
    for g in range(channels // GROUP):
        tile = g * GROUP // 128 * 128
        halves = [jnp.zeros((8, 128), F32)] * 2
        for a in range(taps):
            piece = rows[a][:, tile : min(tile + 128, channels)]
            if piece.shape[1] < 128:
                piece = jnp.concatenate([piece, piece], axis=1)
            for half, slot in ((0, taps - 1 - a), (1, a)):
                moved = pltpu.roll(piece, (slot - g) % 8 * GROUP, axis=1)
                halves[half] = jnp.where(lane == slot, moved, halves[half])
        lines[8 * g : 8 * g + 8] = jnp.concatenate(halves, axis=1)


def build_tiles(lines, rolled, tiles, flip):
    here = iota((1, 256), 1) < 128
    own = jnp.where(here, pltpu.roll(lines[...], 128, axis=1) if flip else lines[...], 0.0)
    for i in range(16):
        rolled[i] = pltpu.roll(own, ((i - 3) * GROUP) % 256, axis=1)
    masks = [band_mask(i) for i in range(16)]

    def group(g):
        for b in range(7):
            for i in range(16):
                k = 8 * g + (6 - b if flip else b)
                line = rolled[i, k : k + 1, :]
                at = b * 256 + i * GROUP
                tiles[g, at : at + GROUP, :] = jnp.where(masks[i], line, 0.0).astype(BF16)

    unrolled(tiles.shape[0], group)


def pack_group(cells, packed, lon, g):
    for half in range(2):
        for b in range(7):
            x = cells[2 * g + half, 2 * EDGE + b - 3 : 2 * EDGE + b - 3 + lon, :]
            at = b * 256 + half * 128
            packed[g, :, at : at + 128] = x.astype(BF16)


BORDER = 24
SMALL = 96


def pack_borders(before, after, borders, left, right, packed):
    groups = packed.shape[0]
    near = iota((EDGE, 1), 0) < EDGE // 2
    blank = jnp.zeros((EDGE, 128), F32)

    def place(g):
        for half in range(2):
            k = 2 * g + half
            at = half * groups * EDGE + g * EDGE
            halo = slice(at, at + EDGE)
            left[k] = jnp.concatenate([blank, before[halo], borders[k, :BORDER]], axis=0)
            right[k] = jnp.concatenate([borders[k, BORDER:], after[halo], blank], axis=0)
            for b in range(7):
                s = b - 3
                inner = left[k, 2 * EDGE + s : 2 * EDGE + s + 16, :]
                outer = right[k, BORDER - 16 + s : BORDER + s, :]
                beyond = jnp.where(
                    near,
                    right[k, BORDER + s : BORDER + s + EDGE, :],
                    left[k, EDGE + s : 2 * EDGE + s, :],
                )
                x = jnp.concatenate([inner, outer, beyond, beyond], axis=0)
                at = b * 256 + half * 128
                packed[g, :, at : at + 128] = x.astype(BF16)

    return place


def gelu_parts(z):
    cumulative = 0.5 + 0.5 * lax.erf(z * math.sqrt(0.5))
    density = jnp.exp2(z * z * (-0.5 * math.log2(math.e))) * (1.0 / math.sqrt(2.0 * math.pi))
    return cumulative, density


def edge_kernel(
    fields, cotangent, mask, first, last, masked, gm, near_mask, held_x, held_g, held_mask, arrived
):
    lat, channels, lon = fields.shape
    groups = channels // GROUP
    count = lat // 2
    copies = [pltpu.make_async_copy(mask, held_mask, arrived.at[0])]
    for r in range(2):
        at = slice(count * r, count * (r + 1))
        for k, (far, held) in enumerate(((fields, held_x), (cotangent, held_g))):
            copies.append(
                pltpu.make_async_copy(far.at[at], held.at[at], arrived.at[1 + 2 * r + k])
            )
    for copy in copies:
        copy.start()
    row, lane = iota((2 * EDGE, lon), 0), iota((2 * EDGE, lon), 1)
    ends = jnp.where(lane == jnp.where(row < EDGE, row, row + lon - 2 * EDGE), 1.0, 0.0)
    ends = ends.astype(BF16)
    copies[0].wait()
    near_mask[...] = held_mask[...].astype(F32)
    rows, outer = [], []
    for r in range(2):
        copies[1 + 2 * r].wait()
        copies[2 + 2 * r].wait()
        for i in range(count * r, count * (r + 1)):
            rows.append(masked_row(held_x, near_mask, i))
            turned = masked_row(held_g, near_mask, i)
            outer.append(dot_t(ends, turned))
            masked[i] = rows[i]
            gm[i] = turned
    cells = [dot_t(ends, group_of(rows, g)) for g in range(groups)]
    for k, out in enumerate((first, last)):
        for half in range(2):
            at = slice(half * 128, (half + 1) * 128)
            x = [cell[k * EDGE : (k + 1) * EDGE, at] for cell in cells]
            count = groups * EDGE
            out[half * count : (half + 1) * count] = jnp.concatenate(x, axis=0).astype(BF16)
        g = jnp.concatenate([x[k * EDGE : (k + 1) * EDGE] for x in outer], axis=0).T
        top, bottom = g[: channels // 2], g[channels // 2 :]
        near = (iota((1, 128), 1) & (EDGE - 1)) < EDGE // 2
        if k == 0:
            g = jnp.where(near, top, pltpu.roll(bottom, EDGE // 2, axis=1))
        else:
            g = jnp.where(near, pltpu.roll(bottom, 128 - EDGE // 2, axis=1), top)
        out[2 * groups * EDGE :] = g.astype(BF16)


def prepare_kernel(
    masked,
    kernel,
    gain,
    w_in,
    bias,
    w_out,
    tiles,
    packed,
    borders,
    turned_in,
    turned_out,
    near_in,
    near_out,
    gain_columns,
    lines,
    rolled,
    cells,
    near_kernel,
    near_gain,
    near_bias,
    arrived,
):
    lat, channels, lon = masked.shape
    hidden = w_in.shape[1]
    groups = channels // GROUP
    far = (kernel, gain, w_in, bias, w_out)
    near = (near_kernel, near_gain, near_in, near_bias, near_out)
    copies = [
        pltpu.make_async_copy(x, y, arrived.at[k])
        for k, (x, y) in enumerate(zip(far, near, strict=True))
    ]
    for copy in copies:
        copy.start()

    rows = [masked[i] for i in range(lat)]
    blank = jnp.zeros((2 * EDGE, 128), F32)
    for g in range(groups):
        x = group_of(rows, g).astype(F32).T
        for half in range(2):
            k = 2 * g + half
            part = x[:, half * 128 : (half + 1) * 128]
            cells[k] = jnp.concatenate([blank, part, blank], axis=0)
            borders[k] = jnp.concatenate([part[:BORDER], part[lon - BORDER :]], axis=0)
        pack_group(cells, packed, lon, g)

    for copy in copies:
        copy.wait()
    lay_lines(near_kernel, lines)
    build_tiles(lines, rolled, tiles, False)
    gain_row = near_gain[...].reshape(1, channels)
    gain_columns[...] = jnp.broadcast_to(gain_row, (128, channels)).T
    bias_row = near_bias[...].reshape(1, hidden)
    bias_columns = jnp.broadcast_to(bias_row, (64, hidden)).T
    lane = iota((hidden, 64), 1)
    high = bias_columns.astype(BF16).astype(F32)
    middle = (bias_columns - high).astype(BF16).astype(F32)
    low = bias_columns - high - middle
    bias_columns = jnp.where(
        lane == 0, high, jnp.where(lane == 1, middle, jnp.where(lane == 2, low, 0.0))
    )
    turned_in[...] = jnp.concatenate([near_in[...].T, bias_columns.astype(BF16)], axis=1)
    turned_out[...] = near_out[...].T


def forward_kernel(
    core,
    halo_before,
    halo_after,
    masked,
    gm,
    mask,
    tiles,
    packed,
    borders,
    turned_in,
    turned_out,
    w_in,
    w_out,
    gain_columns,
    output,
    d_conv,
    d_edge,
    keep,
    send,
    sums,
    left,
    right,
    packed_border,
    conv,
    conv_edge,
    total_in,
    total_out,
    total_gain,
    rows_out,
    sent,
    shards,
):
    lat, channels, lon = gm.shape
    hidden = w_in.shape[1]
    groups = channels // GROUP
    before, after = halo_before[...].astype(F32), halo_after[...].astype(F32)
    place_borders = pack_borders(before, after, borders, left, right, packed_border)

    def band(g):
        place_borders(g)
        border = packed_border[g]
        x = jnp.concatenate([border[:16], packed[g, 16 : lon - 16], border[16:]], axis=0)
        y = dot(x, tiles[g])
        conv[g] = y[:lon].T
        conv_edge[g] = y[lon : lon + EDGE]

    unrolled(groups, band)

    total_in[...] = jnp.zeros_like(total_in)
    total_out[...] = jnp.zeros_like(total_out)
    total_gain[...] = jnp.zeros_like(total_gain)

    gain_tile = gain_columns[...]

    def normalise(y, g, inner):
        cols = y.shape[1]
        gains = jnp.concatenate([gain_tile] * (cols // 128), axis=1)
        y = y - jnp.sum(y, axis=0, keepdims=True) * (1.0 / channels)
        var = jnp.sum(y * y, axis=0, keepdims=True) * (1.0 / channels)
        sigma = lax.rsqrt(var + 1e-6)
        nhat = y * sigma
        normed = (nhat * gains).astype(BF16)
        normed = jnp.concatenate([normed, jnp.ones((64, cols), BF16)], axis=0)
        state = dict(inner=inner, gains=gains, sigma=sigma, nhat=nhat, normed=normed, g=g)
        if inner:
            state.update(upright=normed.T, g_upright=g.T)
        return state

    def head(state, h):
        at = slice(h, h + 256)
        return dot(turned_in[at, :], state["normed"]), dot(turned_out[at, :], state["g"])

    def tail(state, h, z, d_act):
        at = slice(h, h + 256)
        cumulative, density = gelu_parts(z)
        d_pre = (d_act * (cumulative + z * density)).astype(BF16)
        state.setdefault("d_pre", []).append(d_pre)
        if h + 256 == hidden:
            state["d_normed"] = dot(w_in[...], jnp.concatenate(state["d_pre"], axis=0))
        if state["inner"]:
            act = (z * cumulative).astype(BF16)
            state.setdefault("act", []).append(act)
            if h + 256 == hidden:
                state["branch"] = dot(w_out[...], jnp.concatenate(state["act"], axis=0))
            total_in[at, :] += dot(d_pre, state["upright"])
            total_out[at, :] += dot(act, state["g_upright"])

    def finish(state):
        nhat, gains = state["nhat"], state["gains"]
        prod = state["d_normed"] * nhat
        if state["inner"]:
            part = prod[:, :128]
            for c in range(128, prod.shape[1], 128):
                part = part + prod[:, c : c + 128]
            total_gain[...] += part
        d_hat = state["d_normed"] * gains
        mean = jnp.sum(d_hat, axis=0, keepdims=True) * (1.0 / channels)
        corr = jnp.sum(prod * gains, axis=0, keepdims=True) * (1.0 / channels)
        return (state["sigma"] * (d_hat - mean - nhat * corr)).astype(BF16)

    count = 4
    blocks = lat // count
    copies = []

    def start(r):
        rows = range(count * r, count * (r + 1))
        y = []
        for i in rows:
            at = slice(i * GROUP, (i + 1) * GROUP)
            y.append(jnp.concatenate([conv[g, at, :] for g in range(groups)], axis=0))
        return normalise(
            jnp.concatenate(y, axis=1), jnp.concatenate([gm[i] for i in rows], axis=1), True
        )

    def start_edges():
        lane = iota((1, 128), 1)
        y = []
        for i in range(lat):
            half, k = (i * GROUP) // 128 * 128, i % 8
            line = []
            for tile in range(0, channels, 128):
                x = jnp.zeros((EDGE, 128), F32)
                for g in range(tile // GROUP, min(tile + 128, channels) // GROUP):
                    piece = conv_edge[g, :, half : half + 128]
                    piece = pltpu.roll(piece, (g - k) % 8 * GROUP, axis=1)
                    x = jnp.where((lane >> 4) == g % 8, piece, x)
                line.append(x)
            y.append(jnp.concatenate(line, axis=1))
        y = jnp.concatenate(y, axis=0).T[:channels]
        at = 2 * groups * EDGE
        near = (lane & (EDGE - 1)) < EDGE // 2
        top = jnp.where(near, after[at:], before[at:])
        bottom = jnp.where(
            near,
            pltpu.roll(after[at:], 128 - EDGE // 2, axis=1),
            pltpu.roll(before[at:], EDGE // 2, axis=1),
        )
        g = jnp.concatenate([top, bottom], axis=0).astype(BF16)
        return normalise(y, g, False)

    def end(r, state):
        d = finish(state)
        if r == blocks:
            d_edge[...] = d
            return
        for k in range(count):
            i = count * r + k
            at = slice(k * lon, (k + 1) * lon)
            x = masked[i].astype(F32) + state["branch"][:, at]
            rows_out[i] = (x * mask[i : i + 1]).astype(BF16)
            d_conv[i] = d[:, at]
        at = slice(count * r, count * (r + 1))
        copies.append(pltpu.make_async_copy(rows_out.at[at], output.at[at], sent.at[r]))
        copies[-1].start()

    steps = [(r, h) for r in range(blocks + 1) for h in range(0, hidden, 256)]
    states = {0: start(0)}
    coming = head(states[0], 0)
    for n, (r, h) in enumerate(steps):
        here = coming
        if h == 256 and r < blocks:
            states[r + 1] = start(r + 1) if r + 1 < blocks else start_edges()
        if n + 1 < len(steps):
            coming = head(states[steps[n + 1][0]], steps[n + 1][1])
        tail(states[r], h, *here)
        if h + 256 == hidden:
            end(r, states.pop(r))

    first = core[0] == 0
    rows = channels // shards
    sum_in = total_in[...].T
    parts_in, parts_out = [], []
    for n in range(shards):
        mine = sum_in[n * rows : (n + 1) * rows]
        parts_in += [mine[:, c : c + 128] for c in range(0, hidden, 128)]
    rows = hidden // shards
    for n in range(shards):
        mine = total_out[n * rows : (n + 1) * rows]
        parts_out.append(mine[:, :128])
        parts_out.append(
            jnp.concatenate([mine[: rows // 2, 128:], mine[rows // 2 :, 128:]], axis=1)
        )
    parts_in, parts_out = jnp.concatenate(parts_in, axis=0), jnp.concatenate(parts_out, axis=0)
    keep[...] = jnp.where(first, parts_in, parts_out).astype(BF16)
    send[...] = jnp.where(first, parts_out, parts_in).astype(BF16)
    sums[:, :hidden] = sum_in[channels : channels + 8]
    sums[:, hidden:] = jnp.broadcast_to(
        jnp.sum(total_gain[...].T, axis=0, keepdims=True), (8, channels)
    )
    for copy in copies:
        copy.wait()


def laid_cells(d_conv, d_edge, cells):
    lat, channels, lon = d_conv.shape
    rows = [d_conv[i] for i in range(lat)]
    near = iota((EDGE, 1), 0) < EDGE // 2
    lane = iota((1, 128), 1) >> 4
    blank = jnp.zeros((EDGE, 128), F32)
    edges = d_edge[...].astype(F32).T

    def place(g):
        x = group_of(rows, g).astype(F32).T
        tile = (g * GROUP) // 128 * 128
        for half in range(2):
            edge = blank
            for k in range(8):
                i = 8 * half + k
                piece = edges[i * EDGE : (i + 1) * EDGE, tile : min(tile + 128, channels)]
                if piece.shape[1] < 128:
                    piece = jnp.concatenate([piece, piece], axis=1)
                shift = (k * GROUP - (g * GROUP - tile)) % 128
                edge = jnp.where(lane == k, pltpu.roll(piece, shift, axis=1), edge)
            cells[2 * g + half] = jnp.concatenate(
                [
                    blank,
                    jnp.where(near, 0.0, edge),
                    x[:, half * 128 : (half + 1) * 128],
                    jnp.where(near, edge, 0.0),
                    blank,
                ],
                axis=0,
            )

    return place


def taps_kernel(masked, d_conv, d_edge, sums, out, cells, packed, small):
    lat, channels, lon = masked.shape
    groups = channels // GROUP
    place_cells = laid_cells(d_conv, d_edge, cells)
    rows = [masked[i] for i in range(lat)]
    bands = [band_mask(i) for i in range(lat)]
    sub, lane = iota((8, 1), 0), iota((1, 128), 1) >> 4
    small[...] = jnp.zeros_like(small)

    for g in range(groups):
        place_cells(g)
        pack_group(cells, packed, lon, g)
        products = dot(group_of(rows, g), packed[g])
        taps = jnp.zeros((8, 128), F32)
        for b in range(7):
            parts = [None] * 8
            for i in range(lat):
                at = slice(i * GROUP, (i + 1) * GROUP)
                part = jnp.zeros((GROUP, 128), F32)
                if i < 11:
                    part = jnp.where(bands[i][:, :128], products[at, b * 256 : b * 256 + 128], part)
                if i > 4:
                    part = jnp.where(bands[i][:, 128:], products[at, b * 256 + 128 : b * 256 + 256], part)
                part = part[:8] + part[8:]
                parts[i % 8] = part if parts[i % 8] is None else parts[i % 8] + part
            total = None
            for i in range(8):
                part = pltpu.roll(parts[i], (3 - i) % 8 * GROUP, axis=1)
                total = part if total is None else total + part
            total = jnp.sum(total, axis=0, keepdims=True)
            taps = jnp.where(sub == 6 - b, total, taps)
        for a in range(7):
            place, slot = (a, g) if g < 8 else (7 + a // 2, g % 4 + 4 * (a % 2))
            moved = pltpu.roll(taps, (slot + a - 6) % 8 * GROUP, axis=1)
            small[place] = jnp.where(lane == slot, moved, small[place])

    line = sums[0:1]
    hidden = line.shape[1] - channels
    pieces = [line[:, c : c + 128] for c in range(0, hidden, 128)]
    pieces.append(line[:, hidden : hidden + 128])
    pieces.append(
        jnp.concatenate([line[:, hidden + 128 :], jnp.zeros((1, 256 - channels), F32)], axis=1)
    )
    for k, piece in enumerate(pieces):
        small[k, 7:8] = piece
    out[...] = small[...].reshape(SMALL, 128).astype(BF16)


def fold_kernel(have, keep, arrived, small, kept, sent, shards):
    rows = kept.shape[0]
    total = keep[...].astype(F32) + arrived[...].astype(F32)
    total = total.reshape(-1, 2, total.shape[0] // shards, 128)
    even, odd = total[:, 0].reshape(rows, 128), total[:, 1].reshape(rows, 128)
    first = have[0] == 0
    kept[...] = jnp.where(first, even, odd).astype(BF16)
    sent[:rows] = jnp.where(first, odd, even).astype(BF16)
    sent[rows:] = small[...]


def spread_kernel(gm, mask, lines, d_conv, d_edge, grad_fields, rolled, tiles, cells, packed, spread):
    lat, channels, lon = gm.shape
    groups = channels // GROUP
    build_tiles(lines, rolled, tiles, True)
    place_cells = laid_cells(d_conv, d_edge, cells)

    def band(g):
        place_cells(g)
        pack_group(cells, packed, lon, g)
        spread[g] = dot(packed[g], tiles[g]).T

    unrolled(groups, band)
    for i in range(lat):
        x = jnp.concatenate(
            [spread[g, i * GROUP : (i + 1) * GROUP, :] for g in range(groups)], axis=0
        )
        x = gm[i].astype(F32) + x * mask[i : i + 1]
        grad_fields[i] = x.astype(BF16)


def final_kernel(core, mine, other, grad_in, grad_out, grad_kernel, grad_gain, grad_bias, scale):
    first = core[0] == 0
    mine, other = mine[...].astype(F32) * scale, other[...].astype(F32) * scale
    sum_in, sum_out = jnp.where(first, mine, other), jnp.where(first, other, mine)
    at = mine.shape[0] - SMALL
    small = mine[at:] + other[at:]
    sum_in, sum_out = sum_in[:at], sum_out[:at]
    rows, hidden = grad_in.shape
    for k in range(hidden // 128):
        grad_in[:, k * 128 : (k + 1) * 128] = sum_in[k * rows : (k + 1) * rows]
    rows, channels = grad_out.shape
    grad_out[:, :128] = sum_out[:rows]
    rest = sum_out[rows:]
    grad_out[:, 128:] = jnp.concatenate([rest[:, :64], rest[:, 64:]], axis=0)
    for a in range(7):
        at = 8 * (7 + a // 2)
        half = slice(64 * (a % 2), 64 * (a % 2) + 64)
        grad_kernel[a, :, :128] = small[8 * a : 8 * a + 7]
        grad_kernel[a, :, 128:] = small[at : at + 7, half]
    lines = [small[8 * k + 7 : 8 * k + 8] for k in range(hidden // 128 + 2)]
    grad_bias[...] = jnp.concatenate(lines[:-2], axis=1).reshape(hidden)
    grad_gain[...] = jnp.concatenate([lines[-2], lines[-1][:, : channels - 128]], axis=1).reshape(
        channels
    )


def swapped(x, axis, bit):
    peers = lax.axis_size(axis)
    return lax.ppermute(x, axis, [(i, i ^ bit) for i in range(peers)])


def bits_of(count):
    return [1 << k for k in range(count.bit_length() - 1)]


def pick(x, axis, at):
    return lax.dynamic_index_in_dim(x, at, axis, keepdims=False)


def both(x, y):
    return (x.astype(F32) + y.astype(F32)).astype(BF16)


def halved(mine, bit):
    have = (lax.axis_index("dp") // bit) & 1
    split = mine.reshape(mine.shape[0] // 2, 2, -1, 128)
    kept, sent = pick(split, 1, have), pick(split, 1, 1 - have)
    return kept, sent.reshape(-1, 128)


VMEM, SMEM, FAR = pltpu.VMEM, pltpu.SMEM, pltpu.HBM


def call(body, name, outs, scratch, megabytes, spaces, out_spaces):
    def held(space, shape, dtype):
        return VMEM(shape, dtype) if space is VMEM else jax.ShapeDtypeStruct(shape, dtype)

    def spec(space):
        return pl.BlockSpec(memory_space={SMEM: SMEM, FAR: pl.ANY}.get(space, VMEM))

    kernel = pl.pallas_call(
        body,
        out_shape=[held(space, *out) for space, out in zip(out_spaces, outs, strict=True)],
        in_specs=[spec(space) for space in spaces],
        out_specs=[spec(space) for space in out_spaces],
        scratch_shapes=[x if not isinstance(x, tuple) else VMEM(*x) for x in scratch],
        compiler_params=pltpu.CompilerParams(vmem_limit_bytes=megabytes * 2**20),
        name=name,
    )

    def run(*args):
        return kernel(
            *[
                pltpu.with_memory_space_constraint(x, space) if space in (FAR, VMEM) else x
                for x, space in zip(args, spaces, strict=True)
            ]
        )

    return run


def per_device(fields, cotangent, land_sea, kernel, ln_gain, weight_in, bias_in, weight_out):
    samples, lat, lon, channels = fields.shape
    hidden = weight_in.shape[1]
    shards, tiles = lax.axis_size("dp"), lax.axis_size("lon")
    groups = channels // GROUP
    rows = channels * hidden // 128
    core = (lax.axis_index("lon") & 1).reshape(1)
    fields = fields[0].transpose(0, 2, 1)
    cotangent = cotangent[0].transpose(0, 2, 1)
    w_out = weight_out.T

    field = ((lat, channels, lon), BF16)
    halo = ((channels + channels // 2, 128), BF16)
    edge = ((channels, 128), BF16)
    rolled = ((16, 8 * groups, 256), F32)
    tile = ((groups, 7 * 256, 256), BF16)
    cells = ((2 * groups, lon + 4 * EDGE, 128), F32)
    packed = ((groups, lon, 7 * 256), BF16)
    border = ((2 * groups, 2 * EDGE + BORDER, 128), F32)
    held = ((groups, 256, lon), F32)

    first, last, masked, gm, mask = call(
        edge_kernel,
        "edges",
        [halo, halo, field, field, ((lat, lon), F32)],
        [field, field, ((lat, lon), jnp.int32), pltpu.SemaphoreType.DMA((9,))],
        8,
        [FAR] * 3,
        [VMEM] * 5,
    )(fields, cotangent, land_sea)
    up = [(i, (i + 1) % tiles) for i in range(tiles)]
    before = lax.ppermute(last, "lon", up)
    after = lax.ppermute(first, "lon", [(j, i) for i, j in up])

    ready = call(
        prepare_kernel,
        "prepare",
        [
            tile,
            packed,
            ((2 * groups, 2 * BORDER, 128), F32),
            ((hidden, 256), BF16),
            ((hidden, channels), BF16),
            ((channels, hidden), BF16),
            ((channels, hidden), BF16),
            ((channels, 128), F32),
            ((8 * groups, 256), F32),
        ],
        [
            rolled,
            cells,
            ((7, 7, channels), F32),
            ((channels,), F32),
            ((hidden,), F32),
            pltpu.SemaphoreType.DMA((5,)),
        ],
        8,
        [VMEM] + [FAR] * 5,
        [VMEM] * 9,
    )(masked, kernel, ln_gain, weight_in, bias_in, w_out)
    lines = ready[-1]

    lines = ready[-1]
    output, d_conv, d_edge, keep, send, sums = call(
        functools.partial(forward_kernel, shards=shards),
        "forward",
        [
            field,
            field,
            edge,
            ((rows, 128), BF16),
            ((rows, 128), BF16),
            ((8, hidden + channels), F32),
        ],
        [
            border,
            border,
            ((groups, 48, 7 * 256), BF16),
            held,
            ((groups, EDGE, 256), F32),
            ((hidden, 256), F32),
            ((hidden, channels), F32),
            ((channels, 128), F32),
            field,
            pltpu.SemaphoreType.DMA((lat // 4,)),
        ],
        14,
        [SMEM] + [VMEM] * 13,
        [FAR] + [VMEM] * 5,
    )(core, before, after, masked, gm, mask, *ready[:-1])

    arrived = swapped(send, "lon", 1)
    (small,) = call(
        taps_kernel,
        "taps",
        [((SMALL, 128), BF16)],
        [cells, packed, ((12, 8, 128), F32)],
        10,
        [VMEM] * 4,
        [VMEM],
    )(masked, d_conv, d_edge, sums)
    have = (lax.axis_index("dp") & 1).reshape(1)
    kept, sent = call(
        functools.partial(fold_kernel, shards=shards),
        "fold",
        [((rows // 2, 128), BF16), ((rows // 2 + SMALL, 128), BF16)],
        [],
        6,
        [SMEM] + [VMEM] * 3,
        [VMEM] * 2,
    )(have, keep, arrived, small)

    sent, d_conv = lax.optimization_barrier((sent, d_conv))
    arrived = swapped(sent, "dp", 1)
    (grad_fields,) = call(
        spread_kernel,
        "spread",
        [field],
        [rolled, tile, cells, packed, held],
        24,
        [VMEM] * 5,
        [None],
    )(gm, mask, lines, d_conv, d_edge)
    arrived, grad_fields = lax.optimization_barrier((arrived, grad_fields))
    mine = both(kept, arrived[: rows // 2]).reshape(shards // 2, -1, 128)
    small = both(small, arrived[rows // 2 :])
    for bit in bits_of(shards)[1:]:
        kept, sent = halved(mine, bit)
        count = sent.shape[0]
        arrived = swapped(jnp.concatenate([sent, small], axis=0), "dp", bit)
        mine = both(kept, arrived[:count].reshape(kept.shape))
        small = both(small, arrived[count:])
    mine = jnp.concatenate([mine.reshape(-1, 128), small], axis=0)
    for bit in bits_of(tiles)[1:]:
        mine = both(mine, swapped(mine, "lon", bit))
    other = swapped(mine, "lon", 1)

    scale = 1.0 / math.sqrt(samples * lat * lon * shards * tiles)
    grads = call(
        functools.partial(final_kernel, scale=scale),
        "final",
        [
            ((channels // shards, hidden), F32),
            ((hidden // shards, channels), F32),
            ((7, 7, channels), F32),
            ((channels,), F32),
            ((hidden,), F32),
        ],
        [],
        8,
        [SMEM] + [VMEM] * 2,
        [None] * 5,
    )(core, mine, other)
    return (output.transpose(0, 2, 1)[None], grad_fields.transpose(0, 2, 1)[None], *grads)


def solution(mesh):
    placed = (
        P("dp", None, "lon", None),
        P("dp", None, "lon", None),
        P(None, "lon"),
        P(),
        P(),
        P(),
        P(),
        P(),
    )
    return jax.shard_map(
        per_device,
        mesh=mesh,
        in_specs=placed,
        out_specs=(
            P("dp", None, "lon", None),
            P("dp", None, "lon", None),
            P("dp", None),
            P("dp", None),
            P(),
            P(),
            P(),
        ),
        check_vma=False,
    )
```
